512 devices in a mesh: azim: 64 (over z_lo, y, core), block: 8 (over x, z_hi).
Axes of the slice: x: 4, y: 4, z: 16 (z_hi: 2, z_lo: 8; z = z_hi * 8 + z_lo), core: 2. Of those that a mesh axis runs over, the one named last changes fastest.
Arguments:
- flow_state: float32 [5, 512, 256, 128], P(None, 'azim', 'block'), may hold values from -4 to 4
- cotangent: float32 [5, 512, 256, 128], P(None, 'azim', 'block'), may hold values from -6 to 6
- mix_theta: float32 [5, 5], replicated, may hold values from -2.5 to 2.5
- mix_axial: float32 [5, 5], replicated, may hold values from -2.5 to 2.5
- mix_radial: float32 [5, 5], replicated, may hold values from -2.5 to 2.5
- intersection_slot: int32 [512, 3], replicated, may hold values from 0 to 15
- intersection_code: int32 [512, 3], replicated, may hold values from 0 to 7
Outputs:
- advanced: float32 [5, 512, 256, 128], P(None, 'azim', 'block')
- sensitivity: float32 [5, 512, 256, 128], P(None, 'azim', 'block')
The draws below stay inside these ranges and needn't reach their ends.
Inputs may be any that keep to these rules, and one draw needn't show every extreme that they name: `intersection_slot`: A slot below 8 names a rotor cell of the previous sector, else one of the own sector.
All inputs are finite; a program needn't handle non-finite values.
Results may differ from the reference program's by a relative error of at most 0.00005.
Values sent between devices are 32-bit elements; how exact they have to be, the bound alone decides.
No kernel may reach another device: no remote copies, remote signals or barrier semaphores. Data moves between devices by JAX's collectives and lax.ppermute only.
A program may use at most 64 MiB of HBM per device.

```python
import jax
import jax.numpy as jnp
from jax import lax

FIELDS = 5
SLOTS = 3
CT = 8
CR = 128
NT = 512
NA = 256


def with_ends(array, own_key, smallest, largest):
    extent = array.shape
    spot = [jax.random.randint(jax.random.fold_in(own_key, axis), (), 0, extent[axis]) for axis in range(len(extent))]
    array = array.at[tuple(spot)].set(smallest)
    longest = extent.index(max(extent))
    spot[longest] = (spot[longest] + 1) % extent[longest]
    return array.at[tuple(spot)].set(largest)


def block_levels(stream_key, dims, cuts, least, largest):
    level, own = 1.0, jax.random.fold_in(stream_key, 6)
    for axis_at, blocks in cuts:
        heights = jnp.exp(jax.random.uniform(jax.random.fold_in(own, axis_at), (blocks,), jnp.float32, least / len(cuts), largest / len(cuts)))
        level = level * jnp.repeat(heights, dims[axis_at] // blocks).reshape([-1 if axis == axis_at else 1 for axis in range(len(dims))])
    return level


def bell_draw(own_key, shape, scale, limit, pieces=(), held_as=jnp.bfloat16):
    level = block_levels(own_key, shape, pieces, -0.22, 0.18) if pieces else 1.0
    result = jax.random.normal(own_key, shape, jnp.float32) * scale * level
    return jnp.minimum(jnp.maximum(result, -limit), limit).astype(held_as)


def setup_inputs(seed: int = 0) -> dict:
    streams_of = jax.random.split(jax.random.key(seed), 8)
    return {
        "flow_state": bell_draw(streams_of[0], (FIELDS, NT, NA, CR), 1.0, 4.0, ((1, 64), (2, 8)), jnp.float32),
        "cotangent": bell_draw(streams_of[1], (FIELDS, NT, NA, CR), 1.0, 6.0, ((1, 64), (2, 8)), jnp.float32),
        "mix_theta": bell_draw(streams_of[2], (FIELDS, FIELDS), FIELDS ** -0.5, 2.5, (), jnp.float32),
        "mix_axial": bell_draw(streams_of[3], (FIELDS, FIELDS), FIELDS ** -0.5, 2.5, (), jnp.float32),
        "mix_radial": bell_draw(streams_of[4], (FIELDS, FIELDS), FIELDS ** -0.5, 2.5, (), jnp.float32),
        "intersection_slot": with_ends(jax.random.randint(streams_of[5], (NT, SLOTS), 0, 2 * CT), jax.random.fold_in(streams_of[5], 1), 0, (2 * CT) - 1).astype(jnp.int32),
        "intersection_code": with_ends(jax.random.randint(streams_of[6], (NT, SLOTS), 0, 8), jax.random.fold_in(streams_of[6], 1), 0, 7).astype(jnp.int32),
    }


nonlinear_gain = 0.4
time_step = 0.25
forward_rates = (0.55, 0.15, 0.5, 0.2, 0.35, 0.35)
reverse_rates = (0.15, 0.55, 0.2, 0.5, 0.35, 0.35)

def mixing(matrix, values_in):
    return jnp.einsum('gf,ftar->gtar', matrix, values_in, precision=lax.Precision.HIGHEST)

def interface_lists(intersection_slot, intersection_code):
    theta_cells = jnp.arange(NT, dtype=jnp.int32)[:, None]
    source = ((theta_cells - theta_cells % CT - CT + intersection_slot) % NT).astype(jnp.int32)
    weights = (intersection_code.astype(jnp.float32) + 1.0) / 12.0
    return (source, weights)

def stencil(values_in, source, weights, coefficients):
    theta_low, theta_high, axial_low, axial_high, radial_low, radial_high = coefficients
    theta_term = theta_low * jnp.roll(values_in, 1, axis=1) + theta_high * jnp.roll(values_in, -1, axis=1) - (theta_low + theta_high) * values_in
    axial_pad = jnp.pad(values_in, ((0, 0), (0, 0), (1, 1), (0, 0)))
    lower_side = axial_pad[:, :, :-2]
    upper_side = axial_pad[:, :, 2:]
    middle = NA // 2
    rotor_face = values_in[:, :, middle - 1]
    stator_face = values_in[:, :, middle]
    from_rotor = lax.optimization_barrier(jnp.sum(rotor_face[:, source, :] * weights[None, :, :, None], axis=2))
    spread = (stator_face[:, :, None, :] * weights[None, :, :, None]).reshape(FIELDS, NT * SLOTS, CR)
    to_rotor = jnp.zeros_like(rotor_face).at[:, source.reshape(-1), :].add(spread)
    lower_side = lower_side.at[:, :, middle].set(from_rotor)
    upper_side = upper_side.at[:, :, middle - 1].set(to_rotor)
    axial_term = axial_low * lower_side + axial_high * upper_side - (axial_low + axial_high) * values_in
    radial_pad = jnp.pad(values_in, ((0, 0), (0, 0), (0, 0), (1, 1)))
    radial_term = radial_low * radial_pad[..., :-2] + radial_high * radial_pad[..., 2:] - (radial_low + radial_high) * values_in
    return (theta_term, axial_term, radial_term)

def reference(flow_state, cotangent, mix_theta, mix_axial, mix_radial, intersection_slot, intersection_code):
    source, weights = interface_lists(intersection_slot, intersection_code)

    def residual(values_in):
        shaped = values_in + 0.5 * nonlinear_gain * values_in * values_in
        theta_term, axial_term, radial_term = stencil(shaped, source, weights, forward_rates)
        return mixing(mix_theta, theta_term) + mixing(mix_axial, axial_term) + mixing(mix_radial, radial_term)

    def advance(start_state):
        section_one = start_state + time_step * residual(start_state)
        return 0.5 * start_state + 0.5 * (section_one + time_step * residual(section_one))
    advanced, pullback = jax.vjp(advance, flow_state)
    sensitivity, = pullback(cotangent)
    return (advanced, sensitivity)
```

```python
import functools

import jax
import jax.numpy as jnp
from jax import lax
from jax.experimental import pallas as pl
from jax.experimental.pallas import tpu as pltpu
from jax.sharding import PartitionSpec as P

nonlinear_gain = 0.4
time_step = 0.25
forward_rates = (0.55, 0.15, 0.5, 0.2, 0.35, 0.35)
reverse_rates = (0.15, 0.55, 0.2, 0.5, 0.35, 0.35)
HALF, EVEN, BLOCK4, BLOCK3, GIVER = range(5)

VMEM = pl.BlockSpec(memory_space=pltpu.VMEM)
SMEM = pl.BlockSpec(memory_space=pltpu.SMEM)
f32 = jnp.float32


def shaping(v):
    return v + 0.5 * nonlinear_gain * v * v


def identity(v):
    return v


def call(kernel, ins, outs, scratch=(), flops=0, name=None):
    small = lambda x: x.dtype == jnp.int32 or x.ndim < 3
    moved = 4 * (sum(x.size for x in ins) + sum(x.size for x in outs))
    return pl.pallas_call(
        kernel,
        out_shape=outs,
        in_specs=[SMEM if small(x) else VMEM for x in ins],
        out_specs=[VMEM] * len(outs),
        scratch_shapes=list(scratch),
        compiler_params=pltpu.CompilerParams(vmem_limit_bytes=24 * 2**20),
        cost_estimate=pl.CostEstimate(flops=flops, bytes_accessed=moved, transcendentals=0),
        name=name,
    )(*ins)


def local_part(source, shaped, rates, mixers, transposed, finish):
    theta_low, theta_high, axial_low, axial_high, radial_low, radial_high = rates
    fields, columns, layers, radii = source.shape
    row = lax.broadcasted_iota(jnp.int32, (layers, radii), 0)
    lane = lax.broadcasted_iota(jnp.int32, (layers, radii), 1)

    def column(t, _):
        before = jnp.where(t > 0, theta_low, 0.0).astype(f32)
        after = jnp.where(t < columns - 1, theta_high, 0.0).astype(f32)
        totals = [None] * fields
        for f in range(fields):
            v = shaped(source[f, t])
            prior = shaped(source[f, jnp.maximum(t - 1, 0)])
            later = shaped(source[f, jnp.minimum(t + 1, columns - 1)])
            theta = before * prior + after * later - (theta_low + theta_high) * v
            lower = jnp.where(row == 0, 0.0, pltpu.roll(v, 1, 0))
            upper = jnp.where(row == layers - 1, 0.0, pltpu.roll(v, layers - 1, 0))
            axial = axial_low * lower + axial_high * upper - (axial_low + axial_high) * v
            inner = jnp.where(lane == 0, 0.0, pltpu.roll(v, 1, 1))
            outer = jnp.where(lane == radii - 1, 0.0, pltpu.roll(v, radii - 1, 1))
            radial = radial_low * inner + radial_high * outer - (radial_low + radial_high) * v
            for g in range(fields):
                at = (f, g) if transposed else (g, f)
                part = mixers[0][at] * theta + mixers[1][at] * axial + mixers[2][at] * radial
                totals[g] = part if totals[g] is None else totals[g] + part
        for g in range(fields):
            finish(g, t, totals[g])
        return 0

    lax.fori_loop(0, columns, column, 0)


def mixed(matrix, transposed, rate, values):
    fields = len(values)
    out = []
    for g in range(fields):
        total = None
        for f in range(fields):
            part = (rate * matrix[(f, g) if transposed else (g, f)]) * values[f]
            total = part if total is None else total + part
        out.append(total)
    return out


def pack_into(sources, shapes, place, xsend, own, send_a, send_b):
    columns, layers = sources[0].shape[1:3]
    half = place[HALF]
    even = place[EVEN]
    first = jnp.where(even == 1, columns - 1, 0)
    other = columns - 1 - first
    for n, (source, shaped) in enumerate(zip(sources, shapes)):
        for f in range(source.shape[0]):
            send_a[n, f] = shaped(source[f, first])
            send_b[n, f] = shaped(source[f, other])
            for t in range(columns):
                low = source[f, t, 0:1, :]
                high = source[f, t, layers - 1 : layers, :]
                xsend[n, f, t : t + 1, :] = shaped(jnp.where(half == 1, high, low))
                own[n, f, t : t + 1, :] = shaped(jnp.where(half == 1, low, high))


def pack_kernel(place, flow, cotangent, xsend, own, send_a, send_b):
    pack_into((flow, cotangent), (shaping, identity), place, xsend, own, send_a, send_b)


def applied(weights, face):
    total = weights[0] * face[0:1, :]
    for j in range(1, face.shape[0]):
        total = total + weights[j] * face[j : j + 1, :]
    return total


def payload_kernel(place, arrived, own, across, weights, send):
    half = place[HALF]
    scale = place[GIVER].astype(f32)
    for n in range(2):
        for f in range(own.shape[1]):
            face = applied(weights[0], arrived[n, f]) + scale * applied(weights[1], across[n, f])
            send[1 - half, n, f] = face
            send[half, n, f] = own[n, f]


def halo_parts(place, got_a, got_b, faces, across, weights, mixers, add_column, add_face):
    even = place[EVEN]
    fields, columns = faces.shape[2:4]
    first = jnp.where(even == 1, columns - 1, 0)
    other = columns - 1 - first
    scales = (place[BLOCK4].astype(f32), place[BLOCK3].astype(f32))
    for n, rates in enumerate((forward_rates, reverse_rates)):
        theta_low, theta_high, axial_low, axial_high = rates[:4]
        rate_a = jnp.where(even == 1, theta_high, theta_low).astype(f32)
        rate_b = jnp.where(even == 1, theta_low, theta_high).astype(f32)
        for at, rate, got in ((first, rate_a, got_a), (other, rate_b, got_b)):
            parts = mixed(mixers[0], n == 1, rate, [got[n, f] for f in range(fields)])
            for g in range(fields):
                add_column(n, g, at, parts[g])
        extra = [applied(weights[1], across[n, f]) for f in range(fields)]
        for side, rate in enumerate((axial_low, axial_high)):
            values = [faces[side, n, f] + scales[side] * extra[f] for f in range(fields)]
            parts = mixed(mixers[1], n == 1, rate, values)
            for g in range(fields):
                for t in range(columns):
                    add_face(n, g, t, side, parts[g][t : t + 1, :])


def first_local_kernel(mix_t, mix_a, mix_r, flow, cotangent, section, reverse):
    mixers = (mix_t, mix_a, mix_r)

    def section_at(g, t, total):
        section[g, t] = flow[g, t] + time_step * total

    def reverse_at(g, t, total):
        reverse[g, t] = total

    local_part(flow, shaping, forward_rates, mixers, False, section_at)
    local_part(cotangent, identity, reverse_rates, mixers, True, reverse_at)


def first_halo_kernel(
    place, mix_t, mix_a, mix_r, cotangent, section_local, reverse_local, got_a, got_b, faces, across, weights,
    section, adjoint, xsend, own, send_a, send_b, reverse,
):
    fields, columns, layers, _ = section.shape
    section[...] = section_local[...]
    reverse[...] = reverse_local[...]

    def add_column(n, g, t, part):
        if n == 0:
            section[g, t] += time_step * part
        else:
            reverse[g, t] += part

    def add_face(n, g, t, side, part):
        rows = slice(layers - 1, layers) if side else slice(0, 1)
        if n == 0:
            section[g, t, rows, :] += time_step * part
        else:
            reverse[g, t, rows, :] += part

    halo_parts(place, got_a, got_b, faces, across, weights, (mix_t, mix_a, mix_r), add_column, add_face)

    def column(t, _):
        for g in range(fields):
            adjoint[g, t] = 0.5 * cotangent[g, t] + 0.5 * time_step * (
                1.0 + nonlinear_gain * section[g, t]
            ) * reverse[g, t]
        return 0

    lax.fori_loop(0, columns, column, 0)
    pack_into((section, adjoint), (shaping, identity), place, xsend, own, send_a, send_b)


def second_local_kernel(mix_t, mix_a, mix_r, flow, cotangent, section, adjoint, advanced, sensitivity):
    mixers = (mix_t, mix_a, mix_r)

    def advanced_at(g, t, total):
        advanced[g, t] = 0.5 * flow[g, t] + 0.5 * (section[g, t] + time_step * total)

    def sensitivity_at(g, t, total):
        sensitivity[g, t] = (
            0.5 * cotangent[g, t]
            + adjoint[g, t]
            + time_step * (1.0 + nonlinear_gain * flow[g, t]) * total
        )

    local_part(section, shaping, forward_rates, mixers, False, advanced_at)
    local_part(adjoint, identity, reverse_rates, mixers, True, sensitivity_at)


def second_halo_kernel(
    place, mix_t, mix_a, mix_r, flow, advanced_local, sensitivity_local, got_a, got_b, faces, across, weights,
    advanced, sensitivity,
):
    layers = flow.shape[2]
    advanced[...] = advanced_local[...]
    sensitivity[...] = sensitivity_local[...]

    def add_column(n, g, t, part):
        if n == 0:
            advanced[g, t] += 0.5 * time_step * part
        else:
            sensitivity[g, t] += time_step * (1.0 + nonlinear_gain * flow[g, t]) * part

    def add_face(n, g, t, side, part):
        rows = slice(layers - 1, layers) if side else slice(0, 1)
        if n == 0:
            advanced[g, t, rows, :] += 0.5 * time_step * part
        else:
            scale = time_step * (1.0 + nonlinear_gain * flow[g, t, rows, :])
            sensitivity[g, t, rows, :] += scale * part

    halo_parts(place, got_a, got_b, faces, across, weights, (mix_t, mix_a, mix_r), add_column, add_face)


def sector_matrix(slot_list, code_list, sector_cells):
    columns = jnp.arange(2 * sector_cells, dtype=jnp.int32)
    matches = (slot_list[:, :, None] == columns[None, None, :]).astype(jnp.float32)
    weights = (code_list.astype(jnp.float32) + 1.0) / 12.0
    return jnp.sum(matches * weights[:, :, None], axis=1)


def interface_weights(intersection_slot, intersection_code, sector_cells, sector, n_sector, block, middle, lanes):
    own_start = sector * sector_cells
    next_start = (sector + 1) % n_sector * sector_cells

    def matrix(start):
        return sector_matrix(
            lax.dynamic_slice_in_dim(intersection_slot, start, sector_cells, 0),
            lax.dynamic_slice_in_dim(intersection_code, start, sector_cells, 0),
            sector_cells,
        )

    own, later = matrix(own_start), matrix(next_start)
    rising = (block == middle) | (block == middle + 1)
    here = jnp.where(block == middle + 1, own[:, sector_cells:].T, own[:, sector_cells:])
    here = jnp.where((block == middle + 1) | (block == middle - 2), here, jnp.eye(sector_cells, dtype=f32))
    there = jnp.where(rising, own[:, :sector_cells].T, later[:, :sector_cells])
    there = jnp.stack([here, there])
    return jnp.broadcast_to(there[..., None], (2, sector_cells, sector_cells, lanes))


def shards(
    flow_state, cotangent, mix_theta, mix_axial, mix_radial, intersection_slot, intersection_code
):
    fields, columns, layers, radii = flow_state.shape
    sector, block = lax.axis_index("azim"), lax.axis_index("block")
    n_sector, n_block = lax.axis_size("azim"), lax.axis_size("block")
    middle = n_block // 2

    pairs_a = [(i, i ^ 1) for i in range(n_sector)]
    pairs_b = [(i, (i + 1 if i % 2 else i - 1) % n_sector) for i in range(n_sector)]
    pairs_x = [(b, b - 2) for b in range(2, n_block, 2)] + [(b, b + 2) for b in range(1, n_block - 2, 2)]
    pairs_long = [(b, b ^ 1) for b in range(n_block)]
    at = lambda s, b: s * n_block + b
    pairs_face = []
    for s in range(n_sector):
        last, zero = s == n_sector - 1, s == 0
        pairs_face.append(
            (at(s, middle - 1), at(0, middle) if last else at(s + 1, middle + 1))
        )
        pairs_face.append(
            (at(s, middle), at(n_sector - 1, middle - 1) if zero else at(s - 1, middle - 2))
        )

    place = jnp.stack(
        [
            block % 2,
            1 - sector % 2,
            block == middle,
            block == middle - 1,
            (block == middle + 1) | (block == middle - 2),
        ]
    ).astype(jnp.int32)
    mixers = (mix_theta, mix_axial, mix_radial)

    shape = jax.ShapeDtypeStruct
    whole = shape(flow_state.shape, f32)
    face = shape((2, fields, columns, radii), f32)
    side = shape((2, fields, layers, radii), f32)
    faces = shape((2, 2, fields, columns, radii), f32)
    work = 4 * 5 * 5 * 3 * 2 * columns * layers * radii

    def exchange(xsend, own, send_a, send_b, weights):
        arrived = lax.ppermute(xsend, "block", pairs_x)
        across = lax.ppermute(xsend, ("azim", "block"), pairs_face)
        if callable(weights):
            weights = weights()
        (payload,) = call(payload_kernel, (place, arrived, own, across, weights), [faces], name="payload")
        both = lax.ppermute(payload, "block", pairs_long)
        got_a = lax.ppermute(send_a, "azim", pairs_a)
        got_b = lax.ppermute(send_b, "azim", pairs_b)
        return (got_a, got_b, both, across, weights)

    weights_of = functools.partial(
        interface_weights, intersection_slot, intersection_code, columns, sector, n_sector, block, middle, radii
    )
    packs = call(pack_kernel, (place, flow_state, cotangent), [face, face, side, side], name="pack")
    halos = exchange(*packs, weights_of)
    weights = halos[-1]
    section_local, reverse_local = call(
        first_local_kernel, (*mixers, flow_state, cotangent), [whole, whole], flops=work, name="first_local"
    )
    section, adjoint, *packs = call(
        first_halo_kernel,
        (place, *mixers, cotangent, section_local, reverse_local, *halos),
        [whole, whole, face, face, side, side],
        scratch=[pltpu.VMEM(whole.shape, f32)],
        name="first_halo",
    )
    halos = exchange(*packs, weights)
    advanced_local, sensitivity_local = call(
        second_local_kernel,
        (*mixers, flow_state, cotangent, section, adjoint),
        [whole, whole],
        flops=work,
        name="second_local",
    )
    return tuple(
        call(
            second_halo_kernel,
            (place, *mixers, flow_state, advanced_local, sensitivity_local, *halos),
            [whole, whole],
            name="second_halo",
        )
    )


def solution(mesh):
    placed = (
        P(None, "azim", "block", None),
        P(None, "azim", "block", None),
        P(),
        P(),
        P(),
        P(),
        P(),
    )
    return jax.shard_map(
        shards,
        mesh=mesh,
        in_specs=placed,
        out_specs=(P(None, "azim", "block", None), P(None, "azim", "block", None)),
        check_vma=False,
    )
```

```python
import jax
import jax.numpy as jnp
from jax import lax
from jax.experimental import pallas as pl
from jax.experimental.pallas import tpu as pltpu
from jax.sharding import PartitionSpec as P

nonlinear_gain = 0.4
time_step = 0.25
forward_rates = (0.55, 0.15, 0.5, 0.2, 0.35, 0.35)
reverse_rates = (0.15, 0.55, 0.2, 0.5, 0.35, 0.35)
HALF, EVEN, PICK, PARTNER_PICK, WRAP, ACROSS = range(6)

VMEM = pl.BlockSpec(memory_space=pltpu.VMEM)
SMEM = pl.BlockSpec(memory_space=pltpu.SMEM)
f32 = jnp.float32
exact = lax.Precision.HIGHEST


def shaping(v):
    return v + 0.5 * nonlinear_gain * v * v


def identity(v):
    return v


def call(kernel, ins, outs, scratch=(), flops=0, name=None):
    small = lambda x: x.dtype == jnp.int32 or x.ndim < 3
    moved = 4 * (sum(x.size for x in ins) + sum(x.size for x in outs))
    return pl.pallas_call(
        kernel,
        out_shape=outs,
        in_specs=[SMEM if small(x) else VMEM for x in ins],
        out_specs=[VMEM] * len(outs),
        scratch_shapes=[pltpu.VMEM(s, f32) for s in scratch],
        compiler_params=pltpu.CompilerParams(vmem_limit_bytes=32 * 2**20),
        cost_estimate=pl.CostEstimate(flops=flops, bytes_accessed=moved, transcendentals=0),
        name=name,
    )(*ins)


def radial_term(v, rates):
    inner_rate, outer_rate = rates[4:]
    radii = v.shape[1]
    lane = lax.broadcasted_iota(jnp.int32, v.shape, 1)
    inner = jnp.where(lane == 0, 0.0, pltpu.roll(v, 1, 1))
    outer = jnp.where(lane == radii - 1, 0.0, pltpu.roll(v, radii - 1, 1))
    return inner_rate * inner + outer_rate * outer - (inner_rate + outer_rate) * v


def mix_into(totals, mixers, transposed, f, terms):
    for g in range(len(totals)):
        at = (f, g) if transposed else (g, f)
        part = None
        for matrix, term in zip(mixers, terms):
            scaled = matrix[at] * term
            part = scaled if part is None else part + scaled
        totals[g] = part if totals[g] is None else totals[g] + part


def operator(source, shaped, rates, mixers, transposed, ends, finish):
    theta_low, theta_high, axial_low, axial_high = rates[:4]
    fields, columns, layers, radii = source.shape

    def column(t, _):
        row = lax.broadcasted_iota(jnp.int32, (layers, radii), 0)
        totals = [None] * fields
        for f in range(fields):
            v = shaped(source[f, t + 1])
            theta = (
                theta_low * shaped(source[f, t])
                + theta_high * shaped(source[f, t + 2])
                - (theta_low + theta_high) * v
            )
            low_end, high_end = ends(f, t)
            lower = jnp.where(row == 0, low_end, pltpu.roll(v, 1, 0))
            upper = jnp.where(row == layers - 1, high_end, pltpu.roll(v, layers - 1, 0))
            axial = axial_low * lower + axial_high * upper - (axial_low + axial_high) * v
            mix_into(totals, mixers, transposed, f, (theta, axial, radial_term(v, rates)))
        for g in range(fields):
            finish(g, t, totals[g])
        return 0

    lax.fori_loop(0, columns - 2, column, 0)


def pack_kernel(place, flow, cotangent, xsend, own, send_a, send_b):
    fields, columns, layers, _ = flow.shape
    half, even, pick = place[HALF], place[EVEN], place[PICK]
    for n, source in enumerate((flow, cotangent)):
        for f in range(fields):
            for t in range(columns):
                rows = slice(t, t + 1)
                for depth in range(2):
                    low = source[f, t, depth : depth + 1, :]
                    high = source[f, t, layers - 1 - depth : layers - depth, :]
                    xsend[depth, n, f, rows, :] = jnp.where(half == 1, high, low)
                    own[depth, n, f, rows, :] = jnp.where(half == 1, low, high)
                    if depth == 0:
                        near = jnp.where(pick == 1, high, low)
                        rows_near = slice(2 * layers + t, 2 * layers + t + 1)
                        send_a[n, f, rows_near, :] = near
                        send_b[n, f, rows_near, :] = near
            for depth in range(2):
                first = jnp.where(even == 1, columns - 1 - depth, depth)
                rows = slice(depth * layers, (depth + 1) * layers)
                send_a[n, f, rows, :] = source[f, first]
                send_b[n, f, rows, :] = source[f, columns - 1 - first]


def payload_kernel(place, arrived, own, send):
    half = place[HALF]
    send[half] = own[...]
    send[1 - half] = arrived[...]


def pass_kernel(place, faces, sent, pass_a, pass_b, pass_far):
    pick, partner_pick = place[PICK], place[PARTNER_PICK]
    wrap, across = place[WRAP], place[ACROSS]

    def choice(flag, depth, other):
        here = 1 - pick if other else pick
        there = 1 - partner_pick if other else partner_pick
        return jnp.where(flag == 1, sent[there, depth], faces[here, depth])

    for n, (depth, other) in enumerate(((0, False), (1, False), (0, True))):
        pass_a[n] = faces[1 - pick if other else pick, depth]
        pass_b[n] = choice(wrap, depth, other)
    pass_far[...] = choice(across, 0, False)


def first_kernel(
    place, mix_t, mix_a, mix_r, flow, cotangent, got_a, got_b,
    section, reverse, reach, flow_wide, reach_wide,
):
    fields, columns, layers, _ = flow.shape
    even = place[EVEN]
    mixers = (mix_t, mix_a, mix_r)
    for n, (source, wide) in enumerate(((flow, flow_wide), (cotangent, reach_wide))):
        wide[:, 2 : 2 + columns] = source[...]
        for f in range(fields):
            for depth in range(2):
                rows = slice(depth * layers, (depth + 1) * layers)
                from_a, from_b = got_a[n, f, rows, :], got_b[n, f, rows, :]
                wide[f, 1 - depth] = jnp.where(even == 1, from_b, from_a)
                wide[f, 2 + columns + depth] = jnp.where(even == 1, from_a, from_b)
    reach[...] = reach_wide[:, 1 : 3 + columns]

    def section_at(g, t, total):
        section[g, t] = flow_wide[g, t + 1] + time_step * total

    def reverse_at(g, t, total):
        reverse[g, t] = total

    ends = lambda f, t: (0.0, 0.0)
    operator(flow_wide, shaping, forward_rates, mixers, False, ends, section_at)
    operator(reach_wide, identity, reverse_rates, mixers, True, ends, reverse_at)


def second_kernel(
    place, mix_t, mix_a, mix_r, flow, cotangent, section_local, reverse_local, reach, got_a, got_b,
    faces, pass_a, pass_b, pass_far, weights,
    advanced, sensitivity,
    section, adjoint, reverse, far_one, far_two, near, virtual, beyond, ends_two,
):
    fields, columns, layers, radii = flow.shape
    even, pick = place[EVEN], place[PICK]
    mixers = (mix_t, mix_a, mix_r)
    all_rates = (forward_rates, reverse_rates)
    all_shapes = (shaping, identity)
    lanes = [
        [slice((n * fields + f) * radii, (n * fields + f + 1) * radii) for f in range(fields)] for n in range(2)
    ]

    def sector_rows(place_in):
        return slice(place_in * columns, (place_in + 1) * columns)

    for side in range(2):
        at_own, at_prior, at_later, at_far = ((2, 1, 3, 0), (1, 0, 2, 3))[side]
        picked = jnp.where(pick == side, 0, 2)
        for n, shaped in enumerate(all_shapes):
            for f in range(fields):
                lane = lanes[n][f]
                from_a, from_b = pass_a[picked, n, f], pass_b[picked, n, f]
                far_one[side, sector_rows(at_own), lane] = shaped(faces[side, 0, n, f])
                far_one[side, sector_rows(at_prior), lane] = shaped(jnp.where(even == 1, from_b, from_a))
                far_one[side, sector_rows(at_later), lane] = shaped(jnp.where(even == 1, from_a, from_b))
                far_one[side, sector_rows(at_far), lane] = shaped(pass_far[n, f])
                from_a, from_b = pass_a[1, n, f], pass_b[1, n, f]
                beside = jnp.where(even == 1, from_b, from_a) if side == 0 else jnp.where(even == 1, from_a, from_b)
                far_two[side, sector_rows(at_own - 1), lane] = shaped(faces[side, 1, n, f])
                far_two[side, sector_rows(2 - at_own), lane] = shaped(beside)
                rows = slice(2 * layers, 2 * layers + columns)
                from_a, from_b = got_a[n, f, rows, :], got_b[n, f, rows, :]
                near[side, sector_rows(0), lane] = shaped(jnp.where(even == 1, from_b, from_a))
                near[side, sector_rows(2), lane] = shaped(jnp.where(even == 1, from_a, from_b))
                source = (flow, cotangent)[n]
                at = layers - 1 if side else 0
                for t in range(columns):
                    rows = slice(columns + t, columns + t + 1)
                    near[side, rows, lane] = shaped(source[f, t, at : at + 1, :])

    two = 2 * columns
    for side in range(2):
        virtual[side] = jnp.dot(weights[side, 0:16, :], far_one[side], precision=exact)
        back = jnp.dot(weights[side, 16:32, 0 : 3 * columns], near[side], precision=exact)
        values = []
        for n, rates in enumerate(all_rates):
            theta_low, theta_high, axial_low, axial_high = rates[:4]
            totals = [None] * fields
            for f in range(fields):
                lane = lanes[n][f]
                v = far_one[side, columns : columns + two, lane]
                theta = (
                    theta_low * far_one[side, columns - 1 : columns - 1 + two, lane]
                    + theta_high * far_one[side, columns + 1 : columns + 1 + two, lane]
                    - (theta_low + theta_high) * v
                )
                lower, upper = far_two[side, :, lane], back[:, lane]
                if side:
                    lower, upper = upper, lower
                axial = axial_low * lower + axial_high * upper - (axial_low + axial_high) * v
                mix_into(totals, mixers, n == 1, f, (theta, axial, radial_term(v, rates)))
            values.append(totals)
        for g in range(fields):
            parts = [faces[side, 0, 0, g], None]
            from_a, from_b = pass_a[jnp.where(pick == side, 0, 2), 0, g], pass_b[jnp.where(pick == side, 0, 2), 0, g]
            if side:
                parts = [parts[0], jnp.where(even == 1, from_a, from_b)]
            else:
                parts = [jnp.where(even == 1, from_b, from_a), parts[0]]
            one = jnp.concatenate(parts, axis=0) + time_step * values[0][g]
            reach_far = far_one[side, columns : columns + two, lanes[1][g]]
            beyond[side, :, lanes[0][g]] = shaping(one)
            beyond[side, :, lanes[1][g]] = 0.5 * reach_far + 0.5 * time_step * (
                1.0 + nonlinear_gain * one
            ) * values[1][g]
        rows_two = jnp.dot(weights[side, 32:40, 0:two], beyond[side], precision=exact)
        for n in range(2):
            for f in range(fields):
                k = (side * 2 + n) * fields + f
                for t in range(columns):
                    ends_two[t, k : k + 1, :] = rows_two[t : t + 1, lanes[n][f]]

    section[...] = section_local[...]
    reverse[...] = reverse_local[...]
    for n, (rates, target, scale) in enumerate(zip(all_rates, (section, reverse), (time_step, 1.0))):
        for side in range(2):
            totals = [None] * fields
            for f in range(fields):
                mix_into(totals, mixers[1:2], n == 1, f, (virtual[side, :, lanes[n][f]],))
            at = slice(layers - 1, layers) if side else slice(0, 1)
            for g in range(fields):
                part = (scale * rates[2 + side]) * totals[g]
                for t in range(columns + 2):
                    target[g, t, at, :] += part[t : t + 1, :]

    def column(t, _):
        for g in range(fields):
            adjoint[g, t] = 0.5 * reach[g, t] + 0.5 * time_step * (
                1.0 + nonlinear_gain * section[g, t]
            ) * reverse[g, t]
        return 0

    lax.fori_loop(0, columns + 2, column, 0)

    def advanced_at(g, t, total):
        advanced[g, t] = 0.5 * flow[g, t] + 0.5 * (section[g, t + 1] + time_step * total)

    def sensitivity_at(g, t, total):
        sensitivity[g, t] = (
            0.5 * cotangent[g, t]
            + adjoint[g, t + 1]
            + time_step * (1.0 + nonlinear_gain * flow[g, t]) * total
        )

    def ends_of(n):
        places = [[(side * 2 + n) * fields + f for side in range(2)] for f in range(fields)]
        return lambda f, t: tuple(ends_two[t, k : k + 1, :] for k in places[f])

    operator(section, shaping, forward_rates, mixers, False, ends_of(0), advanced_at)
    operator(adjoint, identity, reverse_rates, mixers, True, ends_of(1), sensitivity_at)


def interface_weights(slots, codes, cells, sector, block, n_block):
    middle = n_block // 2

    def around(table):
        wide = jnp.concatenate([table[-cells:], table, table[: 2 * cells]], axis=0)
        return lax.dynamic_slice_in_dim(wide, sector * cells, 4 * cells, 0)

    slot = around(slots)
    weight = (around(codes).astype(f32) + 1.0) / 12.0
    index = jnp.arange(4 * cells, dtype=jnp.int32)
    rise = cells * (index // cells)[:, None] + slot
    rotor = jnp.arange(6 * cells, dtype=jnp.int32)
    table = jnp.sum((rise[:, :, None] == rotor) * weight[:, :, None], axis=1)

    def padded(block_of):
        rows, columns = block_of.shape
        return jnp.pad(block_of, ((0, 16 - rows), (0, 4 * cells - columns)))

    def plain(rows, columns, shift):
        return (jnp.arange(columns) == jnp.arange(rows)[:, None] + shift).astype(f32)

    ends = cells + 2
    stator = (table[cells - 1 : 2 * cells + 1, 0 : 4 * cells], table[0 : 3 * cells, cells : 3 * cells].T)
    rotor_side = (table[:, 2 * cells - 1 : 3 * cells + 1].T, table[cells : 3 * cells, cells : 4 * cells])
    sides = []
    for at_interface, inside, pair, shifts in (
        (block == middle, block > 0, stator, (2 * cells - 1, 0)),
        (block == middle - 1, block < n_block - 1, rotor_side, (cells - 1, cells)),
    ):
        forth = jnp.where(at_interface, pair[0], plain(ends, 4 * cells, shifts[0])) * inside
        back = jnp.where(at_interface, pair[1], plain(2 * cells, 3 * cells, shifts[1]))
        sides.append(
            jnp.concatenate(
                [padded(forth), padded(back), padded(forth[1 : cells + 1, cells : 3 * cells])[:cells]], axis=0
            )
        )
    return jnp.stack(sides)


def shards(
    flow_state, cotangent, mix_theta, mix_axial, mix_radial, intersection_slot, intersection_code
):
    fields, columns, layers, radii = flow_state.shape
    sector, block = lax.axis_index("azim"), lax.axis_index("block")
    n_sector, n_block = lax.axis_size("azim"), lax.axis_size("block")
    middle = n_block // 2

    at = lambda s, b: s * n_block + b
    sectors, blocks = range(n_sector), range(n_block)
    pairs_a = [(i, i ^ 1) for i in sectors]
    pairs_b = [(i, (i + 1 if i % 2 else i - 1) % n_sector) for i in sectors]
    pairs_x = [(b, b - 2) for b in range(2, n_block, 2)] + [(b, b + 2) for b in range(1, n_block - 2, 2)]
    pairs_long = [(b, b ^ 1) for b in blocks]
    pairs_pass = [
        (at(i, b), at(j, b ^ 1 if abs(i - j) > 1 else b)) for i, j in pairs_b for b in blocks
    ]
    pairs_far = []
    for s in sectors:
        inside = s + 2 < n_sector
        pairs_far.append((at(s, middle if inside else middle + 1), at((s + 2) % n_sector, middle)))
        inside = s >= 2
        pairs_far.append((at(s, middle - 1 if inside else middle - 2), at((s - 2) % n_sector, middle - 1)))

    place = jnp.stack(
        [
            block % 2,
            1 - sector % 2,
            block != middle,
            block != middle + 1,
            (sector == 0) | (sector == n_sector - 1),
            (block == middle + 1) | (block == middle - 2),
        ]
    ).astype(jnp.int32)
    mixers = (mix_theta, mix_axial, mix_radial)

    shape = lambda *dims: jax.ShapeDtypeStruct(dims, f32)
    whole = shape(*flow_state.shape)
    wide = shape(fields, columns + 2, layers, radii)
    face = shape(2, 2, fields, columns, radii)
    side = shape(2, fields, 2 * layers + columns, radii)
    both = shape(2, 2, 2, fields, columns, radii)
    passed = shape(3, 2, fields, columns, radii)
    far = shape(2, fields, columns, radii)
    work = 4 * 5 * 5 * 3 * 2 * columns * layers * radii

    xsend, own, send_a, send_b = call(
        pack_kernel, (place, flow_state, cotangent), [face, face, side, side], name="pack"
    )
    arrived = lax.ppermute(xsend, "block", pairs_x)
    got_b = lax.ppermute(send_b, "azim", pairs_b)
    (payload,) = call(payload_kernel, (place, arrived, own), [both], name="payload")
    faces = lax.ppermute(payload, "block", pairs_long)
    got_a = lax.ppermute(send_a, "azim", pairs_a)
    got_a, slots, codes = lax.optimization_barrier((got_a, intersection_slot, intersection_code))
    weights = interface_weights(slots, codes, columns, sector, block, n_block)
    section, reverse, reach = call(
        first_kernel,
        (place, *mixers, flow_state, cotangent, got_a, got_b),
        [wide, wide, wide],
        scratch=[(fields, columns + 4, layers, radii)] * 2,
        flops=work,
        name="first",
    )
    faces, section, weights = lax.optimization_barrier((faces, section, weights))
    passes = call(pass_kernel, (place, faces, payload), [passed, passed, far], name="pass_on")
    pass_a = lax.ppermute(passes[0], "azim", pairs_a)
    pass_b = lax.ppermute(passes[1], ("azim", "block"), pairs_pass)
    pass_far = lax.ppermute(passes[2], ("azim", "block"), pairs_far)
    span = 2 * fields * radii
    return tuple(
        call(
            second_kernel,
            (place, *mixers, flow_state, cotangent, section, reverse, reach, got_a, got_b)
            + (faces, pass_a, pass_b, pass_far, weights),
            [whole, whole],
            scratch=[wide.shape] * 3
            + [(2, 4 * columns, span), (2, 2 * columns, span), (2, 3 * columns, span)]
            + [(2, 16, span), (2, 2 * columns, span), (columns, 4 * fields, radii)],
            flops=work,
            name="second",
        )
    )


def solution(mesh):
    placed = (
        P(None, "azim", "block", None),
        P(None, "azim", "block", None),
        P(),
        P(),
        P(),
        P(),
        P(),
    )
    return jax.shard_map(
        shards,
        mesh=mesh,
        in_specs=placed,
        out_specs=(P(None, "azim", "block", None), P(None, "azim", "block", None)),
        check_vma=False,
    )
```

```python
import jax
import jax.numpy as jnp
from jax import lax
from jax.experimental import pallas as pl
from jax.experimental.pallas import tpu as pltpu
from jax.sharding import PartitionSpec as P

nonlinear_gain = 0.4
time_step = 0.25
forward_rates = (0.55, 0.15, 0.5, 0.2, 0.35, 0.35)
reverse_rates = (0.15, 0.55, 0.2, 0.5, 0.35, 0.35)
HALF, EVEN, PICK, ACROSS, RISING, SECTOR = range(6)

VMEM = pl.BlockSpec(memory_space=pltpu.VMEM)
SMEM = pl.BlockSpec(memory_space=pltpu.SMEM)
f32 = jnp.float32
exact = lax.Precision.HIGHEST


def shaping(v):
    return v + 0.5 * nonlinear_gain * v * v


def identity(v):
    return v


def call(kernel, ins, outs, scratch=(), flops=0, name=None, fetched=False):
    small = lambda x: x.dtype == jnp.int32 or x.ndim < 3
    place = pl.BlockSpec(memory_space=pl.ANY) if fetched else VMEM
    moved = 4 * (sum(x.size for x in ins) + sum(x.size for x in outs))
    return pl.pallas_call(
        kernel,
        out_shape=outs,
        in_specs=[SMEM if small(x) else place for x in ins],
        out_specs=[VMEM] * len(outs),
        scratch_shapes=[pltpu.VMEM(s, f32) if isinstance(s, tuple) else s for s in scratch],
        compiler_params=pltpu.CompilerParams(vmem_limit_bytes=(60 if fetched else 32) * 2**20),
        cost_estimate=pl.CostEstimate(flops=flops, bytes_accessed=moved, transcendentals=0),
        name=name,
    )(*ins)


def radial_term(v, rates):
    inner_rate, outer_rate = rates[4:]
    radii = v.shape[1]
    lane = lax.broadcasted_iota(jnp.int32, v.shape, 1)
    inner = jnp.where(lane == 0, 0.0, pltpu.roll(v, 1, 1))
    outer = jnp.where(lane == radii - 1, 0.0, pltpu.roll(v, radii - 1, 1))
    return inner_rate * inner + outer_rate * outer - (inner_rate + outer_rate) * v


def mix_into(totals, mixers, transposed, f, terms):
    for g in range(len(totals)):
        at = (f, g) if transposed else (g, f)
        part = None
        for matrix, term in zip(mixers, terms):
            scaled = matrix[at] * term
            part = scaled if part is None else part + scaled
        totals[g] = part if totals[g] is None else totals[g] + part


def axial_term(v, low_end, high_end, rates):
    axial_low, axial_high = rates[2:4]
    count = v.shape[0]
    row = lax.broadcasted_iota(jnp.int32, v.shape, 0)
    lower = jnp.where(row == 0, low_end, pltpu.roll(v, 1, 0))
    upper = jnp.where(row == count - 1, high_end, pltpu.roll(v, count - 1, 0))
    return axial_low * lower + axial_high * upper - (axial_low + axial_high) * v


def theta_term(prior, v, later, rates):
    theta_low, theta_high = rates[:2]
    return theta_low * prior + theta_high * later - (theta_low + theta_high) * v


def axial_term(v, low_end, high_end, rates):
    axial_low, axial_high = rates[2:4]
    count = v.shape[0]
    row = lax.broadcasted_iota(jnp.int32, v.shape, 0)
    lower = jnp.where(row == 0, low_end, pltpu.roll(v, 1, 0))
    upper = jnp.where(row == count - 1, high_end, pltpu.roll(v, count - 1, 0))
    return axial_low * lower + axial_high * upper - (axial_low + axial_high) * v


def theta_term(prior, v, later, rates):
    theta_low, theta_high = rates[:2]
    return theta_low * prior + theta_high * later - (theta_low + theta_high) * v


def axial_term(v, low_end, high_end, rates):
    axial_low, axial_high = rates[2:4]
    count = v.shape[0]
    row = lax.broadcasted_iota(jnp.int32, v.shape, 0)
    lower = jnp.where(row == 0, low_end, pltpu.roll(v, 1, 0))
    upper = jnp.where(row == count - 1, high_end, pltpu.roll(v, count - 1, 0))
    return axial_low * lower + axial_high * upper - (axial_low + axial_high) * v


def theta_term(prior, v, later, rates):
    theta_low, theta_high = rates[:2]
    return theta_low * prior + theta_high * later - (theta_low + theta_high) * v


def axial_term(v, low_end, high_end, rates):
    axial_low, axial_high = rates[2:4]
    count = v.shape[0]
    row = lax.broadcasted_iota(jnp.int32, v.shape, 0)
    lower = jnp.where(row == 0, low_end, pltpu.roll(v, 1, 0))
    upper = jnp.where(row == count - 1, high_end, pltpu.roll(v, count - 1, 0))
    return axial_low * lower + axial_high * upper - (axial_low + axial_high) * v


def theta_term(prior, v, later, rates):
    theta_low, theta_high = rates[:2]
    return theta_low * prior + theta_high * later - (theta_low + theta_high) * v


def axial_term(v, low_end, high_end, rates):
    axial_low, axial_high = rates[2:4]
    count = v.shape[0]
    row = lax.broadcasted_iota(jnp.int32, v.shape, 0)
    lower = jnp.where(row == 0, low_end, pltpu.roll(v, 1, 0))
    upper = jnp.where(row == count - 1, high_end, pltpu.roll(v, count - 1, 0))
    return axial_low * lower + axial_high * upper - (axial_low + axial_high) * v


def theta_term(prior, v, later, rates):
    theta_low, theta_high = rates[:2]
    return theta_low * prior + theta_high * later - (theta_low + theta_high) * v


def axial_term(v, low_end, high_end, rates):
    axial_low, axial_high = rates[2:4]
    count = v.shape[0]
    row = lax.broadcasted_iota(jnp.int32, v.shape, 0)
    lower = jnp.where(row == 0, low_end, pltpu.roll(v, 1, 0))
    upper = jnp.where(row == count - 1, high_end, pltpu.roll(v, count - 1, 0))
    return axial_low * lower + axial_high * upper - (axial_low + axial_high) * v


def theta_term(prior, v, later, rates):
    theta_low, theta_high = rates[:2]
    return theta_low * prior + theta_high * later - (theta_low + theta_high) * v


def axial_term(v, low_end, high_end, rates):
    axial_low, axial_high = rates[2:4]
    count = v.shape[0]
    row = lax.broadcasted_iota(jnp.int32, v.shape, 0)
    lower = jnp.where(row == 0, low_end, pltpu.roll(v, 1, 0))
    upper = jnp.where(row == count - 1, high_end, pltpu.roll(v, count - 1, 0))
    return axial_low * lower + axial_high * upper - (axial_low + axial_high) * v


def theta_term(prior, v, later, rates):
    theta_low, theta_high = rates[:2]
    return theta_low * prior + theta_high * later - (theta_low + theta_high) * v


def operator(source, shaped, rates, mixers, transposed, rows, finish):
    fields, columns, layers, _ = source.shape
    first, last = rows

    def column(t, _):
        totals = [None] * fields
        for f in range(fields):
            v = shaped(source[f, t + 1, first:last, :])
            low_end = shaped(source[f, t + 1, first - 1 : first, :]) if first > 0 else 0.0
            high_end = shaped(source[f, t + 1, last : last + 1, :]) if last < layers else 0.0
            theta = theta_term(
                shaped(source[f, t, first:last, :]), v, shaped(source[f, t + 2, first:last, :]), rates
            )
            axial = axial_term(v, low_end, high_end, rates)
            mix_into(totals, mixers, transposed, f, (theta, axial, radial_term(v, rates)))
        for g in range(fields):
            finish(g, t, totals[g])
        return 0

    lax.fori_loop(0, columns - 2, column, 0)


def first_step(flow, cotangent, mixers, flow_at, cotangent_at, section, adjoint, reverse):
    columns, layers = flow.shape[1:3]

    def section_at(g, t, total):
        section[g, t] = flow_at(g, t) + time_step * total

    def reverse_at(g, t, total):
        reverse[g, t] = total
        adjoint[g, t] = adjoint_of(cotangent_at(g, t), section[g, t], total)

    operator(flow, shaping, forward_rates, mixers, False, (0, layers), section_at)
    operator(cotangent, identity, reverse_rates, mixers, True, (0, layers), reverse_at)


def adjoint_of(reach, section, reverse):
    return 0.5 * reach + 0.5 * time_step * (1.0 + nonlinear_gain * section) * reverse


def advanced_of(flow, section, total):
    return 0.5 * flow + 0.5 * (section + time_step * total)


def sensitivity_of(reach, adjoint, flow, total):
    return 0.5 * reach + adjoint + time_step * (1.0 + nonlinear_gain * flow) * total


def second_step(section, adjoint, mixers, flow_at, cotangent_at, rows, advanced_to, sensitivity_to):
    inner = slice(*rows)

    def advanced_at(g, t, total):
        advanced_to(g, t, advanced_of(flow_at(g, t), section[g, t + 1, inner, :], total))

    def sensitivity_at(g, t, total):
        value = sensitivity_of(cotangent_at(g, t), adjoint[g, t + 1, inner, :], flow_at(g, t), total)
        sensitivity_to(g, t, value)

    operator(section, shaping, forward_rates, mixers, False, rows, advanced_at)
    operator(adjoint, identity, reverse_rates, mixers, True, rows, sensitivity_at)


def pack_axial_kernel(place, flow, cotangent, xsend, farsend, tiles, landed):
    fields, columns, layers, _ = flow.shape
    half = place[HALF]
    at = pl.ds(pl.multiple_of(half * (layers - 8), 8), 8)
    copies = [
        pltpu.make_async_copy(source.at[:, :, at, :], tiles.at[n], landed.at[n])
        for n, source in enumerate((flow, cotangent))
    ]
    for copy in copies:
        copy.start()
    for n in range(2):
        copies[n].wait()
        for f in range(fields):
            for t in range(columns):
                rows = slice(t, t + 1)
                for depth in range(2):
                    low = tiles[n, f, t, depth : depth + 1, :]
                    high = tiles[n, f, t, 7 - depth : 8 - depth, :]
                    value = jnp.where(half == 1, high, low)
                    xsend[depth, n, f, rows, :] = value
                    if depth == 0:
                        farsend[n, f, rows, :] = value


def pack_column(place, n, f, source, first, send):
    columns, layers = source.shape[1:3]
    pick = place[PICK]
    for depth in range(2):
        rows = slice(depth * layers, (depth + 1) * layers)
        send[n, f, rows, :] = source[f, first + depth - 2 * depth * (first > 0)]
    for t in range(columns):
        low = source[f, t, 0:1, :]
        high = source[f, t, layers - 1 : layers, :]
        rows = slice(2 * layers + t, 2 * layers + t + 1)
        send[n, f, rows, :] = jnp.where(pick == 1, high, low)


def pack_own_kernel(place, flow, cotangent, own, send_wrap):
    fields, columns, layers, _ = flow.shape
    half, even = place[HALF], place[EVEN]
    first = jnp.where(even == 1, 0, columns - 1)
    for n, source in enumerate((flow, cotangent)):
        for f in range(fields):
            pack_column(place, n, f, source, first, send_wrap)
            for t in range(columns):
                for depth in range(2):
                    low = source[f, t, depth : depth + 1, :]
                    high = source[f, t, layers - 1 - depth : layers - depth, :]
                    own[depth, n, f, t : t + 1, :] = jnp.where(half == 1, low, high)


def pack_columns(place, flow, cotangent, send_a, send_b):
    fields, columns = flow.shape[:2]
    first = jnp.where(place[EVEN] == 1, 0, columns - 1)
    for n, source in enumerate((flow, cotangent)):
        for f in range(fields):
            pack_column(place, n, f, source, first, send_b)
            pack_column(place, n, f, source, columns - 1 - first, send_a)


def payload_kernel(place, slots, codes, arrived, own, far, send):
    fields, columns = own.shape[2:4]
    count = slots.shape[1]
    half, rising, sector = place[HALF], place[RISING], place[SECTOR]
    for depth in range(2):
        for n in range(2):
            for f in range(fields):
                k = (depth * 2 + n) * fields + f
                send[4 * fields * half + k] = own[depth, n, f]
                send[4 * fields * (1 - half) + k] = arrived[depth, n, f]
    rest = send.shape[0] - 8 * fields
    for k in range(rest):
        send[8 * fields + k] = jnp.zeros(send.shape[1:], f32)

    @pl.when(place[ACROSS] == 1)
    def _():
        weights = []
        for j in range(columns):
            spot = jnp.where(rising == 1, sector * columns - 1, (sector + 2) * columns + j)
            spot = jnp.where(spot < 0, spot + count, jnp.where(spot >= count, spot - count, spot))
            wanted = jnp.where(rising == 1, j, 0)
            weight = jnp.float32(0.0)
            for k in range(slots.shape[0]):
                share = (codes[k, spot].astype(f32) + 1.0) * (1.0 / 12.0)
                weight = weight + jnp.where(slots[k, spot] == wanted, share, 0.0)
            weights.append(weight)
        for n, shaped in enumerate((shaping, identity)):
            for f in range(fields):
                face = shaped(far[n, f])
                total = weights[0] * face[0:1, :]
                for j in range(1, columns):
                    total = total + weights[j] * face[j : j + 1, :]
                side_row = jnp.where(rising == 1, face[columns - 1 : columns, :], face[0:1, :])
                for k, value in ((n * fields + f, total), ((2 + n) * fields + f, side_row)):
                    send[8 * fields + k // 8, k % 8 : k % 8 + 1, :] = value


def inner_kernel(
    place, mix_t, mix_a, mix_r, flow, cotangent,
    section, adjoint, reverse_ends, advanced, sensitivity, send_a, send_b, reverse,
):
    fields, columns, layers, _ = flow.shape
    mixers = (mix_t, mix_a, mix_r)
    pack_columns(place, flow, cotangent, send_a, send_b)
    first_step(
        flow, cotangent, mixers, lambda g, t: flow[g, t + 1], lambda g, t: cotangent[g, t + 1],
        section, adjoint, reverse,
    )
    for side, a in enumerate((0, layers - 1)):
        for g in range(fields):
            for t in range(columns - 2):
                reverse_ends[side, g, t : t + 1, :] = reverse[g, t, a : a + 1, :]
    rows = (8, layers - 8)
    inner = slice(*rows)

    def advanced_to(g, t, value):
        advanced[g, t] = value

    def sensitivity_to(g, t, value):
        sensitivity[g, t] = value

    second_step(
        section, adjoint, mixers, lambda g, t: flow[g, t + 2, inner, :], lambda g, t: cotangent[g, t + 2, inner, :],
        rows, advanced_to, sensitivity_to,
    )


def outer_kernel(
    place, mix_t, mix_a, mix_r, flow, cotangent, got_a, got_b, got_wrap,
    section_inner, adjoint_inner, reverse_ends,
    section, adjoint, ends, advanced, sensitivity, flow_ends, reach_ends, reverse,
):
    fields, columns, layers, _ = flow.shape
    even = place[EVEN]
    mixers = (mix_t, mix_a, mix_r)
    wide = columns + 2
    for n, (source, both) in enumerate(((flow, flow_ends), (cotangent, reach_ends))):
        for f in range(fields):
            for depth in range(2):
                rows = slice(depth * layers, (depth + 1) * layers)
                from_a = got_a[n, f, rows, :]
                from_b = got_b[n, f, rows, :] + got_wrap[n, f, rows, :]
                both[0, f, 1 - depth] = jnp.where(even == 1, from_b, from_a)
                both[0, f, 2 + depth] = source[f, depth]
                both[1, f, 1 - depth] = source[f, columns - 1 - depth]
                both[1, f, 2 + depth] = jnp.where(even == 1, from_a, from_b)
    section[:, 2 : wide - 2] = section_inner[...]
    adjoint[:, 2 : wide - 2] = adjoint_inner[...]
    rows = (8, layers - 8)
    inner = slice(*rows)
    for side in range(2):
        flow_side, reach_side = flow_ends.at[side], reach_ends.at[side]
        at = slice(wide - 2, wide) if side else slice(0, 2)
        first_step(
            flow_side, reach_side, mixers, lambda g, t: flow_side[g, t + 1], lambda g, t: reach_side[g, t + 1],
            section.at[:, at], adjoint.at[:, at], reverse.at[side],
        )
    for side in range(2):
        at = slice(wide - 4, wide) if side else slice(0, 4)
        own = columns - 2 if side else 0

        def advanced_to(g, t, value):
            advanced[g, 2 * side + t] = value

        def sensitivity_to(g, t, value):
            sensitivity[g, 2 * side + t] = value

        second_step(
            section.at[:, at], adjoint.at[:, at], mixers,
            lambda g, t: flow[g, own + t, inner, :], lambda g, t: cotangent[g, own + t, inner, :],
            rows, advanced_to, sensitivity_to,
        )
    for side, a in enumerate((0, layers - 1)):
        row = slice(a, a + 1)
        for g in range(fields):
            for t in range(wide):
                to = slice(t, t + 1)
                ends[side, 0, g, to, :] = section[g, t, row, :]
                if t < 2 or t >= wide - 2:
                    end, place_in = (0, t) if t < 2 else (1, t - wide + 2)
                    ends[side, 1, g, to, :] = reverse[end, g, place_in, row, :]
                    ends[side, 2, g, to, :] = reach_ends[end, g, place_in + 1, row, :]
                else:
                    ends[side, 1, g, to, :] = reverse_ends[side, g, t - 2 : t - 1, :]
                    ends[side, 2, g, to, :] = cotangent[g, t - 1, row, :]


def last_kernel(
    place, mix_t, mix_a, mix_r, flow, cotangent, section, adjoint, ends, faces, pass_a, pass_b, far,
    got_a, got_b, got_wrap, weights, advanced_inner, sensitivity_inner, advanced_outer, sensitivity_outer,
    advanced, sensitivity,
    far_one, far_two, near, virtual, beyond, ends_two, tiles, section_ends,
):
    fields, columns, layers, radii = flow.shape
    even, pick = place[EVEN], place[PICK]
    mixers = (mix_t, mix_a, mix_r)
    all_rates = (forward_rates, reverse_rates)
    all_shapes = (shaping, identity)
    lanes = [
        [slice((n * fields + f) * radii, (n * fields + f + 1) * radii) for f in range(fields)] for n in range(2)
    ]
    inner = slice(8, layers - 8)
    advanced[:, 2 : columns - 2, inner, :] = advanced_inner[...]
    sensitivity[:, 2 : columns - 2, inner, :] = sensitivity_inner[...]
    for side in range(2):
        at = slice(columns - 2, columns) if side else slice(0, 2)
        from_outer = slice(2 * side, 2 * side + 2)
        advanced[:, at, inner, :] = advanced_outer[:, from_outer]
        sensitivity[:, at, inner, :] = sensitivity_outer[:, from_outer]

    def prior_later(from_a, from_b):
        return jnp.where(even == 1, from_b, from_a), jnp.where(even == 1, from_a, from_b)

    def spot(side, depth, n, f):
        return ((side * 2 + depth) * 2 + n) * fields + f

    def sector_rows(place_in):
        return slice(place_in * columns, (place_in + 1) * columns)

    for side in range(2):
        at_own, at_prior, at_later, at_far = ((2, 1, 3, 0), (1, 0, 2, 3))[side]
        for n, shaped in enumerate(all_shapes):
            for f in range(fields):
                lane = lanes[n][f]
                k = spot(side, 0, n, f)
                prior, later = prior_later(pass_a[k], pass_b[k])
                far_one[side, sector_rows(at_own), lane] = shaped(faces[k])
                far_one[side, sector_rows(at_prior), lane] = shaped(prior)
                far_one[side, sector_rows(at_later), lane] = shaped(later)
                far_one[side, sector_rows(at_far), lane] = shaped(far[n, f])
                k = spot(side, 1, n, f)
                beside = prior_later(pass_a[k], pass_b[k])[side]
                far_two[side, sector_rows(at_own - 1), lane] = shaped(faces[k])
                far_two[side, sector_rows(2 - at_own), lane] = shaped(beside)
                rows = slice(2 * layers, 2 * layers + columns)
                prior, later = prior_later(got_a[n, f, rows, :], got_b[n, f, rows, :] + got_wrap[n, f, rows, :])
                near[side, sector_rows(0), lane] = shaped(prior)
                near[side, sector_rows(2), lane] = shaped(later)
                source = (flow, cotangent)[n]
                at = layers - 1 if side else 0
                for t in range(columns):
                    rows = slice(columns + t, columns + t + 1)
                    near[side, rows, lane] = shaped(source[f, t, at : at + 1, :])

    two = 2 * columns
    for side in range(2):
        virtual[side] = jnp.dot(weights[side, 0:16, :], far_one[side], precision=exact)
        back = jnp.dot(weights[side, 16:32, 0 : 3 * columns], near[side], precision=exact)
        here = jnp.where(pick == side, 1.0, 0.0).astype(f32)
        row = slice(columns + 1, columns + 2) if side else slice(0, 1)
        spot_near = 3 * columns if side else columns - 1
        nearest = slice(spot_near, spot_near + 1)
        values = []
        for n, rates in enumerate(all_rates):
            totals = [None] * fields
            for f in range(fields):
                lane = lanes[n][f]
                k = n * fields + f
                for target, at, k in ((virtual, row, k), (far_one, nearest, k + 2 * fields)):
                    target[side, at, lane] += here * faces[8 * fields + k // 8, k % 8 : k % 8 + 1, :]
                v = far_one[side, columns : columns + two, lane]
                theta = theta_term(
                    far_one[side, columns - 1 : columns - 1 + two, lane], v,
                    far_one[side, columns + 1 : columns + 1 + two, lane], rates,
                )
                lower, upper = far_two[side, :, lane], back[:, lane]
                if side:
                    lower, upper = upper, lower
                axial_low, axial_high = rates[2:4]
                axial = axial_low * lower + axial_high * upper - (axial_low + axial_high) * v
                mix_into(totals, mixers, n == 1, f, (theta, axial, radial_term(v, rates)))
            values.append(totals)
        for g in range(fields):
            k = spot(side, 0, 0, g)
            parts = [faces[k], prior_later(pass_a[k], pass_b[k])[side]]
            one = jnp.concatenate(parts if side else parts[::-1], axis=0) + time_step * values[0][g]
            reach_far = far_one[side, columns : columns + two, lanes[1][g]]
            beyond[side, :, lanes[0][g]] = shaping(one)
            beyond[side, :, lanes[1][g]] = adjoint_of(reach_far, one, values[1][g])
        ends_two[side] = jnp.dot(weights[side, 32:40, 0:two], beyond[side], precision=exact)

        totals = [[None] * fields for _ in range(2)]
        for n in range(2):
            for f in range(fields):
                mix_into(totals[n], mixers[1:2], n == 1, f, (virtual[side, :, lanes[n][f]],))
        a = layers - 8 if side else 0
        edge = lax.broadcasted_iota(jnp.int32, (8, radii), 0) == (7 if side else 0)
        for g in range(fields):
            section_end = ends[side, 0, g] + (time_step * forward_rates[2 + side]) * totals[0][g]
            reverse_end = ends[side, 1, g] + reverse_rates[2 + side] * totals[1][g]
            adjoint_end = adjoint_of(ends[side, 2, g], section_end, reverse_end)
            section_ends[side, g] = section_end
            for t in range(columns + 2):
                to = slice(t, t + 1)
                tile = jnp.where(edge, section_end[to, :], section[g, t, a : a + 8, :])
                tiles[side, 0, g, t] = shaping(tile)
                tiles[side, 1, g, t] = jnp.where(edge, adjoint_end[to, :], adjoint[g, t, a : a + 8, :])

        for t in range(columns):
            for n, (rates, shaped, source) in enumerate(zip(all_rates, all_shapes, (section, adjoint))):
                totals = [None] * fields
                for f in range(fields):
                    v = tiles[side, n, f, t + 1]
                    theta = theta_term(tiles[side, n, f, t], v, tiles[side, n, f, t + 2], rates)
                    far_end = ends_two[side, t : t + 1, lanes[n][f]]
                    b = a - 1 if side else a + 8
                    inner_end = shaped(source[f, t + 1, b : b + 1, :])
                    low_end, high_end = (inner_end, far_end) if side else (far_end, inner_end)
                    axial = axial_term(v, low_end, high_end, rates)
                    mix_into(totals, mixers, n == 1, f, (theta, axial, radial_term(v, rates)))
                rows = slice(a, a + 8)
                for g in range(fields):
                    flow_tile = flow[g, t, rows, :]
                    if n == 0:
                        tile = jnp.where(
                            edge, section_ends[side, g, t + 1 : t + 2, :], section[g, t + 1, rows, :]
                        )
                        advanced[g, t, rows, :] = advanced_of(flow_tile, tile, totals[g])
                    else:
                        sensitivity[g, t, rows, :] = sensitivity_of(
                            cotangent[g, t, rows, :], tiles[side, 1, g, t + 1], flow_tile, totals[g]
                        )


def interface_weights(slots, codes, cells, sector, block, n_block):
    middle = n_block // 2

    def around(table):
        wide = jnp.concatenate([table[-cells:], table, table[: 2 * cells]], axis=0)
        return lax.dynamic_slice_in_dim(wide, sector * cells, 4 * cells, 0)

    slot = around(slots)
    weight = (around(codes).astype(f32) + 1.0) / 12.0
    index = jnp.arange(4 * cells, dtype=jnp.int32)
    rise = cells * (index // cells)[:, None] + slot
    rotor = jnp.arange(6 * cells, dtype=jnp.int32)
    table = jnp.sum((rise[:, :, None] == rotor) * weight[:, :, None], axis=1)

    def padded(block_of):
        rows, columns = block_of.shape
        return jnp.pad(block_of, ((0, 16 - rows), (0, 4 * cells - columns)))

    def plain(rows, columns, shift):
        return (jnp.arange(columns) == jnp.arange(rows)[:, None] + shift).astype(f32)

    ends = cells + 2
    stator = (table[cells - 1 : 2 * cells + 1, 0 : 4 * cells], table[0 : 3 * cells, cells : 3 * cells].T)
    rotor_side = (table[:, 2 * cells - 1 : 3 * cells + 1].T, table[cells : 3 * cells, cells : 4 * cells])
    sides = []
    for at_interface, inside, pair, shifts in (
        (block == middle, block > 0, stator, (2 * cells - 1, 0)),
        (block == middle - 1, block < n_block - 1, rotor_side, (cells - 1, cells)),
    ):
        forth = jnp.where(at_interface, pair[0], plain(ends, 4 * cells, shifts[0])) * inside
        back = jnp.where(at_interface, pair[1], plain(2 * cells, 3 * cells, shifts[1]))
        sides.append(
            jnp.concatenate(
                [padded(forth), padded(back), padded(forth[1 : cells + 1, cells : 3 * cells])[:cells]], axis=0
            )
        )
    return jnp.stack(sides)


def shards(
    flow_state, cotangent, mix_theta, mix_axial, mix_radial, intersection_slot, intersection_code
):
    fields, columns, layers, radii = flow_state.shape
    sector, block = lax.axis_index("azim"), lax.axis_index("block")
    n_sector, n_block = lax.axis_size("azim"), lax.axis_size("block")
    middle = n_block // 2

    at = lambda s, b: s * n_block + b
    sectors, blocks = range(n_sector), range(n_block)
    pairs_a = [(i, i ^ 1) for i in sectors]
    pairs_b = [(i, (i + 1 if i % 2 else i - 1) % n_sector) for i in sectors]
    pairs_wrap = [(i, j) for i, j in pairs_b if abs(i - j) > 1]
    pairs_near = [(i, j) for i, j in pairs_b if abs(i - j) == 1]
    pairs_x = [(b, b - 2) for b in range(2, n_block, 2)] + [(b, b + 2) for b in range(1, n_block - 2, 2)]
    pairs_long = [(b, b ^ 1) for b in blocks]
    pairs_pass = [
        (at(i, b), at(j, b ^ 1 if abs(i - j) > 1 else b)) for i, j in pairs_b for b in blocks
    ]
    pairs_far = []
    for s in sectors:
        inside = s + 2 < n_sector
        pairs_far.append((at(s, middle - 1), at((s + 2) % n_sector, middle + 1 if inside else middle)))
        inside = s >= 2
        pairs_far.append((at(s, middle), at((s - 2) % n_sector, middle - 2 if inside else middle - 1)))

    wrap = (sector == 0) | (sector == n_sector - 1)
    place = jnp.stack(
        [
            block % 2,
            1 - sector % 2,
            block != middle,
            (block == middle + 1) | (block == middle - 2),
            block == middle + 1,
            sector,
        ]
    ).astype(jnp.int32)
    mixers = (mix_theta, mix_axial, mix_radial)

    shape = lambda *dims: jax.ShapeDtypeStruct(dims, f32)
    whole = shape(*flow_state.shape)
    inner = shape(fields, columns - 2, layers, radii)
    wide = shape(fields, columns + 2, layers, radii)
    half_out = shape(fields, columns - 4, layers - 16, radii)
    outer_out = shape(fields, 4, layers - 16, radii)
    face = shape(2, 2, fields, columns, radii)
    side = shape(2, fields, 2 * layers + columns, radii)
    sent = shape(8 * fields + (4 * fields + 7) // 8, columns, radii)
    far_face = shape(2, fields, columns, radii)
    work = 4 * 5 * 5 * 3 * columns * layers * radii

    xsend, farsend = call(
        pack_axial_kernel,
        (place, flow_state, cotangent),
        [face, far_face],
        scratch=[(2, fields, columns, 8, radii), pltpu.SemaphoreType.DMA((2,))],
        name="pack_axial",
        fetched=True,
    )
    arrived = lax.ppermute(xsend, "block", pairs_x)
    far = lax.ppermute(farsend, ("azim", "block"), pairs_far)
    own, send_wrap = call(pack_own_kernel, (place, flow_state, cotangent), [face, side], name="pack_own")
    got_wrap = lax.ppermute(send_wrap, "azim", pairs_wrap)
    (payload,) = call(
        payload_kernel,
        (place, intersection_slot.T, intersection_code.T, arrived, own, far),
        [sent],
        name="payload",
    )
    faces = lax.ppermute(payload, "block", pairs_long)

    place_later, payload = lax.optimization_barrier((place, payload))
    section, adjoint, reverse_ends, advanced_inner, sensitivity_inner, send_a, send_b = call(
        inner_kernel,
        (place_later, *mixers, flow_state, cotangent),
        [inner, inner, shape(2, fields, columns, radii), half_out, half_out, side, side],
        scratch=[inner.shape],
        flops=20 * work,
        name="inner",
    )
    got_a = lax.ppermute(send_a, "azim", pairs_a)
    got_b = lax.ppermute(send_b, "azim", pairs_near)
    faces, section, slots, codes = lax.optimization_barrier(
        (faces, section, intersection_slot, intersection_code)
    )
    pass_a = lax.ppermute(faces, "azim", pairs_a)
    pass_b = lax.ppermute(jnp.where(wrap, payload, faces), ("azim", "block"), pairs_pass)
    section, adjoint, ends, advanced_outer, sensitivity_outer = call(
        outer_kernel,
        (place, *mixers, flow_state, cotangent, got_a, got_b, got_wrap, section, adjoint, reverse_ends),
        [wide, wide, shape(2, 3, fields, 16, radii), outer_out, outer_out],
        scratch=[(2, fields, 4, layers, radii), (2, fields, 4, layers, radii), (2, fields, 2, layers, radii)],
        flops=0,
        name="outer",
    )
    weights = interface_weights(slots, codes, columns, sector, block, n_block)
    span = 2 * fields * radii
    return tuple(
        call(
            last_kernel,
            (place, *mixers, flow_state, cotangent, section, adjoint, ends, faces, pass_a, pass_b, far)
            + (got_a, got_b, got_wrap, weights)
            + (advanced_inner, sensitivity_inner, advanced_outer, sensitivity_outer),
            [whole, whole],
            scratch=[
                (2, 4 * columns, span),
                (2, 2 * columns, span),
                (2, 3 * columns, span),
                (2, 16, span),
                (2, 2 * columns, span),
                (2, columns, span),
                (2, 2, fields, columns + 2, 8, radii),
                (2, fields, 16, radii),
            ],
            flops=0,
            name="last",
        )
    )


def solution(mesh):
    placed = (
        P(None, "azim", "block", None),
        P(None, "azim", "block", None),
        P(),
        P(),
        P(),
        P(),
        P(),
    )
    return jax.shard_map(
        shards,
        mesh=mesh,
        in_specs=placed,
        out_specs=(P(None, "azim", "block", None), P(None, "azim", "block", None)),
        check_vma=False,
    )
```

```python
import jax
import jax.numpy as jnp
from jax import lax
from jax.experimental import pallas as pl
from jax.experimental.pallas import tpu as pltpu
from jax.sharding import PartitionSpec as P

nonlinear_gain = 0.4
time_step = 0.25
forward_rates = (0.55, 0.15, 0.5, 0.2, 0.35, 0.35)
reverse_rates = (0.15, 0.55, 0.2, 0.5, 0.35, 0.35)
HALF, EVEN, PICK, ACROSS, RISING, SECTOR = range(6)

VMEM = pl.BlockSpec(memory_space=pltpu.VMEM)
SMEM = pl.BlockSpec(memory_space=pltpu.SMEM)
f32 = jnp.float32
exact = lax.Precision.HIGHEST


def shaping(v):
    return v + 0.5 * nonlinear_gain * v * v


def identity(v):
    return v


def call(kernel, ins, outs, scratch=(), flops=0, name=None):
    small = lambda x: x.dtype == jnp.int32 or x.ndim < 3
    moved = 4 * (sum(x.size for x in ins) + sum(x.size for x in outs))
    return pl.pallas_call(
        kernel,
        out_shape=outs,
        in_specs=[SMEM if small(x) else VMEM for x in ins],
        out_specs=[VMEM] * len(outs),
        scratch_shapes=[pltpu.VMEM(s, f32) for s in scratch],
        compiler_params=pltpu.CompilerParams(vmem_limit_bytes=24 * 2**20),
        cost_estimate=pl.CostEstimate(flops=flops, bytes_accessed=moved, transcendentals=0),
        name=name,
    )(*ins)


def radial_term(v, rates):
    inner_rate, outer_rate = rates[4:]
    radii = v.shape[1]
    lane = lax.broadcasted_iota(jnp.int32, v.shape, 1)
    inner = jnp.where(lane == 0, 0.0, pltpu.roll(v, 1, 1))
    outer = jnp.where(lane == radii - 1, 0.0, pltpu.roll(v, radii - 1, 1))
    return inner_rate * inner + outer_rate * outer - (inner_rate + outer_rate) * v


def mix_into(totals, mixers, transposed, f, terms):
    for g in range(len(totals)):
        at = (f, g) if transposed else (g, f)
        part = None
        for matrix, term in zip(mixers, terms):
            scaled = matrix[at] * term
            part = scaled if part is None else part + scaled
        totals[g] = part if totals[g] is None else totals[g] + part


def axial_term(v, low_end, high_end, rates):
    axial_low, axial_high = rates[2:4]
    count = v.shape[0]
    row = lax.broadcasted_iota(jnp.int32, v.shape, 0)
    lower = jnp.where(row == 0, low_end, pltpu.roll(v, 1, 0))
    upper = jnp.where(row == count - 1, high_end, pltpu.roll(v, count - 1, 0))
    return axial_low * lower + axial_high * upper - (axial_low + axial_high) * v


def theta_term(prior, v, later, rates):
    theta_low, theta_high = rates[:2]
    return theta_low * prior + theta_high * later - (theta_low + theta_high) * v


def axial_term(v, low_end, high_end, rates):
    axial_low, axial_high = rates[2:4]
    count = v.shape[0]
    row = lax.broadcasted_iota(jnp.int32, v.shape, 0)
    lower = jnp.where(row == 0, low_end, pltpu.roll(v, 1, 0))
    upper = jnp.where(row == count - 1, high_end, pltpu.roll(v, count - 1, 0))
    return axial_low * lower + axial_high * upper - (axial_low + axial_high) * v


def theta_term(prior, v, later, rates):
    theta_low, theta_high = rates[:2]
    return theta_low * prior + theta_high * later - (theta_low + theta_high) * v


def axial_term(v, low_end, high_end, rates):
    axial_low, axial_high = rates[2:4]
    count = v.shape[0]
    row = lax.broadcasted_iota(jnp.int32, v.shape, 0)
    lower = jnp.where(row == 0, low_end, pltpu.roll(v, 1, 0))
    upper = jnp.where(row == count - 1, high_end, pltpu.roll(v, count - 1, 0))
    return axial_low * lower + axial_high * upper - (axial_low + axial_high) * v


def theta_term(prior, v, later, rates):
    theta_low, theta_high = rates[:2]
    return theta_low * prior + theta_high * later - (theta_low + theta_high) * v


def axial_term(v, low_end, high_end, rates):
    axial_low, axial_high = rates[2:4]
    count = v.shape[0]
    row = lax.broadcasted_iota(jnp.int32, v.shape, 0)
    lower = jnp.where(row == 0, low_end, pltpu.roll(v, 1, 0))
    upper = jnp.where(row == count - 1, high_end, pltpu.roll(v, count - 1, 0))
    return axial_low * lower + axial_high * upper - (axial_low + axial_high) * v


def theta_term(prior, v, later, rates):
    theta_low, theta_high = rates[:2]
    return theta_low * prior + theta_high * later - (theta_low + theta_high) * v


def axial_term(v, low_end, high_end, rates):
    axial_low, axial_high = rates[2:4]
    count = v.shape[0]
    row = lax.broadcasted_iota(jnp.int32, v.shape, 0)
    lower = jnp.where(row == 0, low_end, pltpu.roll(v, 1, 0))
    upper = jnp.where(row == count - 1, high_end, pltpu.roll(v, count - 1, 0))
    return axial_low * lower + axial_high * upper - (axial_low + axial_high) * v


def theta_term(prior, v, later, rates):
    theta_low, theta_high = rates[:2]
    return theta_low * prior + theta_high * later - (theta_low + theta_high) * v


def axial_term(v, low_end, high_end, rates):
    axial_low, axial_high = rates[2:4]
    count = v.shape[0]
    row = lax.broadcasted_iota(jnp.int32, v.shape, 0)
    lower = jnp.where(row == 0, low_end, pltpu.roll(v, 1, 0))
    upper = jnp.where(row == count - 1, high_end, pltpu.roll(v, count - 1, 0))
    return axial_low * lower + axial_high * upper - (axial_low + axial_high) * v


def theta_term(prior, v, later, rates):
    theta_low, theta_high = rates[:2]
    return theta_low * prior + theta_high * later - (theta_low + theta_high) * v


def axial_term(v, low_end, high_end, rates):
    axial_low, axial_high = rates[2:4]
    count = v.shape[0]
    row = lax.broadcasted_iota(jnp.int32, v.shape, 0)
    lower = jnp.where(row == 0, low_end, pltpu.roll(v, 1, 0))
    upper = jnp.where(row == count - 1, high_end, pltpu.roll(v, count - 1, 0))
    return axial_low * lower + axial_high * upper - (axial_low + axial_high) * v


def theta_term(prior, v, later, rates):
    theta_low, theta_high = rates[:2]
    return theta_low * prior + theta_high * later - (theta_low + theta_high) * v


def axial_term(v, low_end, high_end, rates):
    axial_low, axial_high = rates[2:4]
    count = v.shape[0]
    row = lax.broadcasted_iota(jnp.int32, v.shape, 0)
    lower = jnp.where(row == 0, low_end, pltpu.roll(v, 1, 0))
    upper = jnp.where(row == count - 1, high_end, pltpu.roll(v, count - 1, 0))
    return axial_low * lower + axial_high * upper - (axial_low + axial_high) * v


def theta_term(prior, v, later, rates):
    theta_low, theta_high = rates[:2]
    return theta_low * prior + theta_high * later - (theta_low + theta_high) * v


def operator(source, shaped, rates, mixers, transposed, rows, finish):
    fields, columns, layers, _ = source.shape
    first, last = rows

    def column(t, _):
        totals = [None] * fields
        for f in range(fields):
            v = shaped(source[f, t + 1, first:last, :])
            low_end = shaped(source[f, t + 1, first - 1 : first, :]) if first > 0 else 0.0
            high_end = shaped(source[f, t + 1, last : last + 1, :]) if last < layers else 0.0
            theta = theta_term(
                shaped(source[f, t, first:last, :]), v, shaped(source[f, t + 2, first:last, :]), rates
            )
            axial = axial_term(v, low_end, high_end, rates)
            mix_into(totals, mixers, transposed, f, (theta, axial, radial_term(v, rates)))
        for g in range(fields):
            finish(g, t, totals[g])
        return 0

    lax.fori_loop(0, columns - 2, column, 0)


def first_step(flow, cotangent, mixers, flow_at, cotangent_at, section, adjoint, reverse):
    columns, layers = flow.shape[1:3]

    def section_at(g, t, total):
        section[g, t] = flow_at(g, t) + time_step * total

    def reverse_at(g, t, total):
        reverse[g, t] = total
        adjoint[g, t] = adjoint_of(cotangent_at(g, t), section[g, t], total)

    operator(flow, shaping, forward_rates, mixers, False, (0, layers), section_at)
    operator(cotangent, identity, reverse_rates, mixers, True, (0, layers), reverse_at)


def adjoint_of(reach, section, reverse):
    return 0.5 * reach + 0.5 * time_step * (1.0 + nonlinear_gain * section) * reverse


def advanced_of(flow, section, total):
    return 0.5 * flow + 0.5 * (section + time_step * total)


def sensitivity_of(reach, adjoint, flow, total):
    return 0.5 * reach + adjoint + time_step * (1.0 + nonlinear_gain * flow) * total


def second_step(section, adjoint, mixers, flow_at, cotangent_at, rows, advanced_to, sensitivity_to):
    inner = slice(*rows)

    def advanced_at(g, t, total):
        advanced_to(g, t, advanced_of(flow_at(g, t), section[g, t + 1, inner, :], total))

    def sensitivity_at(g, t, total):
        value = sensitivity_of(cotangent_at(g, t), adjoint[g, t + 1, inner, :], flow_at(g, t), total)
        sensitivity_to(g, t, value)

    operator(section, shaping, forward_rates, mixers, False, rows, advanced_at)
    operator(adjoint, identity, reverse_rates, mixers, True, rows, sensitivity_at)


def pack_axial_kernel(place, flow, cotangent, xsend, farsend):
    fields, columns, layers, _ = flow.shape
    half = place[HALF]
    for n, source in enumerate((flow, cotangent)):
        for f in range(fields):
            for t in range(columns):
                rows = slice(t, t + 1)
                for depth in range(2):
                    low = source[f, t, depth : depth + 1, :]
                    high = source[f, t, layers - 1 - depth : layers - depth, :]
                    value = jnp.where(half == 1, high, low)
                    xsend[depth, n, f, rows, :] = value
                    if depth == 0:
                        farsend[n, f, rows, :] = value


def pack_column(place, n, f, source, first, send):
    columns, layers = source.shape[1:3]
    pick = place[PICK]
    for depth in range(2):
        rows = slice(depth * layers, (depth + 1) * layers)
        send[n, f, rows, :] = source[f, first + depth - 2 * depth * (first > 0)]
    for t in range(columns):
        low = source[f, t, 0:1, :]
        high = source[f, t, layers - 1 : layers, :]
        rows = slice(2 * layers + t, 2 * layers + t + 1)
        send[n, f, rows, :] = jnp.where(pick == 1, high, low)


def pack_own_kernel(place, flow, cotangent, own, send_wrap):
    fields, columns, layers, _ = flow.shape
    half, even = place[HALF], place[EVEN]
    first = jnp.where(even == 1, 0, columns - 1)
    for n, source in enumerate((flow, cotangent)):
        for f in range(fields):
            pack_column(place, n, f, source, first, send_wrap)
            for t in range(columns):
                for depth in range(2):
                    low = source[f, t, depth : depth + 1, :]
                    high = source[f, t, layers - 1 - depth : layers - depth, :]
                    own[depth, n, f, t : t + 1, :] = jnp.where(half == 1, low, high)


def pack_columns(place, flow, cotangent, send_a, send_b):
    fields, columns = flow.shape[:2]
    first = jnp.where(place[EVEN] == 1, 0, columns - 1)
    for n, source in enumerate((flow, cotangent)):
        for f in range(fields):
            pack_column(place, n, f, source, first, send_b)
            pack_column(place, n, f, source, columns - 1 - first, send_a)


def payload_kernel(place, slots, codes, arrived, own, far, send):
    fields, columns = own.shape[2:4]
    count = slots.shape[1]
    half, rising, sector = place[HALF], place[RISING], place[SECTOR]
    for depth in range(2):
        for n in range(2):
            for f in range(fields):
                k = (depth * 2 + n) * fields + f
                send[4 * fields * half + k] = own[depth, n, f]
                send[4 * fields * (1 - half) + k] = arrived[depth, n, f]
    rest = send.shape[0] - 8 * fields
    for k in range(rest):
        send[8 * fields + k] = jnp.zeros(send.shape[1:], f32)

    @pl.when(place[ACROSS] == 1)
    def _():
        weights = []
        for j in range(columns):
            spot = jnp.where(rising == 1, sector * columns - 1, (sector + 2) * columns + j)
            spot = jnp.where(spot < 0, spot + count, jnp.where(spot >= count, spot - count, spot))
            wanted = jnp.where(rising == 1, j, 0)
            weight = jnp.float32(0.0)
            for k in range(slots.shape[0]):
                share = (codes[k, spot].astype(f32) + 1.0) * (1.0 / 12.0)
                weight = weight + jnp.where(slots[k, spot] == wanted, share, 0.0)
            weights.append(weight)
        for n, shaped in enumerate((shaping, identity)):
            for f in range(fields):
                face = shaped(far[n, f])
                total = weights[0] * face[0:1, :]
                for j in range(1, columns):
                    total = total + weights[j] * face[j : j + 1, :]
                side_row = jnp.where(rising == 1, face[columns - 1 : columns, :], face[0:1, :])
                for k, value in ((n * fields + f, total), ((2 + n) * fields + f, side_row)):
                    send[8 * fields + k // 8, k % 8 : k % 8 + 1, :] = value


def inner_kernel(
    place, mix_t, mix_a, mix_r, flow, cotangent,
    section, adjoint, reverse_ends, advanced, sensitivity, send_a, send_b, reverse,
):
    fields, columns, layers, _ = flow.shape
    mixers = (mix_t, mix_a, mix_r)
    pack_columns(place, flow, cotangent, send_a, send_b)
    first_step(
        flow, cotangent, mixers, lambda g, t: flow[g, t + 1], lambda g, t: cotangent[g, t + 1],
        section, adjoint, reverse,
    )
    for side, a in enumerate((0, layers - 1)):
        for g in range(fields):
            for t in range(columns - 2):
                reverse_ends[side, g, t : t + 1, :] = reverse[g, t, a : a + 1, :]
    rows = (8, layers - 8)
    inner = slice(*rows)

    def advanced_to(g, t, value):
        advanced[g, t] = value

    def sensitivity_to(g, t, value):
        sensitivity[g, t] = value

    second_step(
        section, adjoint, mixers, lambda g, t: flow[g, t + 2, inner, :], lambda g, t: cotangent[g, t + 2, inner, :],
        rows, advanced_to, sensitivity_to,
    )


def outer_kernel(
    place, mix_t, mix_a, mix_r, flow, cotangent, got_a, got_b, got_wrap,
    section_inner, adjoint_inner, reverse_ends,
    section, adjoint, ends, advanced, sensitivity, flow_ends, reach_ends, reverse,
):
    fields, columns, layers, _ = flow.shape
    even = place[EVEN]
    mixers = (mix_t, mix_a, mix_r)
    wide = columns + 2
    for n, (source, both) in enumerate(((flow, flow_ends), (cotangent, reach_ends))):
        for f in range(fields):
            for depth in range(2):
                rows = slice(depth * layers, (depth + 1) * layers)
                from_a = got_a[n, f, rows, :]
                from_b = got_b[n, f, rows, :] + got_wrap[n, f, rows, :]
                both[0, f, 1 - depth] = jnp.where(even == 1, from_b, from_a)
                both[0, f, 2 + depth] = source[f, depth]
                both[1, f, 1 - depth] = source[f, columns - 1 - depth]
                both[1, f, 2 + depth] = jnp.where(even == 1, from_a, from_b)
    section[:, 2 : wide - 2] = section_inner[...]
    adjoint[:, 2 : wide - 2] = adjoint_inner[...]
    rows = (8, layers - 8)
    inner = slice(*rows)
    for side in range(2):
        flow_side, reach_side = flow_ends.at[side], reach_ends.at[side]
        at = slice(wide - 2, wide) if side else slice(0, 2)
        first_step(
            flow_side, reach_side, mixers, lambda g, t: flow_side[g, t + 1], lambda g, t: reach_side[g, t + 1],
            section.at[:, at], adjoint.at[:, at], reverse.at[side],
        )
    for side in range(2):
        at = slice(wide - 4, wide) if side else slice(0, 4)
        own = columns - 2 if side else 0

        def advanced_to(g, t, value):
            advanced[g, 2 * side + t] = value

        def sensitivity_to(g, t, value):
            sensitivity[g, 2 * side + t] = value

        second_step(
            section.at[:, at], adjoint.at[:, at], mixers,
            lambda g, t: flow[g, own + t, inner, :], lambda g, t: cotangent[g, own + t, inner, :],
            rows, advanced_to, sensitivity_to,
        )
    for side, a in enumerate((0, layers - 1)):
        row = slice(a, a + 1)
        for g in range(fields):
            for t in range(wide):
                to = slice(t, t + 1)
                ends[side, 0, g, to, :] = section[g, t, row, :]
                if t < 2 or t >= wide - 2:
                    end, place_in = (0, t) if t < 2 else (1, t - wide + 2)
                    ends[side, 1, g, to, :] = reverse[end, g, place_in, row, :]
                    ends[side, 2, g, to, :] = reach_ends[end, g, place_in + 1, row, :]
                else:
                    ends[side, 1, g, to, :] = reverse_ends[side, g, t - 2 : t - 1, :]
                    ends[side, 2, g, to, :] = cotangent[g, t - 1, row, :]


def last_kernel(
    place, mix_t, mix_a, mix_r, flow, cotangent, section, adjoint, ends, faces, pass_a, pass_b, far,
    got_a, got_b, got_wrap, weights, advanced_inner, sensitivity_inner, advanced_outer, sensitivity_outer,
    advanced, sensitivity,
    far_one, far_two, near, virtual, beyond, ends_two, tiles, section_ends,
):
    fields, columns, layers, radii = flow.shape
    even, pick = place[EVEN], place[PICK]
    mixers = (mix_t, mix_a, mix_r)
    all_rates = (forward_rates, reverse_rates)
    all_shapes = (shaping, identity)
    lanes = [
        [slice((n * fields + f) * radii, (n * fields + f + 1) * radii) for f in range(fields)] for n in range(2)
    ]
    inner = slice(8, layers - 8)
    advanced[:, 2 : columns - 2, inner, :] = advanced_inner[...]
    sensitivity[:, 2 : columns - 2, inner, :] = sensitivity_inner[...]
    for side in range(2):
        at = slice(columns - 2, columns) if side else slice(0, 2)
        from_outer = slice(2 * side, 2 * side + 2)
        advanced[:, at, inner, :] = advanced_outer[:, from_outer]
        sensitivity[:, at, inner, :] = sensitivity_outer[:, from_outer]

    def prior_later(from_a, from_b):
        return jnp.where(even == 1, from_b, from_a), jnp.where(even == 1, from_a, from_b)

    def spot(side, depth, n, f):
        return ((side * 2 + depth) * 2 + n) * fields + f

    def sector_rows(place_in):
        return slice(place_in * columns, (place_in + 1) * columns)

    for side in range(2):
        at_own, at_prior, at_later, at_far = ((2, 1, 3, 0), (1, 0, 2, 3))[side]
        for n, shaped in enumerate(all_shapes):
            for f in range(fields):
                lane = lanes[n][f]
                k = spot(side, 0, n, f)
                prior, later = prior_later(pass_a[k], pass_b[k])
                far_one[side, sector_rows(at_own), lane] = shaped(faces[k])
                far_one[side, sector_rows(at_prior), lane] = shaped(prior)
                far_one[side, sector_rows(at_later), lane] = shaped(later)
                far_one[side, sector_rows(at_far), lane] = shaped(far[n, f])
                k = spot(side, 1, n, f)
                beside = prior_later(pass_a[k], pass_b[k])[side]
                far_two[side, sector_rows(at_own - 1), lane] = shaped(faces[k])
                far_two[side, sector_rows(2 - at_own), lane] = shaped(beside)
                rows = slice(2 * layers, 2 * layers + columns)
                prior, later = prior_later(got_a[n, f, rows, :], got_b[n, f, rows, :] + got_wrap[n, f, rows, :])
                near[side, sector_rows(0), lane] = shaped(prior)
                near[side, sector_rows(2), lane] = shaped(later)
                source = (flow, cotangent)[n]
                at = layers - 1 if side else 0
                for t in range(columns):
                    rows = slice(columns + t, columns + t + 1)
                    near[side, rows, lane] = shaped(source[f, t, at : at + 1, :])

    two = 2 * columns
    for side in range(2):
        virtual[side] = jnp.dot(weights[side, 0:16, :], far_one[side], precision=exact)
        back = jnp.dot(weights[side, 16:32, 0 : 3 * columns], near[side], precision=exact)
        here = jnp.where(pick == side, 1.0, 0.0).astype(f32)
        row = slice(columns + 1, columns + 2) if side else slice(0, 1)
        spot_near = 3 * columns if side else columns - 1
        nearest = slice(spot_near, spot_near + 1)
        values = []
        for n, rates in enumerate(all_rates):
            totals = [None] * fields
            for f in range(fields):
                lane = lanes[n][f]
                k = n * fields + f
                for target, at, k in ((virtual, row, k), (far_one, nearest, k + 2 * fields)):
                    target[side, at, lane] += here * faces[8 * fields + k // 8, k % 8 : k % 8 + 1, :]
                v = far_one[side, columns : columns + two, lane]
                theta = theta_term(
                    far_one[side, columns - 1 : columns - 1 + two, lane], v,
                    far_one[side, columns + 1 : columns + 1 + two, lane], rates,
                )
                lower, upper = far_two[side, :, lane], back[:, lane]
                if side:
                    lower, upper = upper, lower
                axial_low, axial_high = rates[2:4]
                axial = axial_low * lower + axial_high * upper - (axial_low + axial_high) * v
                mix_into(totals, mixers, n == 1, f, (theta, axial, radial_term(v, rates)))
            values.append(totals)
        for g in range(fields):
            k = spot(side, 0, 0, g)
            parts = [faces[k], prior_later(pass_a[k], pass_b[k])[side]]
            one = jnp.concatenate(parts if side else parts[::-1], axis=0) + time_step * values[0][g]
            reach_far = far_one[side, columns : columns + two, lanes[1][g]]
            beyond[side, :, lanes[0][g]] = shaping(one)
            beyond[side, :, lanes[1][g]] = adjoint_of(reach_far, one, values[1][g])
        ends_two[side] = jnp.dot(weights[side, 32:40, 0:two], beyond[side], precision=exact)

        totals = [[None] * fields for _ in range(2)]
        for n in range(2):
            for f in range(fields):
                mix_into(totals[n], mixers[1:2], n == 1, f, (virtual[side, :, lanes[n][f]],))
        a = layers - 8 if side else 0
        edge = lax.broadcasted_iota(jnp.int32, (8, radii), 0) == (7 if side else 0)
        for g in range(fields):
            section_end = ends[side, 0, g] + (time_step * forward_rates[2 + side]) * totals[0][g]
            reverse_end = ends[side, 1, g] + reverse_rates[2 + side] * totals[1][g]
            adjoint_end = adjoint_of(ends[side, 2, g], section_end, reverse_end)
            section_ends[side, g] = section_end
            for t in range(columns + 2):
                to = slice(t, t + 1)
                tile = jnp.where(edge, section_end[to, :], section[g, t, a : a + 8, :])
                tiles[side, 0, g, t] = shaping(tile)
                tiles[side, 1, g, t] = jnp.where(edge, adjoint_end[to, :], adjoint[g, t, a : a + 8, :])

        for t in range(columns):
            for n, (rates, shaped, source) in enumerate(zip(all_rates, all_shapes, (section, adjoint))):
                totals = [None] * fields
                for f in range(fields):
                    v = tiles[side, n, f, t + 1]
                    theta = theta_term(tiles[side, n, f, t], v, tiles[side, n, f, t + 2], rates)
                    far_end = ends_two[side, t : t + 1, lanes[n][f]]
                    b = a - 1 if side else a + 8
                    inner_end = shaped(source[f, t + 1, b : b + 1, :])
                    low_end, high_end = (inner_end, far_end) if side else (far_end, inner_end)
                    axial = axial_term(v, low_end, high_end, rates)
                    mix_into(totals, mixers, n == 1, f, (theta, axial, radial_term(v, rates)))
                rows = slice(a, a + 8)
                for g in range(fields):
                    flow_tile = flow[g, t, rows, :]
                    if n == 0:
                        tile = jnp.where(
                            edge, section_ends[side, g, t + 1 : t + 2, :], section[g, t + 1, rows, :]
                        )
                        advanced[g, t, rows, :] = advanced_of(flow_tile, tile, totals[g])
                    else:
                        sensitivity[g, t, rows, :] = sensitivity_of(
                            cotangent[g, t, rows, :], tiles[side, 1, g, t + 1], flow_tile, totals[g]
                        )


def interface_weights(slots, codes, cells, sector, block, n_block):
    middle = n_block // 2

    def around(table):
        wide = jnp.concatenate([table[-cells:], table, table[: 2 * cells]], axis=0)
        return lax.dynamic_slice_in_dim(wide, sector * cells, 4 * cells, 0)

    slot = around(slots)
    weight = (around(codes).astype(f32) + 1.0) / 12.0
    index = jnp.arange(4 * cells, dtype=jnp.int32)
    rise = cells * (index // cells)[:, None] + slot
    rotor = jnp.arange(6 * cells, dtype=jnp.int32)
    table = jnp.sum((rise[:, :, None] == rotor) * weight[:, :, None], axis=1)

    def padded(block_of):
        rows, columns = block_of.shape
        return jnp.pad(block_of, ((0, 16 - rows), (0, 4 * cells - columns)))

    def plain(rows, columns, shift):
        return (jnp.arange(columns) == jnp.arange(rows)[:, None] + shift).astype(f32)

    ends = cells + 2
    stator = (table[cells - 1 : 2 * cells + 1, 0 : 4 * cells], table[0 : 3 * cells, cells : 3 * cells].T)
    rotor_side = (table[:, 2 * cells - 1 : 3 * cells + 1].T, table[cells : 3 * cells, cells : 4 * cells])
    sides = []
    for at_interface, inside, pair, shifts in (
        (block == middle, block > 0, stator, (2 * cells - 1, 0)),
        (block == middle - 1, block < n_block - 1, rotor_side, (cells - 1, cells)),
    ):
        forth = jnp.where(at_interface, pair[0], plain(ends, 4 * cells, shifts[0])) * inside
        back = jnp.where(at_interface, pair[1], plain(2 * cells, 3 * cells, shifts[1]))
        sides.append(
            jnp.concatenate(
                [padded(forth), padded(back), padded(forth[1 : cells + 1, cells : 3 * cells])[:cells]], axis=0
            )
        )
    return jnp.stack(sides)


def shards(
    flow_state, cotangent, mix_theta, mix_axial, mix_radial, intersection_slot, intersection_code
):
    fields, columns, layers, radii = flow_state.shape
    sector, block = lax.axis_index("azim"), lax.axis_index("block")
    n_sector, n_block = lax.axis_size("azim"), lax.axis_size("block")
    middle = n_block // 2

    at = lambda s, b: s * n_block + b
    sectors, blocks = range(n_sector), range(n_block)
    pairs_a = [(i, i ^ 1) for i in sectors]
    pairs_b = [(i, (i + 1 if i % 2 else i - 1) % n_sector) for i in sectors]
    pairs_wrap = [(i, j) for i, j in pairs_b if abs(i - j) > 1]
    pairs_near = [(i, j) for i, j in pairs_b if abs(i - j) == 1]
    pairs_x = [(b, b - 2) for b in range(2, n_block, 2)] + [(b, b + 2) for b in range(1, n_block - 2, 2)]
    pairs_long = [(b, b ^ 1) for b in blocks]
    pairs_pass = [
        (at(i, b), at(j, b ^ 1 if abs(i - j) > 1 else b)) for i, j in pairs_b for b in blocks
    ]
    pairs_far = []
    for s in sectors:
        inside = s + 2 < n_sector
        pairs_far.append((at(s, middle - 1), at((s + 2) % n_sector, middle + 1 if inside else middle)))
        inside = s >= 2
        pairs_far.append((at(s, middle), at((s - 2) % n_sector, middle - 2 if inside else middle - 1)))

    wrap = (sector == 0) | (sector == n_sector - 1)
    place = jnp.stack(
        [
            block % 2,
            1 - sector % 2,
            block != middle,
            (block == middle + 1) | (block == middle - 2),
            block == middle + 1,
            sector,
        ]
    ).astype(jnp.int32)
    mixers = (mix_theta, mix_axial, mix_radial)

    shape = lambda *dims: jax.ShapeDtypeStruct(dims, f32)
    whole = shape(*flow_state.shape)
    inner = shape(fields, columns - 2, layers, radii)
    wide = shape(fields, columns + 2, layers, radii)
    half_out = shape(fields, columns - 4, layers - 16, radii)
    outer_out = shape(fields, 4, layers - 16, radii)
    face = shape(2, 2, fields, columns, radii)
    side = shape(2, fields, 2 * layers + columns, radii)
    sent = shape(8 * fields + (4 * fields + 7) // 8, columns, radii)
    far_face = shape(2, fields, columns, radii)
    work = 4 * 5 * 5 * 3 * columns * layers * radii

    xsend, farsend = call(
        pack_axial_kernel,
        (place, flow_state, cotangent),
        [face, far_face],
        name="pack_axial",
    )
    arrived = lax.ppermute(xsend, "block", pairs_x)
    far = lax.ppermute(farsend, ("azim", "block"), pairs_far)
    own, send_wrap = call(pack_own_kernel, (place, flow_state, cotangent), [face, side], name="pack_own")
    got_wrap = lax.ppermute(send_wrap, "azim", pairs_wrap)
    (payload,) = call(
        payload_kernel,
        (place, intersection_slot.T, intersection_code.T, arrived, own, far),
        [sent],
        name="payload",
    )
    faces = lax.ppermute(payload, "block", pairs_long)

    place_later, payload = lax.optimization_barrier((place, payload))
    section, adjoint, reverse_ends, advanced_inner, sensitivity_inner, send_a, send_b = call(
        inner_kernel,
        (place_later, *mixers, flow_state, cotangent),
        [inner, inner, shape(2, fields, columns, radii), half_out, half_out, side, side],
        scratch=[inner.shape],
        flops=20 * work,
        name="inner",
    )
    send_a, slots, codes = lax.optimization_barrier((send_a, intersection_slot, intersection_code))
    weights = interface_weights(slots, codes, columns, sector, block, n_block)
    got_a = lax.ppermute(send_a, "azim", pairs_a)
    got_b = lax.ppermute(send_b, "azim", pairs_near)
    faces, section, weights = lax.optimization_barrier((faces, section, weights))
    pass_a = lax.ppermute(faces, "azim", pairs_a)
    pass_b = lax.ppermute(jnp.where(wrap, payload, faces), ("azim", "block"), pairs_pass)
    section, adjoint, ends, advanced_outer, sensitivity_outer = call(
        outer_kernel,
        (place, *mixers, flow_state, cotangent, got_a, got_b, got_wrap, section, adjoint, reverse_ends),
        [wide, wide, shape(2, 3, fields, 16, radii), outer_out, outer_out],
        scratch=[(2, fields, 4, layers, radii), (2, fields, 4, layers, radii), (2, fields, 2, layers, radii)],
        flops=0,
        name="outer",
    )
    span = 2 * fields * radii
    return tuple(
        call(
            last_kernel,
            (place, *mixers, flow_state, cotangent, section, adjoint, ends, faces, pass_a, pass_b, far)
            + (got_a, got_b, got_wrap, weights)
            + (advanced_inner, sensitivity_inner, advanced_outer, sensitivity_outer),
            [whole, whole],
            scratch=[
                (2, 4 * columns, span),
                (2, 2 * columns, span),
                (2, 3 * columns, span),
                (2, 16, span),
                (2, 2 * columns, span),
                (2, columns, span),
                (2, 2, fields, columns + 2, 8, radii),
                (2, fields, 16, radii),
            ],
            flops=0,
            name="last",
        )
    )


def solution(mesh):
    placed = (
        P(None, "azim", "block", None),
        P(None, "azim", "block", None),
        P(),
        P(),
        P(),
        P(),
        P(),
    )
    return jax.shard_map(
        shards,
        mesh=mesh,
        in_specs=placed,
        out_specs=(P(None, "azim", "block", None), P(None, "azim", "block", None)),
        check_vma=False,
    )
```

```python
import jax
import jax.numpy as jnp
from jax import lax
from jax.experimental import pallas as pl
from jax.experimental.pallas import tpu as pltpu
from jax.sharding import PartitionSpec as P

nonlinear_gain = 0.4
time_step = 0.25
forward_rates = (0.55, 0.15, 0.5, 0.2, 0.35, 0.35)
reverse_rates = (0.15, 0.55, 0.2, 0.5, 0.35, 0.35)
HALF, EVEN, PICK, ACROSS, RISING, SECTOR = range(6)

VMEM = pl.BlockSpec(memory_space=pltpu.VMEM)
SMEM = pl.BlockSpec(memory_space=pltpu.SMEM)
f32 = jnp.float32
exact = lax.Precision.HIGHEST


def shaping(v):
    return v + 0.5 * nonlinear_gain * v * v


def identity(v):
    return v


def call(kernel, ins, outs, scratch=(), flops=0, name=None):
    small = lambda x: x.dtype == jnp.int32 or x.ndim < 3
    moved = 4 * (sum(x.size for x in ins) + sum(x.size for x in outs))
    return pl.pallas_call(
        kernel,
        out_shape=outs,
        in_specs=[SMEM if small(x) else VMEM for x in ins],
        out_specs=[VMEM] * len(outs),
        scratch_shapes=[pltpu.VMEM(s, f32) for s in scratch],
        compiler_params=pltpu.CompilerParams(vmem_limit_bytes=24 * 2**20),
        cost_estimate=pl.CostEstimate(flops=flops, bytes_accessed=moved, transcendentals=0),
        name=name,
    )(*ins)


def radial_term(v, rates):
    inner_rate, outer_rate = rates[4:]
    radii = v.shape[1]
    lane = lax.broadcasted_iota(jnp.int32, v.shape, 1)
    inner = jnp.where(lane == 0, 0.0, pltpu.roll(v, 1, 1))
    outer = jnp.where(lane == radii - 1, 0.0, pltpu.roll(v, radii - 1, 1))
    return inner_rate * inner + outer_rate * outer - (inner_rate + outer_rate) * v


def mix_into(totals, mixers, transposed, f, terms):
    for g in range(len(totals)):
        at = (f, g) if transposed else (g, f)
        part = None
        for matrix, term in zip(mixers, terms):
            scaled = matrix[at] * term
            part = scaled if part is None else part + scaled
        totals[g] = part if totals[g] is None else totals[g] + part


def axial_term(v, low_end, high_end, rates):
    axial_low, axial_high = rates[2:4]
    count = v.shape[0]
    row = lax.broadcasted_iota(jnp.int32, v.shape, 0)
    lower = jnp.where(row == 0, low_end, pltpu.roll(v, 1, 0))
    upper = jnp.where(row == count - 1, high_end, pltpu.roll(v, count - 1, 0))
    return axial_low * lower + axial_high * upper - (axial_low + axial_high) * v


def theta_term(prior, v, later, rates):
    theta_low, theta_high = rates[:2]
    return theta_low * prior + theta_high * later - (theta_low + theta_high) * v


def axial_term(v, low_end, high_end, rates):
    axial_low, axial_high = rates[2:4]
    count = v.shape[0]
    row = lax.broadcasted_iota(jnp.int32, v.shape, 0)
    lower = jnp.where(row == 0, low_end, pltpu.roll(v, 1, 0))
    upper = jnp.where(row == count - 1, high_end, pltpu.roll(v, count - 1, 0))
    return axial_low * lower + axial_high * upper - (axial_low + axial_high) * v


def theta_term(prior, v, later, rates):
    theta_low, theta_high = rates[:2]
    return theta_low * prior + theta_high * later - (theta_low + theta_high) * v


def axial_term(v, low_end, high_end, rates):
    axial_low, axial_high = rates[2:4]
    count = v.shape[0]
    row = lax.broadcasted_iota(jnp.int32, v.shape, 0)
    lower = jnp.where(row == 0, low_end, pltpu.roll(v, 1, 0))
    upper = jnp.where(row == count - 1, high_end, pltpu.roll(v, count - 1, 0))
    return axial_low * lower + axial_high * upper - (axial_low + axial_high) * v


def theta_term(prior, v, later, rates):
    theta_low, theta_high = rates[:2]
    return theta_low * prior + theta_high * later - (theta_low + theta_high) * v


def axial_term(v, low_end, high_end, rates):
    axial_low, axial_high = rates[2:4]
    count = v.shape[0]
    row = lax.broadcasted_iota(jnp.int32, v.shape, 0)
    lower = jnp.where(row == 0, low_end, pltpu.roll(v, 1, 0))
    upper = jnp.where(row == count - 1, high_end, pltpu.roll(v, count - 1, 0))
    return axial_low * lower + axial_high * upper - (axial_low + axial_high) * v


def theta_term(prior, v, later, rates):
    theta_low, theta_high = rates[:2]
    return theta_low * prior + theta_high * later - (theta_low + theta_high) * v


def axial_term(v, low_end, high_end, rates):
    axial_low, axial_high = rates[2:4]
    count = v.shape[0]
    row = lax.broadcasted_iota(jnp.int32, v.shape, 0)
    lower = jnp.where(row == 0, low_end, pltpu.roll(v, 1, 0))
    upper = jnp.where(row == count - 1, high_end, pltpu.roll(v, count - 1, 0))
    return axial_low * lower + axial_high * upper - (axial_low + axial_high) * v


def theta_term(prior, v, later, rates):
    theta_low, theta_high = rates[:2]
    return theta_low * prior + theta_high * later - (theta_low + theta_high) * v


def axial_term(v, low_end, high_end, rates):
    axial_low, axial_high = rates[2:4]
    count = v.shape[0]
    row = lax.broadcasted_iota(jnp.int32, v.shape, 0)
    lower = jnp.where(row == 0, low_end, pltpu.roll(v, 1, 0))
    upper = jnp.where(row == count - 1, high_end, pltpu.roll(v, count - 1, 0))
    return axial_low * lower + axial_high * upper - (axial_low + axial_high) * v


def theta_term(prior, v, later, rates):
    theta_low, theta_high = rates[:2]
    return theta_low * prior + theta_high * later - (theta_low + theta_high) * v


def axial_term(v, low_end, high_end, rates):
    axial_low, axial_high = rates[2:4]
    count = v.shape[0]
    row = lax.broadcasted_iota(jnp.int32, v.shape, 0)
    lower = jnp.where(row == 0, low_end, pltpu.roll(v, 1, 0))
    upper = jnp.where(row == count - 1, high_end, pltpu.roll(v, count - 1, 0))
    return axial_low * lower + axial_high * upper - (axial_low + axial_high) * v


def theta_term(prior, v, later, rates):
    theta_low, theta_high = rates[:2]
    return theta_low * prior + theta_high * later - (theta_low + theta_high) * v


def axial_term(v, low_end, high_end, rates):
    axial_low, axial_high = rates[2:4]
    count = v.shape[0]
    row = lax.broadcasted_iota(jnp.int32, v.shape, 0)
    lower = jnp.where(row == 0, low_end, pltpu.roll(v, 1, 0))
    upper = jnp.where(row == count - 1, high_end, pltpu.roll(v, count - 1, 0))
    return axial_low * lower + axial_high * upper - (axial_low + axial_high) * v


def theta_term(prior, v, later, rates):
    theta_low, theta_high = rates[:2]
    return theta_low * prior + theta_high * later - (theta_low + theta_high) * v


def axial_term(v, low_end, high_end, rates):
    axial_low, axial_high = rates[2:4]
    count = v.shape[0]
    row = lax.broadcasted_iota(jnp.int32, v.shape, 0)
    lower = jnp.where(row == 0, low_end, pltpu.roll(v, 1, 0))
    upper = jnp.where(row == count - 1, high_end, pltpu.roll(v, count - 1, 0))
    return axial_low * lower + axial_high * upper - (axial_low + axial_high) * v


def theta_term(prior, v, later, rates):
    theta_low, theta_high = rates[:2]
    return theta_low * prior + theta_high * later - (theta_low + theta_high) * v


def axial_term(v, low_end, high_end, rates):
    axial_low, axial_high = rates[2:4]
    count = v.shape[0]
    row = lax.broadcasted_iota(jnp.int32, v.shape, 0)
    lower = jnp.where(row == 0, low_end, pltpu.roll(v, 1, 0))
    upper = jnp.where(row == count - 1, high_end, pltpu.roll(v, count - 1, 0))
    return axial_low * lower + axial_high * upper - (axial_low + axial_high) * v


def theta_term(prior, v, later, rates):
    theta_low, theta_high = rates[:2]
    return theta_low * prior + theta_high * later - (theta_low + theta_high) * v


def operator(source, shaped, rates, mixers, transposed, rows, finish):
    fields, columns, layers, _ = source.shape
    first, last = rows

    def column(t, _):
        totals = [None] * fields
        for f in range(fields):
            v = shaped(source[f, t + 1, first:last, :])
            low_end = shaped(source[f, t + 1, first - 1 : first, :]) if first > 0 else 0.0
            high_end = shaped(source[f, t + 1, last : last + 1, :]) if last < layers else 0.0
            theta = theta_term(
                shaped(source[f, t, first:last, :]), v, shaped(source[f, t + 2, first:last, :]), rates
            )
            axial = axial_term(v, low_end, high_end, rates)
            mix_into(totals, mixers, transposed, f, (theta, axial, radial_term(v, rates)))
        for g in range(fields):
            finish(g, t, totals[g])
        return 0

    lax.fori_loop(0, columns - 2, column, 0)


def first_step(flow, cotangent, mixers, flow_at, cotangent_at, section, adjoint, reverse):
    columns, layers = flow.shape[1:3]

    def section_at(g, t, total):
        section[g, t] = flow_at(g, t) + time_step * total

    def reverse_at(g, t, total):
        reverse[g, t] = total
        adjoint[g, t] = adjoint_of(cotangent_at(g, t), section[g, t], total)

    operator(flow, shaping, forward_rates, mixers, False, (0, layers), section_at)
    operator(cotangent, identity, reverse_rates, mixers, True, (0, layers), reverse_at)


def adjoint_of(reach, section, reverse):
    return 0.5 * reach + 0.5 * time_step * (1.0 + nonlinear_gain * section) * reverse


def advanced_of(flow, section, total):
    return 0.5 * flow + 0.5 * (section + time_step * total)


def sensitivity_of(reach, adjoint, flow, total):
    return 0.5 * reach + adjoint + time_step * (1.0 + nonlinear_gain * flow) * total


def second_step(section, adjoint, mixers, flow_at, cotangent_at, rows, advanced_to, sensitivity_to):
    inner = slice(*rows)

    def advanced_at(g, t, total):
        advanced_to(g, t, advanced_of(flow_at(g, t), section[g, t + 1, inner, :], total))

    def sensitivity_at(g, t, total):
        value = sensitivity_of(cotangent_at(g, t), adjoint[g, t + 1, inner, :], flow_at(g, t), total)
        sensitivity_to(g, t, value)

    operator(section, shaping, forward_rates, mixers, False, rows, advanced_at)
    operator(adjoint, identity, reverse_rates, mixers, True, rows, sensitivity_at)


def pack_faces_kernel(place, flow, cotangent, face_a, face_b, farsend):
    fields, columns, layers, _ = flow.shape
    half = place[HALF]
    for n, source in enumerate((flow, cotangent)):
        for f in range(fields):
            for t in range(columns):
                rows = slice(t, t + 1)
                for depth in range(2):
                    k = (depth * 2 + n) * fields + f
                    low = source[f, t, depth : depth + 1, :]
                    high = source[f, t, layers - 1 - depth : layers - depth, :]
                    face_a[k, rows, :] = jnp.where(half == 1, low, high)
                    value = jnp.where(half == 1, high, low)
                    face_b[k, rows, :] = value
                    if depth == 0:
                        farsend[k, rows, :] = value


def pack_column(place, n, f, source, first, send):
    columns, layers = source.shape[1:3]
    pick = place[PICK]
    for depth in range(2):
        rows = slice(depth * layers, (depth + 1) * layers)
        send[n, f, rows, :] = source[f, first + depth - 2 * depth * (first > 0)]
    for t in range(columns):
        low = source[f, t, 0:1, :]
        high = source[f, t, layers - 1 : layers, :]
        rows = slice(2 * layers + t, 2 * layers + t + 1)
        send[n, f, rows, :] = jnp.where(pick == 1, high, low)


def pack_columns(place, flow, cotangent, send_a, send_b):
    fields, columns = flow.shape[:2]
    first = jnp.where(place[EVEN] == 1, 0, columns - 1)
    for n, source in enumerate((flow, cotangent)):
        for f in range(fields):
            pack_column(place, n, f, source, first, send_b)
            pack_column(place, n, f, source, columns - 1 - first, send_a)


def payload_kernel(place, slots, codes, face, far, send):
    whole, columns = face.shape[:2]
    fields = whole // 4
    count = slots.shape[1]
    rising, sector = place[RISING], place[SECTOR]
    send[0:whole] = face[...]
    for k in range(whole, send.shape[0]):
        send[k] = jnp.zeros(send.shape[1:], f32)

    @pl.when(place[ACROSS] == 1)
    def _():
        weights = []
        for j in range(columns):
            spot = jnp.where(rising == 1, sector * columns - 1, (sector + 2) * columns + j)
            spot = jnp.where(spot < 0, spot + count, jnp.where(spot >= count, spot - count, spot))
            wanted = jnp.where(rising == 1, j, 0)
            weight = jnp.float32(0.0)
            for k in range(slots.shape[0]):
                share = (codes[k, spot].astype(f32) + 1.0) * (1.0 / 12.0)
                weight = weight + jnp.where(slots[k, spot] == wanted, share, 0.0)
            weights.append(weight)
        for n, shaped in enumerate((shaping, identity)):
            for f in range(fields):
                layer = shaped(far[n * fields + f])
                total = weights[0] * layer[0:1, :]
                for j in range(1, columns):
                    total = total + weights[j] * layer[j : j + 1, :]
                side_row = jnp.where(rising == 1, layer[columns - 1 : columns, :], layer[0:1, :])
                for k, value in ((n * fields + f, total), ((2 + n) * fields + f, side_row)):
                    send[whole + k // 8, k % 8 : k % 8 + 1, :] = value


def inner_kernel(
    place, mix_t, mix_a, mix_r, flow, cotangent,
    section, adjoint, reverse_ends, advanced, sensitivity, send_a, send_b, reverse,
):
    fields, columns, layers, _ = flow.shape
    mixers = (mix_t, mix_a, mix_r)
    pack_columns(place, flow, cotangent, send_a, send_b)
    first_step(
        flow, cotangent, mixers, lambda g, t: flow[g, t + 1], lambda g, t: cotangent[g, t + 1],
        section, adjoint, reverse,
    )
    for side, a in enumerate((0, layers - 1)):
        for g in range(fields):
            for t in range(columns - 2):
                reverse_ends[side, g, t : t + 1, :] = reverse[g, t, a : a + 1, :]
    rows = (8, layers - 8)
    inner = slice(*rows)

    def advanced_to(g, t, value):
        advanced[g, t] = value

    def sensitivity_to(g, t, value):
        sensitivity[g, t] = value

    second_step(
        section, adjoint, mixers, lambda g, t: flow[g, t + 2, inner, :], lambda g, t: cotangent[g, t + 2, inner, :],
        rows, advanced_to, sensitivity_to,
    )


def outer_kernel(
    place, mix_t, mix_a, mix_r, flow, cotangent, got_a, got_b,
    section_inner, adjoint_inner, reverse_ends,
    section, adjoint, ends, advanced, sensitivity, flow_ends, reach_ends, reverse,
):
    fields, columns, layers, _ = flow.shape
    even = place[EVEN]
    mixers = (mix_t, mix_a, mix_r)
    wide = columns + 2
    for n, (source, both) in enumerate(((flow, flow_ends), (cotangent, reach_ends))):
        for f in range(fields):
            for depth in range(2):
                rows = slice(depth * layers, (depth + 1) * layers)
                from_a, from_b = got_a[n, f, rows, :], got_b[n, f, rows, :]
                both[0, f, 1 - depth] = jnp.where(even == 1, from_b, from_a)
                both[0, f, 2 + depth] = source[f, depth]
                both[1, f, 1 - depth] = source[f, columns - 1 - depth]
                both[1, f, 2 + depth] = jnp.where(even == 1, from_a, from_b)
    section[:, 2 : wide - 2] = section_inner[...]
    adjoint[:, 2 : wide - 2] = adjoint_inner[...]
    rows = (8, layers - 8)
    inner = slice(*rows)
    for side in range(2):
        flow_side, reach_side = flow_ends.at[side], reach_ends.at[side]
        at = slice(wide - 2, wide) if side else slice(0, 2)
        first_step(
            flow_side, reach_side, mixers, lambda g, t: flow_side[g, t + 1], lambda g, t: reach_side[g, t + 1],
            section.at[:, at], adjoint.at[:, at], reverse.at[side],
        )
    for side in range(2):
        at = slice(wide - 4, wide) if side else slice(0, 4)
        own = columns - 2 if side else 0

        def advanced_to(g, t, value):
            advanced[g, 2 * side + t] = value

        def sensitivity_to(g, t, value):
            sensitivity[g, 2 * side + t] = value

        second_step(
            section.at[:, at], adjoint.at[:, at], mixers,
            lambda g, t: flow[g, own + t, inner, :], lambda g, t: cotangent[g, own + t, inner, :],
            rows, advanced_to, sensitivity_to,
        )
    for side, a in enumerate((0, layers - 1)):
        row = slice(a, a + 1)
        for g in range(fields):
            for t in range(wide):
                to = slice(t, t + 1)
                ends[side, 0, g, to, :] = section[g, t, row, :]
                if t < 2 or t >= wide - 2:
                    end, place_in = (0, t) if t < 2 else (1, t - wide + 2)
                    ends[side, 1, g, to, :] = reverse[end, g, place_in, row, :]
                    ends[side, 2, g, to, :] = reach_ends[end, g, place_in + 1, row, :]
                else:
                    ends[side, 1, g, to, :] = reverse_ends[side, g, t - 2 : t - 1, :]
                    ends[side, 2, g, to, :] = cotangent[g, t - 1, row, :]


def last_kernel(
    place, mix_t, mix_a, mix_r, flow, cotangent, section, adjoint, ends, long_a, long_b, pass_a, pass_b,
    wrap_a, wrap_b, far, got_a, got_b, weights, advanced_inner, sensitivity_inner, advanced_outer, sensitivity_outer,
    advanced, sensitivity,
    far_one, far_two, near, virtual, beyond, ends_two, tiles, section_ends,
):
    fields, columns, layers, radii = flow.shape
    even, pick = place[EVEN], place[PICK]
    mixers = (mix_t, mix_a, mix_r)
    all_rates = (forward_rates, reverse_rates)
    all_shapes = (shaping, identity)
    lanes = [
        [slice((n * fields + f) * radii, (n * fields + f + 1) * radii) for f in range(fields)] for n in range(2)
    ]
    inner = slice(8, layers - 8)
    advanced[:, 2 : columns - 2, inner, :] = advanced_inner[...]
    sensitivity[:, 2 : columns - 2, inner, :] = sensitivity_inner[...]
    for side in range(2):
        at = slice(columns - 2, columns) if side else slice(0, 2)
        from_outer = slice(2 * side, 2 * side + 2)
        advanced[:, at, inner, :] = advanced_outer[:, from_outer]
        sensitivity[:, at, inner, :] = sensitivity_outer[:, from_outer]

    half = place[HALF]
    whole = 4 * fields

    def prior_later(from_a, from_b):
        return jnp.where(even == 1, from_b, from_a), jnp.where(even == 1, from_a, from_b)

    def of_side(side, from_long_a, from_long_b):
        return jnp.where(half == 1 - side, from_long_a, from_long_b)

    def faces_at(side, k):
        return of_side(side, long_a[k], long_b[k])

    def beside_at(side, k):
        return prior_later(
            of_side(side, pass_a[k], pass_a[whole + k]),
            of_side(side, pass_b[k] + wrap_a[k], pass_b[whole + k] + wrap_b[k]),
        )

    def spot(depth, n, f):
        return (depth * 2 + n) * fields + f

    def sector_rows(place_in):
        return slice(place_in * columns, (place_in + 1) * columns)

    for side in range(2):
        at_own, at_prior, at_later, at_far = ((2, 1, 3, 0), (1, 0, 2, 3))[side]
        for n, shaped in enumerate(all_shapes):
            for f in range(fields):
                lane = lanes[n][f]
                k = spot(0, n, f)
                prior, later = beside_at(side, k)
                far_one[side, sector_rows(at_own), lane] = shaped(faces_at(side, k))
                far_one[side, sector_rows(at_prior), lane] = shaped(prior)
                far_one[side, sector_rows(at_later), lane] = shaped(later)
                far_one[side, sector_rows(at_far), lane] = shaped(far[n * fields + f])
                k = spot(1, n, f)
                beside = beside_at(side, k)[side]
                far_two[side, sector_rows(at_own - 1), lane] = shaped(faces_at(side, k))
                far_two[side, sector_rows(2 - at_own), lane] = shaped(beside)
                rows = slice(2 * layers, 2 * layers + columns)
                prior, later = prior_later(got_a[n, f, rows, :], got_b[n, f, rows, :])
                near[side, sector_rows(0), lane] = shaped(prior)
                near[side, sector_rows(2), lane] = shaped(later)
                source = (flow, cotangent)[n]
                at = layers - 1 if side else 0
                for t in range(columns):
                    rows = slice(columns + t, columns + t + 1)
                    near[side, rows, lane] = shaped(source[f, t, at : at + 1, :])

    two = 2 * columns
    for side in range(2):
        virtual[side] = jnp.dot(weights[side, 0:16, :], far_one[side], precision=exact)
        back = jnp.dot(weights[side, 16:32, 0 : 3 * columns], near[side], precision=exact)
        here = jnp.where(pick == side, 1.0, 0.0).astype(f32)
        row = slice(columns + 1, columns + 2) if side else slice(0, 1)
        spot_near = 3 * columns if side else columns - 1
        nearest = slice(spot_near, spot_near + 1)
        values = []
        for n, rates in enumerate(all_rates):
            totals = [None] * fields
            for f in range(fields):
                lane = lanes[n][f]
                k = n * fields + f
                for target, at, k in ((virtual, row, k), (far_one, nearest, k + 2 * fields)):
                    target[side, at, lane] += here * long_b[whole + k // 8, k % 8 : k % 8 + 1, :]
                v = far_one[side, columns : columns + two, lane]
                theta = theta_term(
                    far_one[side, columns - 1 : columns - 1 + two, lane], v,
                    far_one[side, columns + 1 : columns + 1 + two, lane], rates,
                )
                lower, upper = far_two[side, :, lane], back[:, lane]
                if side:
                    lower, upper = upper, lower
                axial_low, axial_high = rates[2:4]
                axial = axial_low * lower + axial_high * upper - (axial_low + axial_high) * v
                mix_into(totals, mixers, n == 1, f, (theta, axial, radial_term(v, rates)))
            values.append(totals)
        for g in range(fields):
            k = spot(0, 0, g)
            parts = [faces_at(side, k), beside_at(side, k)[side]]
            one = jnp.concatenate(parts if side else parts[::-1], axis=0) + time_step * values[0][g]
            reach_far = far_one[side, columns : columns + two, lanes[1][g]]
            beyond[side, :, lanes[0][g]] = shaping(one)
            beyond[side, :, lanes[1][g]] = adjoint_of(reach_far, one, values[1][g])
        ends_two[side] = jnp.dot(weights[side, 32:40, 0:two], beyond[side], precision=exact)

        totals = [[None] * fields for _ in range(2)]
        for n in range(2):
            for f in range(fields):
                mix_into(totals[n], mixers[1:2], n == 1, f, (virtual[side, :, lanes[n][f]],))
        a = layers - 8 if side else 0
        edge = lax.broadcasted_iota(jnp.int32, (8, radii), 0) == (7 if side else 0)
        for g in range(fields):
            section_end = ends[side, 0, g] + (time_step * forward_rates[2 + side]) * totals[0][g]
            reverse_end = ends[side, 1, g] + reverse_rates[2 + side] * totals[1][g]
            adjoint_end = adjoint_of(ends[side, 2, g], section_end, reverse_end)
            section_ends[side, g] = section_end
            for t in range(columns + 2):
                to = slice(t, t + 1)
                tile = jnp.where(edge, section_end[to, :], section[g, t, a : a + 8, :])
                tiles[side, 0, g, t] = shaping(tile)
                tiles[side, 1, g, t] = jnp.where(edge, adjoint_end[to, :], adjoint[g, t, a : a + 8, :])

        for t in range(columns):
            for n, (rates, shaped, source) in enumerate(zip(all_rates, all_shapes, (section, adjoint))):
                totals = [None] * fields
                for f in range(fields):
                    v = tiles[side, n, f, t + 1]
                    theta = theta_term(tiles[side, n, f, t], v, tiles[side, n, f, t + 2], rates)
                    far_end = ends_two[side, t : t + 1, lanes[n][f]]
                    b = a - 1 if side else a + 8
                    inner_end = shaped(source[f, t + 1, b : b + 1, :])
                    low_end, high_end = (inner_end, far_end) if side else (far_end, inner_end)
                    axial = axial_term(v, low_end, high_end, rates)
                    mix_into(totals, mixers, n == 1, f, (theta, axial, radial_term(v, rates)))
                rows = slice(a, a + 8)
                for g in range(fields):
                    flow_tile = flow[g, t, rows, :]
                    if n == 0:
                        tile = jnp.where(
                            edge, section_ends[side, g, t + 1 : t + 2, :], section[g, t + 1, rows, :]
                        )
                        advanced[g, t, rows, :] = advanced_of(flow_tile, tile, totals[g])
                    else:
                        sensitivity[g, t, rows, :] = sensitivity_of(
                            cotangent[g, t, rows, :], tiles[side, 1, g, t + 1], flow_tile, totals[g]
                        )


def interface_weights(slots, codes, cells, sector, block, n_block):
    middle = n_block // 2

    def around(table):
        wide = jnp.concatenate([table[-cells:], table, table[: 2 * cells]], axis=0)
        return lax.dynamic_slice_in_dim(wide, sector * cells, 4 * cells, 0)

    slot = around(slots)
    weight = (around(codes).astype(f32) + 1.0) / 12.0
    index = jnp.arange(4 * cells, dtype=jnp.int32)
    rise = cells * (index // cells)[:, None] + slot
    rotor = jnp.arange(6 * cells, dtype=jnp.int32)
    table = jnp.sum((rise[:, :, None] == rotor) * weight[:, :, None], axis=1)

    def padded(block_of):
        rows, columns = block_of.shape
        return jnp.pad(block_of, ((0, 16 - rows), (0, 4 * cells - columns)))

    def plain(rows, columns, shift):
        return (jnp.arange(columns) == jnp.arange(rows)[:, None] + shift).astype(f32)

    ends = cells + 2
    stator = (table[cells - 1 : 2 * cells + 1, 0 : 4 * cells], table[0 : 3 * cells, cells : 3 * cells].T)
    rotor_side = (table[:, 2 * cells - 1 : 3 * cells + 1].T, table[cells : 3 * cells, cells : 4 * cells])
    sides = []
    for at_interface, inside, pair, shifts in (
        (block == middle, block > 0, stator, (2 * cells - 1, 0)),
        (block == middle - 1, block < n_block - 1, rotor_side, (cells - 1, cells)),
    ):
        forth = jnp.where(at_interface, pair[0], plain(ends, 4 * cells, shifts[0])) * inside
        back = jnp.where(at_interface, pair[1], plain(2 * cells, 3 * cells, shifts[1]))
        sides.append(
            jnp.concatenate(
                [padded(forth), padded(back), padded(forth[1 : cells + 1, cells : 3 * cells])[:cells]], axis=0
            )
        )
    return jnp.stack(sides)


def shards(
    flow_state, cotangent, mix_theta, mix_axial, mix_radial, intersection_slot, intersection_code
):
    fields, columns, layers, radii = flow_state.shape
    sector, block = lax.axis_index("azim"), lax.axis_index("block")
    n_sector, n_block = lax.axis_size("azim"), lax.axis_size("block")
    middle = n_block // 2

    at = lambda s, b: s * n_block + b
    sectors, blocks = range(n_sector), range(n_block)
    pairs_a = [(i, i ^ 1) for i in sectors]
    pairs_b = [(i, (i + 1 if i % 2 else i - 1) % n_sector) for i in sectors]
    pairs_near = [(i, j) for i, j in pairs_b if abs(i - j) == 1]
    pairs_wrap = [(i, j) for i, j in pairs_b if abs(i - j) > 1]
    axial_a = [(b, b ^ 1) for b in blocks]
    axial_b = [(b, b + 1 if b % 2 else b - 1) for b in blocks if 0 < b < n_block - 1]
    pairs_wrap_a, pairs_wrap_b = (
        [(at(i, b), at(j, c)) for i, j in pairs_wrap for b, c in axial] for axial in (axial_a, axial_b)
    )
    pairs_far, pairs_far_wrap = [], []
    for s in sectors:
        for b, shift in ((middle - 1, 2), (middle, -2)):
            if 0 <= s + shift < n_sector:
                pairs_far.append((at(s, b), at(s + shift, b)))
            else:
                pairs_far_wrap.append((at(s, b), at((s + shift) % n_sector, n_block - 1 - b)))

    place = jnp.stack(
        [
            block % 2,
            1 - sector % 2,
            block != middle,
            (block == middle) | (block == middle - 1),
            block == middle - 1,
            sector,
        ]
    ).astype(jnp.int32)
    mixers = (mix_theta, mix_axial, mix_radial)

    shape = lambda *dims: jax.ShapeDtypeStruct(dims, f32)
    whole = shape(*flow_state.shape)
    inner = shape(fields, columns - 2, layers, radii)
    wide = shape(fields, columns + 2, layers, radii)
    half_out = shape(fields, columns - 4, layers - 16, radii)
    outer_out = shape(fields, 4, layers - 16, radii)
    side = shape(2, fields, 2 * layers + columns, radii)
    face = shape(4 * fields, columns, radii)
    sent = shape(4 * fields + (4 * fields + 7) // 8, columns, radii)
    layer = shape(2 * fields, columns, radii)
    work = 4 * 5 * 5 * 3 * columns * layers * radii

    face_a, face_b, farsend = call(
        pack_faces_kernel, (place, flow_state, cotangent), [face, face, layer], name="pack_faces"
    )
    far = lax.ppermute(farsend, ("azim", "block"), pairs_far)
    long_a = lax.ppermute(face_a, "block", axial_a)
    (payload,) = call(
        payload_kernel, (place, intersection_slot.T, intersection_code.T, face_b, far), [sent], name="payload"
    )
    long_b = lax.ppermute(payload, "block", axial_b)

    place_later, payload = lax.optimization_barrier((place, payload))
    section, adjoint, reverse_ends, advanced_inner, sensitivity_inner, send_a, send_b = call(
        inner_kernel,
        (place_later, *mixers, flow_state, cotangent),
        [inner, inner, shape(2, fields, columns, radii), half_out, half_out, side, side],
        scratch=[inner.shape],
        flops=20 * work,
        name="inner",
    )
    section, face_a, face_b, farsend, slots, codes = lax.optimization_barrier(
        (section, face_a, face_b, farsend, intersection_slot, intersection_code)
    )
    got_b = lax.ppermute(send_b, "azim", pairs_b)
    got_a = lax.ppermute(send_a, "azim", pairs_a)
    wrap_a = lax.ppermute(face_a, ("azim", "block"), pairs_wrap_a)
    wrap_b = lax.ppermute(face_b, ("azim", "block"), pairs_wrap_b)
    far_wrap = lax.ppermute(farsend, ("azim", "block"), pairs_far_wrap)
    weights = interface_weights(slots, codes, columns, sector, block, n_block)

    long_b, section, weights, wrap_a, wrap_b, far_wrap = lax.optimization_barrier(
        (long_b, section, weights, wrap_a, wrap_b, far_wrap)
    )
    both = jnp.concatenate([long_a, long_b[: 4 * fields]])
    pass_a = lax.ppermute(both, "azim", pairs_a)
    pass_b = lax.ppermute(both, "azim", pairs_near)
    section, adjoint, ends, advanced_outer, sensitivity_outer = call(
        outer_kernel,
        (place, *mixers, flow_state, cotangent, got_a, got_b, section, adjoint, reverse_ends),
        [wide, wide, shape(2, 3, fields, 16, radii), outer_out, outer_out],
        scratch=[(2, fields, 4, layers, radii), (2, fields, 4, layers, radii), (2, fields, 2, layers, radii)],
        flops=0,
        name="outer",
    )
    span = 2 * fields * radii
    return tuple(
        call(
            last_kernel,
            (place, *mixers, flow_state, cotangent, section, adjoint, ends, long_a, long_b, pass_a, pass_b)
            + (wrap_a, wrap_b, far_wrap, got_a, got_b, weights)
            + (advanced_inner, sensitivity_inner, advanced_outer, sensitivity_outer),
            [whole, whole],
            scratch=[
                (2, 4 * columns, span),
                (2, 2 * columns, span),
                (2, 3 * columns, span),
                (2, 16, span),
                (2, 2 * columns, span),
                (2, columns, span),
                (2, 2, fields, columns + 2, 8, radii),
                (2, fields, 16, radii),
            ],
            flops=0,
            name="last",
        )
    )


def solution(mesh):
    placed = (
        P(None, "azim", "block", None),
        P(None, "azim", "block", None),
        P(),
        P(),
        P(),
        P(),
        P(),
    )
    return jax.shard_map(
        shards,
        mesh=mesh,
        in_specs=placed,
        out_specs=(P(None, "azim", "block", None), P(None, "azim", "block", None)),
        check_vma=False,
    )
```

```python
import jax
import jax.numpy as jnp
from jax import lax
from jax.experimental import pallas as pl
from jax.experimental.pallas import tpu as pltpu
from jax.sharding import PartitionSpec as P

nonlinear_gain = 0.4
time_step = 0.25
forward_rates = (0.55, 0.15, 0.5, 0.2, 0.35, 0.35)
reverse_rates = (0.15, 0.55, 0.2, 0.5, 0.35, 0.35)
HALF, EVEN, PICK, ACROSS, RISING, SECTOR = range(6)

VMEM = pl.BlockSpec(memory_space=pltpu.VMEM)
SMEM = pl.BlockSpec(memory_space=pltpu.SMEM)
f32 = jnp.float32
exact = lax.Precision.HIGHEST


def shaping(v):
    return v + 0.5 * nonlinear_gain * v * v


def identity(v):
    return v


def call(kernel, ins, outs, scratch=(), flops=0, name=None):
    small = lambda x: x.dtype == jnp.int32 or x.ndim < 3
    moved = 4 * (sum(x.size for x in ins) + sum(x.size for x in outs))
    return pl.pallas_call(
        kernel,
        out_shape=outs,
        in_specs=[SMEM if small(x) else VMEM for x in ins],
        out_specs=[VMEM] * len(outs),
        scratch_shapes=[pltpu.VMEM(s, f32) for s in scratch],
        compiler_params=pltpu.CompilerParams(vmem_limit_bytes=24 * 2**20),
        cost_estimate=pl.CostEstimate(flops=flops, bytes_accessed=moved, transcendentals=0),
        name=name,
    )(*ins)


def radial_term(v, rates):
    inner_rate, outer_rate = rates[4:]
    radii = v.shape[1]
    lane = lax.broadcasted_iota(jnp.int32, v.shape, 1)
    inner = jnp.where(lane == 0, 0.0, pltpu.roll(v, 1, 1))
    outer = jnp.where(lane == radii - 1, 0.0, pltpu.roll(v, radii - 1, 1))
    return inner_rate * inner + outer_rate * outer - (inner_rate + outer_rate) * v


def mix_into(totals, mixers, transposed, f, terms):
    for g in range(len(totals)):
        at = (f, g) if transposed else (g, f)
        part = None
        for matrix, term in zip(mixers, terms):
            scaled = matrix[at] * term
            part = scaled if part is None else part + scaled
        totals[g] = part if totals[g] is None else totals[g] + part


def axial_term(v, low_end, high_end, rates):
    axial_low, axial_high = rates[2:4]
    count = v.shape[0]
    row = lax.broadcasted_iota(jnp.int32, v.shape, 0)
    lower = jnp.where(row == 0, low_end, pltpu.roll(v, 1, 0))
    upper = jnp.where(row == count - 1, high_end, pltpu.roll(v, count - 1, 0))
    return axial_low * lower + axial_high * upper - (axial_low + axial_high) * v


def theta_term(prior, v, later, rates):
    theta_low, theta_high = rates[:2]
    return theta_low * prior + theta_high * later - (theta_low + theta_high) * v


def operator(source, shaped, rates, mixers, transposed, rows, finish):
    fields, columns, layers, _ = source.shape
    first, last = rows

    def column(t, _):
        totals = [None] * fields
        for f in range(fields):
            v = shaped(source[f, t + 1, first:last, :])
            low_end = shaped(source[f, t + 1, first - 1 : first, :]) if first > 0 else 0.0
            high_end = shaped(source[f, t + 1, last : last + 1, :]) if last < layers else 0.0
            theta = theta_term(
                shaped(source[f, t, first:last, :]), v, shaped(source[f, t + 2, first:last, :]), rates
            )
            axial = axial_term(v, low_end, high_end, rates)
            mix_into(totals, mixers, transposed, f, (theta, axial, radial_term(v, rates)))
        for g in range(fields):
            finish(g, t, totals[g])
        return 0

    lax.fori_loop(0, columns - 2, column, 0)


def first_step(flow, cotangent, mixers, flow_at, cotangent_at, section, adjoint, reverse):
    columns, layers = flow.shape[1:3]

    def section_at(g, t, total):
        section[g, t] = flow_at(g, t) + time_step * total

    def reverse_at(g, t, total):
        reverse[g, t] = total
        adjoint[g, t] = adjoint_of(cotangent_at(g, t), section[g, t], total)

    operator(flow, shaping, forward_rates, mixers, False, (0, layers), section_at)
    operator(cotangent, identity, reverse_rates, mixers, True, (0, layers), reverse_at)


def adjoint_of(reach, section, reverse):
    return 0.5 * reach + 0.5 * time_step * (1.0 + nonlinear_gain * section) * reverse


def advanced_of(flow, section, total):
    return 0.5 * flow + 0.5 * (section + time_step * total)


def sensitivity_of(reach, adjoint, flow, total):
    return 0.5 * reach + adjoint + time_step * (1.0 + nonlinear_gain * flow) * total


def second_step(section, adjoint, mixers, flow_at, cotangent_at, rows, advanced_to, sensitivity_to):
    inner = slice(*rows)

    def advanced_at(g, t, total):
        advanced_to(g, t, advanced_of(flow_at(g, t), section[g, t + 1, inner, :], total))

    def sensitivity_at(g, t, total):
        value = sensitivity_of(cotangent_at(g, t), adjoint[g, t + 1, inner, :], flow_at(g, t), total)
        sensitivity_to(g, t, value)

    operator(section, shaping, forward_rates, mixers, False, rows, advanced_at)
    operator(adjoint, identity, reverse_rates, mixers, True, rows, sensitivity_at)


def pack_axial_kernel(place, flow, cotangent, xsend):
    fields, columns, layers, _ = flow.shape
    half = place[HALF]
    for n, source in enumerate((flow, cotangent)):
        for f in range(fields):
            for t in range(columns):
                rows = slice(t, t + 1)
                for depth in range(2):
                    low = source[f, t, depth : depth + 1, :]
                    high = source[f, t, layers - 1 - depth : layers - depth, :]
                    xsend[depth, n, f, rows, :] = jnp.where(half == 1, high, low)


def pack_column(place, n, f, source, first, send):
    columns, layers = source.shape[1:3]
    pick = place[PICK]
    for depth in range(2):
        rows = slice(depth * layers, (depth + 1) * layers)
        send[n, f, rows, :] = source[f, first + depth - 2 * depth * (first > 0)]
    for t in range(columns):
        low = source[f, t, 0:1, :]
        high = source[f, t, layers - 1 : layers, :]
        rows = slice(2 * layers + t, 2 * layers + t + 1)
        send[n, f, rows, :] = jnp.where(pick == 1, high, low)


def pack_own_kernel(place, flow, cotangent, own, send_wrap, farsend):
    fields, columns, layers, _ = flow.shape
    half, even = place[HALF], place[EVEN]
    first = jnp.where(even == 1, 0, columns - 1)
    for n, source in enumerate((flow, cotangent)):
        for f in range(fields):
            pack_column(place, n, f, source, first, send_wrap)
            for t in range(columns):
                for depth in range(2):
                    low = source[f, t, depth : depth + 1, :]
                    high = source[f, t, layers - 1 - depth : layers - depth, :]
                    own[depth, n, f, t : t + 1, :] = jnp.where(half == 1, low, high)
                    if depth == 0:
                        farsend[n, f, t : t + 1, :] = jnp.where(half == 1, high, low)


def pack_columns(place, flow, cotangent, send_a, send_b):
    fields, columns = flow.shape[:2]
    first = jnp.where(place[EVEN] == 1, 0, columns - 1)
    for n, source in enumerate((flow, cotangent)):
        for f in range(fields):
            pack_column(place, n, f, source, first, send_b)
            pack_column(place, n, f, source, columns - 1 - first, send_a)


def payload_kernel(place, slots, codes, arrived, own, far, send):
    fields, columns = own.shape[2:4]
    count = slots.shape[1]
    half, rising, sector = place[HALF], place[RISING], place[SECTOR]
    for depth in range(2):
        for n in range(2):
            for f in range(fields):
                k = (depth * 2 + n) * fields + f
                send[4 * fields * half + k] = own[depth, n, f]
                send[4 * fields * (1 - half) + k] = arrived[depth, n, f]
    rest = send.shape[0] - 8 * fields
    for k in range(rest):
        send[8 * fields + k] = jnp.zeros(send.shape[1:], f32)

    @pl.when(place[ACROSS] == 1)
    def _():
        weights = []
        for j in range(columns):
            spot = jnp.where(rising == 1, sector * columns - 1, (sector + 2) * columns + j)
            spot = jnp.where(spot < 0, spot + count, jnp.where(spot >= count, spot - count, spot))
            wanted = jnp.where(rising == 1, j, 0)
            weight = jnp.float32(0.0)
            for k in range(slots.shape[0]):
                share = (codes[k, spot].astype(f32) + 1.0) * (1.0 / 12.0)
                weight = weight + jnp.where(slots[k, spot] == wanted, share, 0.0)
            weights.append(weight)
        for n, shaped in enumerate((shaping, identity)):
            for f in range(fields):
                face = shaped(far[n, f])
                total = weights[0] * face[0:1, :]
                for j in range(1, columns):
                    total = total + weights[j] * face[j : j + 1, :]
                side_row = jnp.where(rising == 1, face[columns - 1 : columns, :], face[0:1, :])
                for k, value in ((n * fields + f, total), ((2 + n) * fields + f, side_row)):
                    send[8 * fields + k // 8, k % 8 : k % 8 + 1, :] = value


def inner_kernel(
    place, mix_t, mix_a, mix_r, flow, cotangent,
    section, adjoint, reverse_ends, advanced, sensitivity, send_a, send_b, reverse,
):
    fields, columns, layers, _ = flow.shape
    mixers = (mix_t, mix_a, mix_r)
    pack_columns(place, flow, cotangent, send_a, send_b)
    first_step(
        flow, cotangent, mixers, lambda g, t: flow[g, t + 1], lambda g, t: cotangent[g, t + 1],
        section, adjoint, reverse,
    )
    for side, a in enumerate((0, layers - 1)):
        for g in range(fields):
            for t in range(columns - 2):
                reverse_ends[side, g, t : t + 1, :] = reverse[g, t, a : a + 1, :]
    rows = (8, layers - 8)
    inner = slice(*rows)

    def advanced_to(g, t, value):
        advanced[g, t] = value

    def sensitivity_to(g, t, value):
        sensitivity[g, t] = value

    second_step(
        section, adjoint, mixers, lambda g, t: flow[g, t + 2, inner, :], lambda g, t: cotangent[g, t + 2, inner, :],
        rows, advanced_to, sensitivity_to,
    )


def outer_kernel(
    place, mix_t, mix_a, mix_r, flow, cotangent, got_a, got_b, got_wrap,
    section_inner, adjoint_inner, reverse_ends,
    section, adjoint, ends, advanced, sensitivity, flow_ends, reach_ends, reverse,
):
    fields, columns, layers, _ = flow.shape
    even = place[EVEN]
    mixers = (mix_t, mix_a, mix_r)
    wide = columns + 2
    for n, (source, both) in enumerate(((flow, flow_ends), (cotangent, reach_ends))):
        for f in range(fields):
            for depth in range(2):
                rows = slice(depth * layers, (depth + 1) * layers)
                from_a = got_a[n, f, rows, :]
                from_b = got_b[n, f, rows, :] + got_wrap[n, f, rows, :]
                both[0, f, 1 - depth] = jnp.where(even == 1, from_b, from_a)
                both[0, f, 2 + depth] = source[f, depth]
                both[1, f, 1 - depth] = source[f, columns - 1 - depth]
                both[1, f, 2 + depth] = jnp.where(even == 1, from_a, from_b)
    section[:, 2 : wide - 2] = section_inner[...]
    adjoint[:, 2 : wide - 2] = adjoint_inner[...]
    rows = (8, layers - 8)
    inner = slice(*rows)
    for side in range(2):
        flow_side, reach_side = flow_ends.at[side], reach_ends.at[side]
        at = slice(wide - 2, wide) if side else slice(0, 2)
        first_step(
            flow_side, reach_side, mixers, lambda g, t: flow_side[g, t + 1], lambda g, t: reach_side[g, t + 1],
            section.at[:, at], adjoint.at[:, at], reverse.at[side],
        )
    for side in range(2):
        at = slice(wide - 4, wide) if side else slice(0, 4)
        own = columns - 2 if side else 0

        def advanced_to(g, t, value):
            advanced[g, 2 * side + t] = value

        def sensitivity_to(g, t, value):
            sensitivity[g, 2 * side + t] = value

        second_step(
            section.at[:, at], adjoint.at[:, at], mixers,
            lambda g, t: flow[g, own + t, inner, :], lambda g, t: cotangent[g, own + t, inner, :],
            rows, advanced_to, sensitivity_to,
        )
    for side, a in enumerate((0, layers - 1)):
        row = slice(a, a + 1)
        for g in range(fields):
            for t in range(wide):
                to = slice(t, t + 1)
                ends[side, 0, g, to, :] = section[g, t, row, :]
                if t < 2 or t >= wide - 2:
                    end, place_in = (0, t) if t < 2 else (1, t - wide + 2)
                    ends[side, 1, g, to, :] = reverse[end, g, place_in, row, :]
                    ends[side, 2, g, to, :] = reach_ends[end, g, place_in + 1, row, :]
                else:
                    ends[side, 1, g, to, :] = reverse_ends[side, g, t - 2 : t - 1, :]
                    ends[side, 2, g, to, :] = cotangent[g, t - 1, row, :]


def last_kernel(
    place, mix_t, mix_a, mix_r, flow, cotangent, section, adjoint, ends, faces, pass_a, pass_b, pass_wrap, far,
    got_a, got_b, got_wrap, weights, advanced_inner, sensitivity_inner, advanced_outer, sensitivity_outer,
    advanced, sensitivity,
    far_one, far_two, near, virtual, beyond, ends_two, tiles, section_ends,
):
    fields, columns, layers, radii = flow.shape
    even, pick = place[EVEN], place[PICK]
    mixers = (mix_t, mix_a, mix_r)
    all_rates = (forward_rates, reverse_rates)
    all_shapes = (shaping, identity)
    lanes = [
        [slice((n * fields + f) * radii, (n * fields + f + 1) * radii) for f in range(fields)] for n in range(2)
    ]
    inner = slice(8, layers - 8)
    advanced[:, 2 : columns - 2, inner, :] = advanced_inner[...]
    sensitivity[:, 2 : columns - 2, inner, :] = sensitivity_inner[...]
    for side in range(2):
        at = slice(columns - 2, columns) if side else slice(0, 2)
        from_outer = slice(2 * side, 2 * side + 2)
        advanced[:, at, inner, :] = advanced_outer[:, from_outer]
        sensitivity[:, at, inner, :] = sensitivity_outer[:, from_outer]

    def prior_later(from_a, from_b):
        return jnp.where(even == 1, from_b, from_a), jnp.where(even == 1, from_a, from_b)

    def spot(side, depth, n, f):
        return ((side * 2 + depth) * 2 + n) * fields + f

    def sector_rows(place_in):
        return slice(place_in * columns, (place_in + 1) * columns)

    for side in range(2):
        at_own, at_prior, at_later, at_far = ((2, 1, 3, 0), (1, 0, 2, 3))[side]
        for n, shaped in enumerate(all_shapes):
            for f in range(fields):
                lane = lanes[n][f]
                k = spot(side, 0, n, f)
                prior, later = prior_later(pass_a[k], pass_b[k] + pass_wrap[k])
                far_one[side, sector_rows(at_own), lane] = shaped(faces[k])
                far_one[side, sector_rows(at_prior), lane] = shaped(prior)
                far_one[side, sector_rows(at_later), lane] = shaped(later)
                far_one[side, sector_rows(at_far), lane] = shaped(far[n, f])
                k = spot(side, 1, n, f)
                beside = prior_later(pass_a[k], pass_b[k] + pass_wrap[k])[side]
                far_two[side, sector_rows(at_own - 1), lane] = shaped(faces[k])
                far_two[side, sector_rows(2 - at_own), lane] = shaped(beside)
                rows = slice(2 * layers, 2 * layers + columns)
                prior, later = prior_later(got_a[n, f, rows, :], got_b[n, f, rows, :] + got_wrap[n, f, rows, :])
                near[side, sector_rows(0), lane] = shaped(prior)
                near[side, sector_rows(2), lane] = shaped(later)
                source = (flow, cotangent)[n]
                at = layers - 1 if side else 0
                for t in range(columns):
                    rows = slice(columns + t, columns + t + 1)
                    near[side, rows, lane] = shaped(source[f, t, at : at + 1, :])

    two = 2 * columns
    for side in range(2):
        virtual[side] = jnp.dot(weights[side, 0:16, :], far_one[side], precision=exact)
        back = jnp.dot(weights[side, 16:32, 0 : 3 * columns], near[side], precision=exact)
        here = jnp.where(pick == side, 1.0, 0.0).astype(f32)
        row = slice(columns + 1, columns + 2) if side else slice(0, 1)
        spot_near = 3 * columns if side else columns - 1
        nearest = slice(spot_near, spot_near + 1)
        values = []
        for n, rates in enumerate(all_rates):
            totals = [None] * fields
            for f in range(fields):
                lane = lanes[n][f]
                k = n * fields + f
                for target, at, k in ((virtual, row, k), (far_one, nearest, k + 2 * fields)):
                    target[side, at, lane] += here * faces[8 * fields + k // 8, k % 8 : k % 8 + 1, :]
                v = far_one[side, columns : columns + two, lane]
                theta = theta_term(
                    far_one[side, columns - 1 : columns - 1 + two, lane], v,
                    far_one[side, columns + 1 : columns + 1 + two, lane], rates,
                )
                lower, upper = far_two[side, :, lane], back[:, lane]
                if side:
                    lower, upper = upper, lower
                axial_low, axial_high = rates[2:4]
                axial = axial_low * lower + axial_high * upper - (axial_low + axial_high) * v
                mix_into(totals, mixers, n == 1, f, (theta, axial, radial_term(v, rates)))
            values.append(totals)
        for g in range(fields):
            k = spot(side, 0, 0, g)
            parts = [faces[k], prior_later(pass_a[k], pass_b[k] + pass_wrap[k])[side]]
            one = jnp.concatenate(parts if side else parts[::-1], axis=0) + time_step * values[0][g]
            reach_far = far_one[side, columns : columns + two, lanes[1][g]]
            beyond[side, :, lanes[0][g]] = shaping(one)
            beyond[side, :, lanes[1][g]] = adjoint_of(reach_far, one, values[1][g])
        ends_two[side] = jnp.dot(weights[side, 32:40, 0:two], beyond[side], precision=exact)

        totals = [[None] * fields for _ in range(2)]
        for n in range(2):
            for f in range(fields):
                mix_into(totals[n], mixers[1:2], n == 1, f, (virtual[side, :, lanes[n][f]],))
        a = layers - 8 if side else 0
        edge = lax.broadcasted_iota(jnp.int32, (8, radii), 0) == (7 if side else 0)
        for g in range(fields):
            section_end = ends[side, 0, g] + (time_step * forward_rates[2 + side]) * totals[0][g]
            reverse_end = ends[side, 1, g] + reverse_rates[2 + side] * totals[1][g]
            adjoint_end = adjoint_of(ends[side, 2, g], section_end, reverse_end)
            section_ends[side, g] = section_end
            for t in range(columns + 2):
                to = slice(t, t + 1)
                tile = jnp.where(edge, section_end[to, :], section[g, t, a : a + 8, :])
                tiles[side, 0, g, t] = shaping(tile)
                tiles[side, 1, g, t] = jnp.where(edge, adjoint_end[to, :], adjoint[g, t, a : a + 8, :])

        for t in range(columns):
            for n, (rates, shaped, source) in enumerate(zip(all_rates, all_shapes, (section, adjoint))):
                totals = [None] * fields
                for f in range(fields):
                    v = tiles[side, n, f, t + 1]
                    theta = theta_term(tiles[side, n, f, t], v, tiles[side, n, f, t + 2], rates)
                    far_end = ends_two[side, t : t + 1, lanes[n][f]]
                    b = a - 1 if side else a + 8
                    inner_end = shaped(source[f, t + 1, b : b + 1, :])
                    low_end, high_end = (inner_end, far_end) if side else (far_end, inner_end)
                    axial = axial_term(v, low_end, high_end, rates)
                    mix_into(totals, mixers, n == 1, f, (theta, axial, radial_term(v, rates)))
                rows = slice(a, a + 8)
                for g in range(fields):
                    flow_tile = flow[g, t, rows, :]
                    if n == 0:
                        tile = jnp.where(
                            edge, section_ends[side, g, t + 1 : t + 2, :], section[g, t + 1, rows, :]
                        )
                        advanced[g, t, rows, :] = advanced_of(flow_tile, tile, totals[g])
                    else:
                        sensitivity[g, t, rows, :] = sensitivity_of(
                            cotangent[g, t, rows, :], tiles[side, 1, g, t + 1], flow_tile, totals[g]
                        )


def interface_weights(slots, codes, cells, sector, block, n_block):
    middle = n_block // 2

    def around(table):
        wide = jnp.concatenate([table[-cells:], table, table[: 2 * cells]], axis=0)
        return lax.dynamic_slice_in_dim(wide, sector * cells, 4 * cells, 0)

    slot = around(slots)
    weight = (around(codes).astype(f32) + 1.0) / 12.0
    index = jnp.arange(4 * cells, dtype=jnp.int32)
    rise = cells * (index // cells)[:, None] + slot
    rotor = jnp.arange(6 * cells, dtype=jnp.int32)
    table = jnp.sum((rise[:, :, None] == rotor) * weight[:, :, None], axis=1)

    def padded(block_of):
        rows, columns = block_of.shape
        return jnp.pad(block_of, ((0, 16 - rows), (0, 4 * cells - columns)))

    def plain(rows, columns, shift):
        return (jnp.arange(columns) == jnp.arange(rows)[:, None] + shift).astype(f32)

    ends = cells + 2
    stator = (table[cells - 1 : 2 * cells + 1, 0 : 4 * cells], table[0 : 3 * cells, cells : 3 * cells].T)
    rotor_side = (table[:, 2 * cells - 1 : 3 * cells + 1].T, table[cells : 3 * cells, cells : 4 * cells])
    sides = []
    for at_interface, inside, pair, shifts in (
        (block == middle, block > 0, stator, (2 * cells - 1, 0)),
        (block == middle - 1, block < n_block - 1, rotor_side, (cells - 1, cells)),
    ):
        forth = jnp.where(at_interface, pair[0], plain(ends, 4 * cells, shifts[0])) * inside
        back = jnp.where(at_interface, pair[1], plain(2 * cells, 3 * cells, shifts[1]))
        sides.append(
            jnp.concatenate(
                [padded(forth), padded(back), padded(forth[1 : cells + 1, cells : 3 * cells])[:cells]], axis=0
            )
        )
    return jnp.stack(sides)


def shards(
    flow_state, cotangent, mix_theta, mix_axial, mix_radial, intersection_slot, intersection_code
):
    fields, columns, layers, radii = flow_state.shape
    sector, block = lax.axis_index("azim"), lax.axis_index("block")
    n_sector, n_block = lax.axis_size("azim"), lax.axis_size("block")
    middle = n_block // 2

    at = lambda s, b: s * n_block + b
    sectors, blocks = range(n_sector), range(n_block)
    pairs_a = [(i, i ^ 1) for i in sectors]
    pairs_b = [(i, (i + 1 if i % 2 else i - 1) % n_sector) for i in sectors]
    pairs_wrap = [(i, j) for i, j in pairs_b if abs(i - j) > 1]
    pairs_near = [(i, j) for i, j in pairs_b if abs(i - j) == 1]
    pairs_x = [(b, b - 2) for b in range(2, n_block, 2)] + [(b, b + 2) for b in range(1, n_block - 2, 2)]
    pairs_long = [(b, b ^ 1) for b in blocks]
    pairs_pass = [(at(i, b), at(j, b ^ 1)) for i, j in pairs_wrap for b in blocks]
    pairs_far = []
    for s in sectors:
        inside = s + 2 < n_sector
        pairs_far.append((at(s, middle - 1), at((s + 2) % n_sector, middle + 1 if inside else middle)))
        inside = s >= 2
        pairs_far.append((at(s, middle), at((s - 2) % n_sector, middle - 2 if inside else middle - 1)))

    place = jnp.stack(
        [
            block % 2,
            1 - sector % 2,
            block != middle,
            (block == middle + 1) | (block == middle - 2),
            block == middle + 1,
            sector,
        ]
    ).astype(jnp.int32)
    mixers = (mix_theta, mix_axial, mix_radial)

    shape = lambda *dims: jax.ShapeDtypeStruct(dims, f32)
    whole = shape(*flow_state.shape)
    inner = shape(fields, columns - 2, layers, radii)
    wide = shape(fields, columns + 2, layers, radii)
    half_out = shape(fields, columns - 4, layers - 16, radii)
    outer_out = shape(fields, 4, layers - 16, radii)
    face = shape(2, 2, fields, columns, radii)
    side = shape(2, fields, 2 * layers + columns, radii)
    sent = shape(8 * fields + (4 * fields + 7) // 8, columns, radii)
    far_face = shape(2, fields, columns, radii)
    work = 4 * 5 * 5 * 3 * columns * layers * radii

    (xsend,) = call(pack_axial_kernel, (place, flow_state, cotangent), [face], name="pack_axial")
    arrived = lax.ppermute(xsend, "block", pairs_x)
    own, send_wrap, farsend = call(
        pack_own_kernel, (place, flow_state, cotangent), [face, side, far_face], name="pack_own"
    )
    far = lax.ppermute(farsend, ("azim", "block"), pairs_far)
    got_wrap = lax.ppermute(send_wrap, "azim", pairs_wrap)
    (payload,) = call(
        payload_kernel,
        (place, intersection_slot.T, intersection_code.T, arrived, own, far),
        [sent],
        name="payload",
    )
    faces = lax.ppermute(payload, "block", pairs_long)

    place_later, payload = lax.optimization_barrier((place, payload))
    section, adjoint, reverse_ends, advanced_inner, sensitivity_inner, send_a, send_b = call(
        inner_kernel,
        (place_later, *mixers, flow_state, cotangent),
        [inner, inner, shape(2, fields, columns, radii), half_out, half_out, side, side],
        scratch=[inner.shape],
        flops=20 * work,
        name="inner",
    )
    send_a, payload, slots, codes = lax.optimization_barrier(
        (send_a, payload, intersection_slot, intersection_code)
    )
    pass_wrap = lax.ppermute(payload, ("azim", "block"), pairs_pass)
    weights = interface_weights(slots, codes, columns, sector, block, n_block)
    got_a = lax.ppermute(send_a, "azim", pairs_a)
    got_b = lax.ppermute(send_b, "azim", pairs_near)
    faces, section, weights, pass_wrap = lax.optimization_barrier((faces, section, weights, pass_wrap))
    pass_a = lax.ppermute(faces, "azim", pairs_a)
    pass_b = lax.ppermute(faces, "azim", pairs_near)
    section, adjoint, ends, advanced_outer, sensitivity_outer = call(
        outer_kernel,
        (place, *mixers, flow_state, cotangent, got_a, got_b, got_wrap, section, adjoint, reverse_ends),
        [wide, wide, shape(2, 3, fields, 16, radii), outer_out, outer_out],
        scratch=[(2, fields, 4, layers, radii), (2, fields, 4, layers, radii), (2, fields, 2, layers, radii)],
        flops=0,
        name="outer",
    )
    span = 2 * fields * radii
    return tuple(
        call(
            last_kernel,
            (place, *mixers, flow_state, cotangent, section, adjoint, ends, faces, pass_a, pass_b, pass_wrap, far)
            + (got_a, got_b, got_wrap, weights)
            + (advanced_inner, sensitivity_inner, advanced_outer, sensitivity_outer),
            [whole, whole],
            scratch=[
                (2, 4 * columns, span),
                (2, 2 * columns, span),
                (2, 3 * columns, span),
                (2, 16, span),
                (2, 2 * columns, span),
                (2, columns, span),
                (2, 2, fields, columns + 2, 8, radii),
                (2, fields, 16, radii),
            ],
            flops=0,
            name="last",
        )
    )


def solution(mesh):
    placed = (
        P(None, "azim", "block", None),
        P(None, "azim", "block", None),
        P(),
        P(),
        P(),
        P(),
        P(),
    )
    return jax.shard_map(
        shards,
        mesh=mesh,
        in_specs=placed,
        out_specs=(P(None, "azim", "block", None), P(None, "azim", "block", None)),
        check_vma=False,
    )
```

```python
import jax
import jax.numpy as jnp
from jax import lax
from jax.experimental import pallas as pl
from jax.experimental.pallas import tpu as pltpu
from jax.sharding import PartitionSpec as P

nonlinear_gain = 0.4
time_step = 0.25
forward_rates = (0.55, 0.15, 0.5, 0.2, 0.35, 0.35)
reverse_rates = (0.15, 0.55, 0.2, 0.5, 0.35, 0.35)
HALF, EVEN, PICK, ACROSS, RISING, SECTOR = range(6)

VMEM = pl.BlockSpec(memory_space=pltpu.VMEM)
SMEM = pl.BlockSpec(memory_space=pltpu.SMEM)
f32 = jnp.float32
exact = lax.Precision.HIGHEST


def shaping(v):
    return v + 0.5 * nonlinear_gain * v * v


def identity(v):
    return v


def call(kernel, ins, outs, scratch=(), flops=0, name=None):
    small = lambda x: x.dtype == jnp.int32 or x.ndim < 3
    moved = 4 * (sum(x.size for x in ins) + sum(x.size for x in outs))
    return pl.pallas_call(
        kernel,
        out_shape=outs,
        in_specs=[SMEM if small(x) else VMEM for x in ins],
        out_specs=[VMEM] * len(outs),
        scratch_shapes=[pltpu.VMEM(s, f32) for s in scratch],
        compiler_params=pltpu.CompilerParams(vmem_limit_bytes=24 * 2**20),
        cost_estimate=pl.CostEstimate(flops=flops, bytes_accessed=moved, transcendentals=0),
        name=name,
    )(*ins)


def radial_term(v, rates):
    inner_rate, outer_rate = rates[4:]
    radii = v.shape[1]
    lane = lax.broadcasted_iota(jnp.int32, v.shape, 1)
    inner = jnp.where(lane == 0, 0.0, pltpu.roll(v, 1, 1))
    outer = jnp.where(lane == radii - 1, 0.0, pltpu.roll(v, radii - 1, 1))
    return inner_rate * inner + outer_rate * outer - (inner_rate + outer_rate) * v


def mix_into(totals, mixers, transposed, f, terms):
    for g in range(len(totals)):
        at = (f, g) if transposed else (g, f)
        part = None
        for matrix, term in zip(mixers, terms):
            scaled = matrix[at] * term
            part = scaled if part is None else part + scaled
        totals[g] = part if totals[g] is None else totals[g] + part


def axial_term(v, low_end, high_end, rates):
    axial_low, axial_high = rates[2:4]
    count = v.shape[0]
    row = lax.broadcasted_iota(jnp.int32, v.shape, 0)
    lower = jnp.where(row == 0, low_end, pltpu.roll(v, 1, 0))
    upper = jnp.where(row == count - 1, high_end, pltpu.roll(v, count - 1, 0))
    return axial_low * lower + axial_high * upper - (axial_low + axial_high) * v


def theta_term(prior, v, later, rates):
    theta_low, theta_high = rates[:2]
    return theta_low * prior + theta_high * later - (theta_low + theta_high) * v


def operator(source, shaped, rates, mixers, transposed, rows, finish):
    fields, columns, layers, _ = source.shape
    first, last = rows

    def column(t, _):
        totals = [None] * fields
        for f in range(fields):
            v = shaped(source[f, t + 1, first:last, :])
            low_end = shaped(source[f, t + 1, first - 1 : first, :]) if first > 0 else 0.0
            high_end = shaped(source[f, t + 1, last : last + 1, :]) if last < layers else 0.0
            theta = theta_term(
                shaped(source[f, t, first:last, :]), v, shaped(source[f, t + 2, first:last, :]), rates
            )
            axial = axial_term(v, low_end, high_end, rates)
            mix_into(totals, mixers, transposed, f, (theta, axial, radial_term(v, rates)))
        for g in range(fields):
            finish(g, t, totals[g])
        return 0

    lax.fori_loop(0, columns - 2, column, 0)


def first_step(flow, cotangent, mixers, flow_at, cotangent_at, section, adjoint, reverse):
    columns, layers = flow.shape[1:3]

    def section_at(g, t, total):
        section[g, t] = flow_at(g, t) + time_step * total

    def reverse_at(g, t, total):
        reverse[g, t] = total
        adjoint[g, t] = adjoint_of(cotangent_at(g, t), section[g, t], total)

    operator(flow, shaping, forward_rates, mixers, False, (0, layers), section_at)
    operator(cotangent, identity, reverse_rates, mixers, True, (0, layers), reverse_at)


def adjoint_of(reach, section, reverse):
    return 0.5 * reach + 0.5 * time_step * (1.0 + nonlinear_gain * section) * reverse


def advanced_of(flow, section, total):
    return 0.5 * flow + 0.5 * (section + time_step * total)


def sensitivity_of(reach, adjoint, flow, total):
    return 0.5 * reach + adjoint + time_step * (1.0 + nonlinear_gain * flow) * total


def second_step(section, adjoint, mixers, flow_at, cotangent_at, rows, advanced_to, sensitivity_to):
    inner = slice(*rows)

    def advanced_at(g, t, total):
        advanced_to(g, t, advanced_of(flow_at(g, t), section[g, t + 1, inner, :], total))

    def sensitivity_at(g, t, total):
        value = sensitivity_of(cotangent_at(g, t), adjoint[g, t + 1, inner, :], flow_at(g, t), total)
        sensitivity_to(g, t, value)

    operator(section, shaping, forward_rates, mixers, False, rows, advanced_at)
    operator(adjoint, identity, reverse_rates, mixers, True, rows, sensitivity_at)


def pack_axial_kernel(place, flow, cotangent, xsend):
    fields, columns, layers, _ = flow.shape
    half = place[HALF]
    for n, source in enumerate((flow, cotangent)):
        for f in range(fields):
            for t in range(columns):
                rows = slice(t, t + 1)
                for depth in range(2):
                    low = source[f, t, depth : depth + 1, :]
                    high = source[f, t, layers - 1 - depth : layers - depth, :]
                    xsend[depth, n, f, rows, :] = jnp.where(half == 1, high, low)


def pack_column(place, n, f, source, first, send):
    columns, layers = source.shape[1:3]
    pick = place[PICK]
    for depth in range(2):
        rows = slice(depth * layers, (depth + 1) * layers)
        send[n, f, rows, :] = source[f, first + depth - 2 * depth * (first > 0)]
    for t in range(columns):
        low = source[f, t, 0:1, :]
        high = source[f, t, layers - 1 : layers, :]
        rows = slice(2 * layers + t, 2 * layers + t + 1)
        send[n, f, rows, :] = jnp.where(pick == 1, high, low)


def pack_own_kernel(place, flow, cotangent, own, send_wrap, farsend):
    fields, columns, layers, _ = flow.shape
    half, even = place[HALF], place[EVEN]
    first = jnp.where(even == 1, 0, columns - 1)
    for n, source in enumerate((flow, cotangent)):
        for f in range(fields):
            pack_column(place, n, f, source, first, send_wrap)
            for t in range(columns):
                for depth in range(2):
                    low = source[f, t, depth : depth + 1, :]
                    high = source[f, t, layers - 1 - depth : layers - depth, :]
                    own[depth, n, f, t : t + 1, :] = jnp.where(half == 1, low, high)
                    if depth == 0:
                        farsend[n, f, t : t + 1, :] = jnp.where(half == 1, high, low)


def pack_columns(place, flow, cotangent, send_a, send_b):
    fields, columns = flow.shape[:2]
    first = jnp.where(place[EVEN] == 1, 0, columns - 1)
    for n, source in enumerate((flow, cotangent)):
        for f in range(fields):
            pack_column(place, n, f, source, first, send_b)
            pack_column(place, n, f, source, columns - 1 - first, send_a)


def payload_kernel(place, slots, codes, arrived, own, far, send):
    fields, columns = own.shape[2:4]
    count = slots.shape[1]
    half, rising, sector = place[HALF], place[RISING], place[SECTOR]
    for depth in range(2):
        for n in range(2):
            for f in range(fields):
                k = (depth * 2 + n) * fields + f
                send[4 * fields * half + k] = own[depth, n, f]
                send[4 * fields * (1 - half) + k] = arrived[depth, n, f]
    rest = send.shape[0] - 8 * fields
    for k in range(rest):
        send[8 * fields + k] = jnp.zeros(send.shape[1:], f32)

    @pl.when(place[ACROSS] == 1)
    def _():
        weights = []
        for j in range(columns):
            spot = jnp.where(rising == 1, sector * columns - 1, (sector + 2) * columns + j)
            spot = jnp.where(spot < 0, spot + count, jnp.where(spot >= count, spot - count, spot))
            wanted = jnp.where(rising == 1, j, 0)
            weight = jnp.float32(0.0)
            for k in range(slots.shape[0]):
                share = (codes[k, spot].astype(f32) + 1.0) * (1.0 / 12.0)
                weight = weight + jnp.where(slots[k, spot] == wanted, share, 0.0)
            weights.append(weight)
        for n, shaped in enumerate((shaping, identity)):
            for f in range(fields):
                face = shaped(far[n, f])
                total = weights[0] * face[0:1, :]
                for j in range(1, columns):
                    total = total + weights[j] * face[j : j + 1, :]
                side_row = jnp.where(rising == 1, face[columns - 1 : columns, :], face[0:1, :])
                for k, value in ((n * fields + f, total), ((2 + n) * fields + f, side_row)):
                    send[8 * fields + k // 8, k % 8 : k % 8 + 1, :] = value


def inner_kernel(
    place, mix_t, mix_a, mix_r, flow, cotangent,
    section, adjoint, reverse_ends, advanced, sensitivity, send_a, send_b, reverse,
):
    fields, columns, layers, _ = flow.shape
    mixers = (mix_t, mix_a, mix_r)
    pack_columns(place, flow, cotangent, send_a, send_b)
    first_step(
        flow, cotangent, mixers, lambda g, t: flow[g, t + 1], lambda g, t: cotangent[g, t + 1],
        section, adjoint, reverse,
    )
    for side, a in enumerate((0, layers - 1)):
        for g in range(fields):
            for t in range(columns - 2):
                reverse_ends[side, g, t : t + 1, :] = reverse[g, t, a : a + 1, :]
    rows = (8, layers - 8)
    inner = slice(*rows)

    def advanced_to(g, t, value):
        advanced[g, t] = value

    def sensitivity_to(g, t, value):
        sensitivity[g, t] = value

    second_step(
        section, adjoint, mixers, lambda g, t: flow[g, t + 2, inner, :], lambda g, t: cotangent[g, t + 2, inner, :],
        rows, advanced_to, sensitivity_to,
    )


def outer_kernel(
    place, mix_t, mix_a, mix_r, flow, cotangent, got_a, got_b, got_wrap,
    section_inner, adjoint_inner, reverse_ends,
    section, adjoint, ends, advanced, sensitivity, flow_ends, reach_ends, reverse,
):
    fields, columns, layers, _ = flow.shape
    even = place[EVEN]
    mixers = (mix_t, mix_a, mix_r)
    wide = columns + 2
    for n, (source, both) in enumerate(((flow, flow_ends), (cotangent, reach_ends))):
        for f in range(fields):
            for depth in range(2):
                rows = slice(depth * layers, (depth + 1) * layers)
                from_a = got_a[n, f, rows, :]
                from_b = got_b[n, f, rows, :] + got_wrap[n, f, rows, :]
                both[0, f, 1 - depth] = jnp.where(even == 1, from_b, from_a)
                both[0, f, 2 + depth] = source[f, depth]
                both[1, f, 1 - depth] = source[f, columns - 1 - depth]
                both[1, f, 2 + depth] = jnp.where(even == 1, from_a, from_b)
    section[:, 2 : wide - 2] = section_inner[...]
    adjoint[:, 2 : wide - 2] = adjoint_inner[...]
    rows = (8, layers - 8)
    inner = slice(*rows)
    for side in range(2):
        flow_side, reach_side = flow_ends.at[side], reach_ends.at[side]
        at = slice(wide - 2, wide) if side else slice(0, 2)
        first_step(
            flow_side, reach_side, mixers, lambda g, t: flow_side[g, t + 1], lambda g, t: reach_side[g, t + 1],
            section.at[:, at], adjoint.at[:, at], reverse.at[side],
        )
    for side in range(2):
        at = slice(wide - 4, wide) if side else slice(0, 4)
        own = columns - 2 if side else 0

        def advanced_to(g, t, value):
            advanced[g, 2 * side + t] = value

        def sensitivity_to(g, t, value):
            sensitivity[g, 2 * side + t] = value

        second_step(
            section.at[:, at], adjoint.at[:, at], mixers,
            lambda g, t: flow[g, own + t, inner, :], lambda g, t: cotangent[g, own + t, inner, :],
            rows, advanced_to, sensitivity_to,
        )
    for side, a in enumerate((0, layers - 1)):
        row = slice(a, a + 1)
        for g in range(fields):
            for t in range(wide):
                to = slice(t, t + 1)
                ends[side, 0, g, to, :] = section[g, t, row, :]
                if t < 2 or t >= wide - 2:
                    end, place_in = (0, t) if t < 2 else (1, t - wide + 2)
                    ends[side, 1, g, to, :] = reverse[end, g, place_in, row, :]
                    ends[side, 2, g, to, :] = reach_ends[end, g, place_in + 1, row, :]
                else:
                    ends[side, 1, g, to, :] = reverse_ends[side, g, t - 2 : t - 1, :]
                    ends[side, 2, g, to, :] = cotangent[g, t - 1, row, :]


def last_kernel(
    place, mix_t, mix_a, mix_r, flow, cotangent, section, adjoint, ends, faces, pass_a, pass_b, pass_wrap, far,
    got_a, got_b, got_wrap, weights, advanced_inner, sensitivity_inner, advanced_outer, sensitivity_outer,
    advanced, sensitivity,
    far_one, far_two, near, virtual, beyond, ends_two, tiles, section_ends,
):
    fields, columns, layers, radii = flow.shape
    even, pick = place[EVEN], place[PICK]
    mixers = (mix_t, mix_a, mix_r)
    all_rates = (forward_rates, reverse_rates)
    all_shapes = (shaping, identity)
    lanes = [
        [slice((n * fields + f) * radii, (n * fields + f + 1) * radii) for f in range(fields)] for n in range(2)
    ]
    inner = slice(8, layers - 8)
    advanced[:, 2 : columns - 2, inner, :] = advanced_inner[...]
    sensitivity[:, 2 : columns - 2, inner, :] = sensitivity_inner[...]
    for side in range(2):
        at = slice(columns - 2, columns) if side else slice(0, 2)
        from_outer = slice(2 * side, 2 * side + 2)
        advanced[:, at, inner, :] = advanced_outer[:, from_outer]
        sensitivity[:, at, inner, :] = sensitivity_outer[:, from_outer]

    def prior_later(from_a, from_b):
        return jnp.where(even == 1, from_b, from_a), jnp.where(even == 1, from_a, from_b)

    def spot(side, depth, n, f):
        return ((side * 2 + depth) * 2 + n) * fields + f

    def sector_rows(place_in):
        return slice(place_in * columns, (place_in + 1) * columns)

    for side in range(2):
        at_own, at_prior, at_later, at_far = ((2, 1, 3, 0), (1, 0, 2, 3))[side]
        for n, shaped in enumerate(all_shapes):
            for f in range(fields):
                lane = lanes[n][f]
                k = spot(side, 0, n, f)
                prior, later = prior_later(pass_a[k], pass_b[k] + pass_wrap[k])
                far_one[side, sector_rows(at_own), lane] = shaped(faces[k])
                far_one[side, sector_rows(at_prior), lane] = shaped(prior)
                far_one[side, sector_rows(at_later), lane] = shaped(later)
                far_one[side, sector_rows(at_far), lane] = shaped(far[n, f])
                k = spot(side, 1, n, f)
                beside = prior_later(pass_a[k], pass_b[k] + pass_wrap[k])[side]
                far_two[side, sector_rows(at_own - 1), lane] = shaped(faces[k])
                far_two[side, sector_rows(2 - at_own), lane] = shaped(beside)
                rows = slice(2 * layers, 2 * layers + columns)
                prior, later = prior_later(got_a[n, f, rows, :], got_b[n, f, rows, :] + got_wrap[n, f, rows, :])
                near[side, sector_rows(0), lane] = shaped(prior)
                near[side, sector_rows(2), lane] = shaped(later)
                source = (flow, cotangent)[n]
                at = layers - 1 if side else 0
                for t in range(columns):
                    rows = slice(columns + t, columns + t + 1)
                    near[side, rows, lane] = shaped(source[f, t, at : at + 1, :])

    two = 2 * columns
    for side in range(2):
        virtual[side] = jnp.dot(weights[side, 0:16, :], far_one[side], precision=exact)
        back = jnp.dot(weights[side, 16:32, 0 : 3 * columns], near[side], precision=exact)
        here = jnp.where(pick == side, 1.0, 0.0).astype(f32)
        row = slice(columns + 1, columns + 2) if side else slice(0, 1)
        spot_near = 3 * columns if side else columns - 1
        nearest = slice(spot_near, spot_near + 1)
        values = []
        for n, rates in enumerate(all_rates):
            totals = [None] * fields
            for f in range(fields):
                lane = lanes[n][f]
                k = n * fields + f
                for target, at, k in ((virtual, row, k), (far_one, nearest, k + 2 * fields)):
                    target[side, at, lane] += here * faces[8 * fields + k // 8, k % 8 : k % 8 + 1, :]
                v = far_one[side, columns : columns + two, lane]
                theta = theta_term(
                    far_one[side, columns - 1 : columns - 1 + two, lane], v,
                    far_one[side, columns + 1 : columns + 1 + two, lane], rates,
                )
                lower, upper = far_two[side, :, lane], back[:, lane]
                if side:
                    lower, upper = upper, lower
                axial_low, axial_high = rates[2:4]
                axial = axial_low * lower + axial_high * upper - (axial_low + axial_high) * v
                mix_into(totals, mixers, n == 1, f, (theta, axial, radial_term(v, rates)))
            values.append(totals)
        for g in range(fields):
            k = spot(side, 0, 0, g)
            parts = [faces[k], prior_later(pass_a[k], pass_b[k] + pass_wrap[k])[side]]
            one = jnp.concatenate(parts if side else parts[::-1], axis=0) + time_step * values[0][g]
            reach_far = far_one[side, columns : columns + two, lanes[1][g]]
            beyond[side, :, lanes[0][g]] = shaping(one)
            beyond[side, :, lanes[1][g]] = adjoint_of(reach_far, one, values[1][g])
        ends_two[side] = jnp.dot(weights[side, 32:40, 0:two], beyond[side], precision=exact)

        totals = [[None] * fields for _ in range(2)]
        for n in range(2):
            for f in range(fields):
                mix_into(totals[n], mixers[1:2], n == 1, f, (virtual[side, :, lanes[n][f]],))
        a = layers - 8 if side else 0
        edge = lax.broadcasted_iota(jnp.int32, (8, radii), 0) == (7 if side else 0)
        for g in range(fields):
            section_end = ends[side, 0, g] + (time_step * forward_rates[2 + side]) * totals[0][g]
            reverse_end = ends[side, 1, g] + reverse_rates[2 + side] * totals[1][g]
            adjoint_end = adjoint_of(ends[side, 2, g], section_end, reverse_end)
            section_ends[side, g] = section_end
            for t in range(columns + 2):
                to = slice(t, t + 1)
                tile = jnp.where(edge, section_end[to, :], section[g, t, a : a + 8, :])
                tiles[side, 0, g, t] = shaping(tile)
                tiles[side, 1, g, t] = jnp.where(edge, adjoint_end[to, :], adjoint[g, t, a : a + 8, :])

        for t in range(columns):
            for n, (rates, shaped, source) in enumerate(zip(all_rates, all_shapes, (section, adjoint))):
                totals = [None] * fields
                for f in range(fields):
                    v = tiles[side, n, f, t + 1]
                    theta = theta_term(tiles[side, n, f, t], v, tiles[side, n, f, t + 2], rates)
                    far_end = ends_two[side, t : t + 1, lanes[n][f]]
                    b = a - 1 if side else a + 8
                    inner_end = shaped(source[f, t + 1, b : b + 1, :])
                    low_end, high_end = (inner_end, far_end) if side else (far_end, inner_end)
                    axial = axial_term(v, low_end, high_end, rates)
                    mix_into(totals, mixers, n == 1, f, (theta, axial, radial_term(v, rates)))
                rows = slice(a, a + 8)
                for g in range(fields):
                    flow_tile = flow[g, t, rows, :]
                    if n == 0:
                        tile = jnp.where(
                            edge, section_ends[side, g, t + 1 : t + 2, :], section[g, t + 1, rows, :]
                        )
                        advanced[g, t, rows, :] = advanced_of(flow_tile, tile, totals[g])
                    else:
                        sensitivity[g, t, rows, :] = sensitivity_of(
                            cotangent[g, t, rows, :], tiles[side, 1, g, t + 1], flow_tile, totals[g]
                        )


def interface_weights(slots, codes, cells, sector, block, n_block):
    middle = n_block // 2

    def around(table):
        wide = jnp.concatenate([table[-cells:], table, table[: 2 * cells]], axis=0)
        return lax.dynamic_slice_in_dim(wide, sector * cells, 4 * cells, 0)

    slot = around(slots)
    weight = (around(codes).astype(f32) + 1.0) / 12.0
    index = jnp.arange(4 * cells, dtype=jnp.int32)
    rise = cells * (index // cells)[:, None] + slot
    rotor = jnp.arange(6 * cells, dtype=jnp.int32)
    table = jnp.sum((rise[:, :, None] == rotor) * weight[:, :, None], axis=1)

    def padded(block_of):
        rows, columns = block_of.shape
        return jnp.pad(block_of, ((0, 16 - rows), (0, 4 * cells - columns)))

    def plain(rows, columns, shift):
        return (jnp.arange(columns) == jnp.arange(rows)[:, None] + shift).astype(f32)

    ends = cells + 2
    stator = (table[cells - 1 : 2 * cells + 1, 0 : 4 * cells], table[0 : 3 * cells, cells : 3 * cells].T)
    rotor_side = (table[:, 2 * cells - 1 : 3 * cells + 1].T, table[cells : 3 * cells, cells : 4 * cells])
    sides = []
    for at_interface, inside, pair, shifts in (
        (block == middle, block > 0, stator, (2 * cells - 1, 0)),
        (block == middle - 1, block < n_block - 1, rotor_side, (cells - 1, cells)),
    ):
        forth = jnp.where(at_interface, pair[0], plain(ends, 4 * cells, shifts[0])) * inside
        back = jnp.where(at_interface, pair[1], plain(2 * cells, 3 * cells, shifts[1]))
        sides.append(
            jnp.concatenate(
                [padded(forth), padded(back), padded(forth[1 : cells + 1, cells : 3 * cells])[:cells]], axis=0
            )
        )
    return jnp.stack(sides)


def shards(
    flow_state, cotangent, mix_theta, mix_axial, mix_radial, intersection_slot, intersection_code
):
    fields, columns, layers, radii = flow_state.shape
    sector, block = lax.axis_index("azim"), lax.axis_index("block")
    n_sector, n_block = lax.axis_size("azim"), lax.axis_size("block")
    middle = n_block // 2

    at = lambda s, b: s * n_block + b
    sectors, blocks = range(n_sector), range(n_block)
    pairs_a = [(i, i ^ 1) for i in sectors]
    pairs_b = [(i, (i + 1 if i % 2 else i - 1) % n_sector) for i in sectors]
    pairs_wrap = [(i, j) for i, j in pairs_b if abs(i - j) > 1]
    pairs_near = [(i, j) for i, j in pairs_b if abs(i - j) == 1]
    pairs_x = [(b, b - 2) for b in range(2, n_block, 2)] + [(b, b + 2) for b in range(1, n_block - 2, 2)]
    pairs_long = [(b, b ^ 1) for b in blocks]
    pairs_pass = [(at(i, b), at(j, b ^ 1)) for i, j in pairs_wrap for b in blocks]
    pairs_far, pairs_far_wrap = [], []
    for s in sectors:
        for b, shift, relay in ((middle - 1, 2, middle + 1), (middle, -2, middle - 2)):
            if 0 <= s + shift < n_sector:
                pairs_far.append((at(s, b), at(s + shift, relay)))
            else:
                pairs_far_wrap.append((at(s, b), at((s + shift) % n_sector, n_block - 1 - b)))

    place = jnp.stack(
        [
            block % 2,
            1 - sector % 2,
            block != middle,
            (block == middle + 1) | (block == middle - 2),
            block == middle + 1,
            sector,
        ]
    ).astype(jnp.int32)
    mixers = (mix_theta, mix_axial, mix_radial)

    shape = lambda *dims: jax.ShapeDtypeStruct(dims, f32)
    whole = shape(*flow_state.shape)
    inner = shape(fields, columns - 2, layers, radii)
    wide = shape(fields, columns + 2, layers, radii)
    half_out = shape(fields, columns - 4, layers - 16, radii)
    outer_out = shape(fields, 4, layers - 16, radii)
    face = shape(2, 2, fields, columns, radii)
    side = shape(2, fields, 2 * layers + columns, radii)
    sent = shape(8 * fields + (4 * fields + 7) // 8, columns, radii)
    far_face = shape(2, fields, columns, radii)
    work = 4 * 5 * 5 * 3 * columns * layers * radii

    (xsend,) = call(pack_axial_kernel, (place, flow_state, cotangent), [face], name="pack_axial")
    arrived = lax.ppermute(xsend, "block", pairs_x)
    own, send_wrap, farsend = call(
        pack_own_kernel, (place, flow_state, cotangent), [face, side, far_face], name="pack_own"
    )
    far = lax.ppermute(farsend, ("azim", "block"), pairs_far)
    got_wrap = lax.ppermute(send_wrap, "azim", pairs_wrap)
    (payload,) = call(
        payload_kernel,
        (place, intersection_slot.T, intersection_code.T, arrived, own, far),
        [sent],
        name="payload",
    )
    faces = lax.ppermute(payload, "block", pairs_long)

    place_later, payload = lax.optimization_barrier((place, payload))
    section, adjoint, reverse_ends, advanced_inner, sensitivity_inner, send_a, send_b = call(
        inner_kernel,
        (place_later, *mixers, flow_state, cotangent),
        [inner, inner, shape(2, fields, columns, radii), half_out, half_out, side, side],
        scratch=[inner.shape],
        flops=20 * work,
        name="inner",
    )
    send_a, payload, farsend, slots, codes = lax.optimization_barrier(
        (send_a, payload, farsend, intersection_slot, intersection_code)
    )
    pass_wrap = lax.ppermute(payload, ("azim", "block"), pairs_pass)
    far_wrap = lax.ppermute(farsend, ("azim", "block"), pairs_far_wrap)
    weights = interface_weights(slots, codes, columns, sector, block, n_block)
    got_a = lax.ppermute(send_a, "azim", pairs_a)
    got_b = lax.ppermute(send_b, "azim", pairs_near)
    faces, section, weights, pass_wrap, far_wrap = lax.optimization_barrier(
        (faces, section, weights, pass_wrap, far_wrap)
    )
    pass_a = lax.ppermute(faces, "azim", pairs_a)
    pass_b = lax.ppermute(faces, "azim", pairs_near)
    section, adjoint, ends, advanced_outer, sensitivity_outer = call(
        outer_kernel,
        (place, *mixers, flow_state, cotangent, got_a, got_b, got_wrap, section, adjoint, reverse_ends),
        [wide, wide, shape(2, 3, fields, 16, radii), outer_out, outer_out],
        scratch=[(2, fields, 4, layers, radii), (2, fields, 4, layers, radii), (2, fields, 2, layers, radii)],
        flops=0,
        name="outer",
    )
    span = 2 * fields * radii
    return tuple(
        call(
            last_kernel,
            (place, *mixers, flow_state, cotangent, section, adjoint, ends, faces, pass_a, pass_b, pass_wrap, far_wrap)
            + (got_a, got_b, got_wrap, weights)
            + (advanced_inner, sensitivity_inner, advanced_outer, sensitivity_outer),
            [whole, whole],
            scratch=[
                (2, 4 * columns, span),
                (2, 2 * columns, span),
                (2, 3 * columns, span),
                (2, 16, span),
                (2, 2 * columns, span),
                (2, columns, span),
                (2, 2, fields, columns + 2, 8, radii),
                (2, fields, 16, radii),
            ],
            flops=0,
            name="last",
        )
    )


def solution(mesh):
    placed = (
        P(None, "azim", "block", None),
        P(None, "azim", "block", None),
        P(),
        P(),
        P(),
        P(),
        P(),
    )
    return jax.shard_map(
        shards,
        mesh=mesh,
        in_specs=placed,
        out_specs=(P(None, "azim", "block", None), P(None, "azim", "block", None)),
        check_vma=False,
    )
```

```python
import jax
import jax.numpy as jnp
from jax import lax
from jax.experimental import pallas as pl
from jax.experimental.pallas import tpu as pltpu
from jax.sharding import PartitionSpec as P

nonlinear_gain = 0.4
time_step = 0.25
forward_rates = (0.55, 0.15, 0.5, 0.2, 0.35, 0.35)
reverse_rates = (0.15, 0.55, 0.2, 0.5, 0.35, 0.35)
HALF, EVEN, PICK, ACROSS, RISING, SECTOR = range(6)

VMEM = pl.BlockSpec(memory_space=pltpu.VMEM)
SMEM = pl.BlockSpec(memory_space=pltpu.SMEM)
f32 = jnp.float32
exact = lax.Precision.HIGHEST


def shaping(v):
    return v + 0.5 * nonlinear_gain * v * v


def identity(v):
    return v


def call(kernel, ins, outs, scratch=(), flops=0, name=None):
    small = lambda x: x.dtype == jnp.int32 or x.ndim < 3
    moved = 4 * (sum(x.size for x in ins) + sum(x.size for x in outs))
    return pl.pallas_call(
        kernel,
        out_shape=outs,
        in_specs=[SMEM if small(x) else VMEM for x in ins],
        out_specs=[VMEM] * len(outs),
        scratch_shapes=[pltpu.VMEM(s, f32) for s in scratch],
        compiler_params=pltpu.CompilerParams(vmem_limit_bytes=24 * 2**20),
        cost_estimate=pl.CostEstimate(flops=flops, bytes_accessed=moved, transcendentals=0),
        name=name,
    )(*ins)


def radial_term(v, rates):
    inner_rate, outer_rate = rates[4:]
    radii = v.shape[1]
    lane = lax.broadcasted_iota(jnp.int32, v.shape, 1)
    inner = jnp.where(lane == 0, 0.0, pltpu.roll(v, 1, 1))
    outer = jnp.where(lane == radii - 1, 0.0, pltpu.roll(v, radii - 1, 1))
    return inner_rate * inner + outer_rate * outer - (inner_rate + outer_rate) * v


def mix_into(totals, mixers, transposed, f, terms):
    for g in range(len(totals)):
        at = (f, g) if transposed else (g, f)
        part = None
        for matrix, term in zip(mixers, terms):
            scaled = matrix[at] * term
            part = scaled if part is None else part + scaled
        totals[g] = part if totals[g] is None else totals[g] + part


def axial_term(v, low_end, high_end, rates):
    axial_low, axial_high = rates[2:4]
    count = v.shape[0]
    row = lax.broadcasted_iota(jnp.int32, v.shape, 0)
    lower = jnp.where(row == 0, low_end, pltpu.roll(v, 1, 0))
    upper = jnp.where(row == count - 1, high_end, pltpu.roll(v, count - 1, 0))
    return axial_low * lower + axial_high * upper - (axial_low + axial_high) * v


def theta_term(prior, v, later, rates):
    theta_low, theta_high = rates[:2]
    return theta_low * prior + theta_high * later - (theta_low + theta_high) * v


def operator(source, shaped, rates, mixers, transposed, rows, finish):
    fields, columns, layers, _ = source.shape
    first, last = rows

    def column(t, _):
        totals = [None] * fields
        for f in range(fields):
            v = shaped(source[f, t + 1, first:last, :])
            low_end = shaped(source[f, t + 1, first - 1 : first, :]) if first > 0 else 0.0
            high_end = shaped(source[f, t + 1, last : last + 1, :]) if last < layers else 0.0
            theta = theta_term(
                shaped(source[f, t, first:last, :]), v, shaped(source[f, t + 2, first:last, :]), rates
            )
            axial = axial_term(v, low_end, high_end, rates)
            mix_into(totals, mixers, transposed, f, (theta, axial, radial_term(v, rates)))
        for g in range(fields):
            finish(g, t, totals[g])
        return 0

    lax.fori_loop(0, columns - 2, column, 0)


def first_step(flow, cotangent, mixers, flow_at, cotangent_at, section, adjoint, reverse):
    columns, layers = flow.shape[1:3]

    def section_at(g, t, total):
        section[g, t] = flow_at(g, t) + time_step * total

    def reverse_at(g, t, total):
        reverse[g, t] = total
        adjoint[g, t] = adjoint_of(cotangent_at(g, t), section[g, t], total)

    operator(flow, shaping, forward_rates, mixers, False, (0, layers), section_at)
    operator(cotangent, identity, reverse_rates, mixers, True, (0, layers), reverse_at)


def adjoint_of(reach, section, reverse):
    return 0.5 * reach + 0.5 * time_step * (1.0 + nonlinear_gain * section) * reverse


def advanced_of(flow, section, total):
    return 0.5 * flow + 0.5 * (section + time_step * total)


def sensitivity_of(reach, adjoint, flow, total):
    return 0.5 * reach + adjoint + time_step * (1.0 + nonlinear_gain * flow) * total


def second_step(section, adjoint, mixers, flow_at, cotangent_at, rows, advanced_to, sensitivity_to):
    inner = slice(*rows)

    def advanced_at(g, t, total):
        advanced_to(g, t, advanced_of(flow_at(g, t), section[g, t + 1, inner, :], total))

    def sensitivity_at(g, t, total):
        value = sensitivity_of(cotangent_at(g, t), adjoint[g, t + 1, inner, :], flow_at(g, t), total)
        sensitivity_to(g, t, value)

    operator(section, shaping, forward_rates, mixers, False, rows, advanced_at)
    operator(adjoint, identity, reverse_rates, mixers, True, rows, sensitivity_at)


def pack_axial_kernel(place, flow, cotangent, xsend):
    fields, columns, layers, _ = flow.shape
    half = place[HALF]
    for n, source in enumerate((flow, cotangent)):
        for f in range(fields):
            for t in range(columns):
                rows = slice(t, t + 1)
                for depth in range(2):
                    low = source[f, t, depth : depth + 1, :]
                    high = source[f, t, layers - 1 - depth : layers - depth, :]
                    xsend[depth, n, f, rows, :] = jnp.where(half == 1, high, low)


def pack_column(place, n, f, source, first, send):
    columns, layers = source.shape[1:3]
    pick = place[PICK]
    for depth in range(2):
        rows = slice(depth * layers, (depth + 1) * layers)
        send[n, f, rows, :] = source[f, first + depth - 2 * depth * (first > 0)]
    for t in range(columns):
        low = source[f, t, 0:1, :]
        high = source[f, t, layers - 1 : layers, :]
        rows = slice(2 * layers + t, 2 * layers + t + 1)
        send[n, f, rows, :] = jnp.where(pick == 1, high, low)


def pack_own_kernel(place, flow, cotangent, own, send_wrap, farsend):
    fields, columns, layers, _ = flow.shape
    half, even = place[HALF], place[EVEN]
    first = jnp.where(even == 1, 0, columns - 1)
    for n, source in enumerate((flow, cotangent)):
        for f in range(fields):
            pack_column(place, n, f, source, first, send_wrap)
            for t in range(columns):
                for depth in range(2):
                    low = source[f, t, depth : depth + 1, :]
                    high = source[f, t, layers - 1 - depth : layers - depth, :]
                    own[depth, n, f, t : t + 1, :] = jnp.where(half == 1, low, high)
                    if depth == 0:
                        farsend[n, f, t : t + 1, :] = jnp.where(half == 1, high, low)


def pack_columns(place, flow, cotangent, send_a, send_b):
    fields, columns = flow.shape[:2]
    first = jnp.where(place[EVEN] == 1, 0, columns - 1)
    for n, source in enumerate((flow, cotangent)):
        for f in range(fields):
            pack_column(place, n, f, source, first, send_b)
            pack_column(place, n, f, source, columns - 1 - first, send_a)


def payload_kernel(place, slots, codes, arrived, own, far, send):
    fields, columns = own.shape[2:4]
    count = slots.shape[1]
    half, rising, sector = place[HALF], place[RISING], place[SECTOR]
    for depth in range(2):
        for n in range(2):
            for f in range(fields):
                k = (depth * 2 + n) * fields + f
                send[4 * fields * half + k] = own[depth, n, f]
                send[4 * fields * (1 - half) + k] = arrived[depth, n, f]
    rest = send.shape[0] - 8 * fields
    for k in range(rest):
        send[8 * fields + k] = jnp.zeros(send.shape[1:], f32)

    @pl.when(place[ACROSS] == 1)
    def _():
        weights = []
        for j in range(columns):
            spot = jnp.where(rising == 1, sector * columns - 1, (sector + 2) * columns + j)
            spot = jnp.where(spot < 0, spot + count, jnp.where(spot >= count, spot - count, spot))
            wanted = jnp.where(rising == 1, j, 0)
            weight = jnp.float32(0.0)
            for k in range(slots.shape[0]):
                share = (codes[k, spot].astype(f32) + 1.0) * (1.0 / 12.0)
                weight = weight + jnp.where(slots[k, spot] == wanted, share, 0.0)
            weights.append(weight)
        for n, shaped in enumerate((shaping, identity)):
            for f in range(fields):
                face = shaped(far[n, f])
                total = weights[0] * face[0:1, :]
                for j in range(1, columns):
                    total = total + weights[j] * face[j : j + 1, :]
                side_row = jnp.where(rising == 1, face[columns - 1 : columns, :], face[0:1, :])
                for k, value in ((n * fields + f, total), ((2 + n) * fields + f, side_row)):
                    send[8 * fields + k // 8, k % 8 : k % 8 + 1, :] = value


def inner_kernel(
    place, mix_t, mix_a, mix_r, flow, cotangent,
    section, adjoint, reverse_ends, advanced, sensitivity, send_a, send_b, reverse,
):
    fields, columns, layers, _ = flow.shape
    mixers = (mix_t, mix_a, mix_r)
    pack_columns(place, flow, cotangent, send_a, send_b)
    first_step(
        flow, cotangent, mixers, lambda g, t: flow[g, t + 1], lambda g, t: cotangent[g, t + 1],
        section, adjoint, reverse,
    )
    for side, a in enumerate((0, layers - 1)):
        for g in range(fields):
            for t in range(columns - 2):
                reverse_ends[side, g, t : t + 1, :] = reverse[g, t, a : a + 1, :]
    rows = (8, layers - 8)
    inner = slice(*rows)

    def advanced_to(g, t, value):
        advanced[g, t] = value

    def sensitivity_to(g, t, value):
        sensitivity[g, t] = value

    second_step(
        section, adjoint, mixers, lambda g, t: flow[g, t + 2, inner, :], lambda g, t: cotangent[g, t + 2, inner, :],
        rows, advanced_to, sensitivity_to,
    )


def outer_kernel(
    place, mix_t, mix_a, mix_r, flow, cotangent, got_a, got_b, got_wrap,
    section_inner, adjoint_inner, reverse_ends,
    section, adjoint, ends, advanced, sensitivity, flow_ends, reach_ends, reverse,
):
    fields, columns, layers, _ = flow.shape
    even = place[EVEN]
    mixers = (mix_t, mix_a, mix_r)
    wide = columns + 2
    for n, (source, both) in enumerate(((flow, flow_ends), (cotangent, reach_ends))):
        for f in range(fields):
            for depth in range(2):
                rows = slice(depth * layers, (depth + 1) * layers)
                from_a = got_a[n, f, rows, :]
                from_b = got_b[n, f, rows, :] + got_wrap[n, f, rows, :]
                both[0, f, 1 - depth] = jnp.where(even == 1, from_b, from_a)
                both[0, f, 2 + depth] = source[f, depth]
                both[1, f, 1 - depth] = source[f, columns - 1 - depth]
                both[1, f, 2 + depth] = jnp.where(even == 1, from_a, from_b)
    section[:, 2 : wide - 2] = section_inner[...]
    adjoint[:, 2 : wide - 2] = adjoint_inner[...]
    rows = (8, layers - 8)
    inner = slice(*rows)
    for side in range(2):
        flow_side, reach_side = flow_ends.at[side], reach_ends.at[side]
        at = slice(wide - 2, wide) if side else slice(0, 2)
        first_step(
            flow_side, reach_side, mixers, lambda g, t: flow_side[g, t + 1], lambda g, t: reach_side[g, t + 1],
            section.at[:, at], adjoint.at[:, at], reverse.at[side],
        )
    for side in range(2):
        at = slice(wide - 4, wide) if side else slice(0, 4)
        own = columns - 2 if side else 0

        def advanced_to(g, t, value):
            advanced[g, 2 * side + t] = value

        def sensitivity_to(g, t, value):
            sensitivity[g, 2 * side + t] = value

        second_step(
            section.at[:, at], adjoint.at[:, at], mixers,
            lambda g, t: flow[g, own + t, inner, :], lambda g, t: cotangent[g, own + t, inner, :],
            rows, advanced_to, sensitivity_to,
        )
    for side, a in enumerate((0, layers - 1)):
        row = slice(a, a + 1)
        for g in range(fields):
            for t in range(wide):
                to = slice(t, t + 1)
                ends[side, 0, g, to, :] = section[g, t, row, :]
                if t < 2 or t >= wide - 2:
                    end, place_in = (0, t) if t < 2 else (1, t - wide + 2)
                    ends[side, 1, g, to, :] = reverse[end, g, place_in, row, :]
                    ends[side, 2, g, to, :] = reach_ends[end, g, place_in + 1, row, :]
                else:
                    ends[side, 1, g, to, :] = reverse_ends[side, g, t - 2 : t - 1, :]
                    ends[side, 2, g, to, :] = cotangent[g, t - 1, row, :]


def last_kernel(
    place, mix_t, mix_a, mix_r, flow, cotangent, section, adjoint, ends, faces, pass_a, pass_b, pass_wrap, far,
    got_a, got_b, got_wrap, weights, advanced_inner, sensitivity_inner, advanced_outer, sensitivity_outer,
    advanced, sensitivity,
    far_one, far_two, near, virtual, beyond, ends_two, tiles, section_ends,
):
    fields, columns, layers, radii = flow.shape
    even, pick = place[EVEN], place[PICK]
    mixers = (mix_t, mix_a, mix_r)
    all_rates = (forward_rates, reverse_rates)
    all_shapes = (shaping, identity)
    lanes = [
        [slice((n * fields + f) * radii, (n * fields + f + 1) * radii) for f in range(fields)] for n in range(2)
    ]
    inner = slice(8, layers - 8)
    advanced[:, 2 : columns - 2, inner, :] = advanced_inner[...]
    sensitivity[:, 2 : columns - 2, inner, :] = sensitivity_inner[...]
    for side in range(2):
        at = slice(columns - 2, columns) if side else slice(0, 2)
        from_outer = slice(2 * side, 2 * side + 2)
        advanced[:, at, inner, :] = advanced_outer[:, from_outer]
        sensitivity[:, at, inner, :] = sensitivity_outer[:, from_outer]

    def prior_later(from_a, from_b):
        return jnp.where(even == 1, from_b, from_a), jnp.where(even == 1, from_a, from_b)

    def spot(side, depth, n, f):
        return ((side * 2 + depth) * 2 + n) * fields + f

    def sector_rows(place_in):
        return slice(place_in * columns, (place_in + 1) * columns)

    for side in range(2):
        at_own, at_prior, at_later, at_far = ((2, 1, 3, 0), (1, 0, 2, 3))[side]
        for n, shaped in enumerate(all_shapes):
            for f in range(fields):
                lane = lanes[n][f]
                k = spot(side, 0, n, f)
                prior, later = prior_later(pass_a[k], pass_b[k] + pass_wrap[k])
                far_one[side, sector_rows(at_own), lane] = shaped(faces[k])
                far_one[side, sector_rows(at_prior), lane] = shaped(prior)
                far_one[side, sector_rows(at_later), lane] = shaped(later)
                far_one[side, sector_rows(at_far), lane] = shaped(far[n, f])
                k = spot(side, 1, n, f)
                beside = prior_later(pass_a[k], pass_b[k] + pass_wrap[k])[side]
                far_two[side, sector_rows(at_own - 1), lane] = shaped(faces[k])
                far_two[side, sector_rows(2 - at_own), lane] = shaped(beside)
                rows = slice(2 * layers, 2 * layers + columns)
                prior, later = prior_later(got_a[n, f, rows, :], got_b[n, f, rows, :] + got_wrap[n, f, rows, :])
                near[side, sector_rows(0), lane] = shaped(prior)
                near[side, sector_rows(2), lane] = shaped(later)
                source = (flow, cotangent)[n]
                at = layers - 1 if side else 0
                for t in range(columns):
                    rows = slice(columns + t, columns + t + 1)
                    near[side, rows, lane] = shaped(source[f, t, at : at + 1, :])

    two = 2 * columns
    for side in range(2):
        virtual[side] = jnp.dot(weights[side, 0:16, :], far_one[side], precision=exact)
        back = jnp.dot(weights[side, 16:32, 0 : 3 * columns], near[side], precision=exact)
        here = jnp.where(pick == side, 1.0, 0.0).astype(f32)
        row = slice(columns + 1, columns + 2) if side else slice(0, 1)
        spot_near = 3 * columns if side else columns - 1
        nearest = slice(spot_near, spot_near + 1)
        values = []
        for n, rates in enumerate(all_rates):
            totals = [None] * fields
            for f in range(fields):
                lane = lanes[n][f]
                k = n * fields + f
                for target, at, k in ((virtual, row, k), (far_one, nearest, k + 2 * fields)):
                    target[side, at, lane] += here * faces[8 * fields + k // 8, k % 8 : k % 8 + 1, :]
                v = far_one[side, columns : columns + two, lane]
                theta = theta_term(
                    far_one[side, columns - 1 : columns - 1 + two, lane], v,
                    far_one[side, columns + 1 : columns + 1 + two, lane], rates,
                )
                lower, upper = far_two[side, :, lane], back[:, lane]
                if side:
                    lower, upper = upper, lower
                axial_low, axial_high = rates[2:4]
                axial = axial_low * lower + axial_high * upper - (axial_low + axial_high) * v
                mix_into(totals, mixers, n == 1, f, (theta, axial, radial_term(v, rates)))
            values.append(totals)
        for g in range(fields):
            k = spot(side, 0, 0, g)
            parts = [faces[k], prior_later(pass_a[k], pass_b[k] + pass_wrap[k])[side]]
            one = jnp.concatenate(parts if side else parts[::-1], axis=0) + time_step * values[0][g]
            reach_far = far_one[side, columns : columns + two, lanes[1][g]]
            beyond[side, :, lanes[0][g]] = shaping(one)
            beyond[side, :, lanes[1][g]] = adjoint_of(reach_far, one, values[1][g])
        ends_two[side] = jnp.dot(weights[side, 32:40, 0:two], beyond[side], precision=exact)

        totals = [[None] * fields for _ in range(2)]
        for n in range(2):
            for f in range(fields):
                mix_into(totals[n], mixers[1:2], n == 1, f, (virtual[side, :, lanes[n][f]],))
        a = layers - 8 if side else 0
        edge = lax.broadcasted_iota(jnp.int32, (8, radii), 0) == (7 if side else 0)
        for g in range(fields):
            section_end = ends[side, 0, g] + (time_step * forward_rates[2 + side]) * totals[0][g]
            reverse_end = ends[side, 1, g] + reverse_rates[2 + side] * totals[1][g]
            adjoint_end = adjoint_of(ends[side, 2, g], section_end, reverse_end)
            section_ends[side, g] = section_end
            for t in range(columns + 2):
                to = slice(t, t + 1)
                tile = jnp.where(edge, section_end[to, :], section[g, t, a : a + 8, :])
                tiles[side, 0, g, t] = shaping(tile)
                tiles[side, 1, g, t] = jnp.where(edge, adjoint_end[to, :], adjoint[g, t, a : a + 8, :])

        for t in range(columns):
            for n, (rates, shaped, source) in enumerate(zip(all_rates, all_shapes, (section, adjoint))):
                totals = [None] * fields
                for f in range(fields):
                    v = tiles[side, n, f, t + 1]
                    theta = theta_term(tiles[side, n, f, t], v, tiles[side, n, f, t + 2], rates)
                    far_end = ends_two[side, t : t + 1, lanes[n][f]]
                    b = a - 1 if side else a + 8
                    inner_end = shaped(source[f, t + 1, b : b + 1, :])
                    low_end, high_end = (inner_end, far_end) if side else (far_end, inner_end)
                    axial = axial_term(v, low_end, high_end, rates)
                    mix_into(totals, mixers, n == 1, f, (theta, axial, radial_term(v, rates)))
                rows = slice(a, a + 8)
                for g in range(fields):
                    flow_tile = flow[g, t, rows, :]
                    if n == 0:
                        tile = jnp.where(
                            edge, section_ends[side, g, t + 1 : t + 2, :], section[g, t + 1, rows, :]
                        )
                        advanced[g, t, rows, :] = advanced_of(flow_tile, tile, totals[g])
                    else:
                        sensitivity[g, t, rows, :] = sensitivity_of(
                            cotangent[g, t, rows, :], tiles[side, 1, g, t + 1], flow_tile, totals[g]
                        )


def interface_weights(slots, codes, cells, sector, block, n_block):
    middle = n_block // 2

    def around(table):
        wide = jnp.concatenate([table[-cells:], table, table[: 2 * cells]], axis=0)
        return lax.dynamic_slice_in_dim(wide, sector * cells, 4 * cells, 0)

    slot = around(slots)
    weight = (around(codes).astype(f32) + 1.0) / 12.0
    index = jnp.arange(4 * cells, dtype=jnp.int32)
    rise = cells * (index // cells)[:, None] + slot
    rotor = jnp.arange(6 * cells, dtype=jnp.int32)
    table = jnp.sum((rise[:, :, None] == rotor) * weight[:, :, None], axis=1)

    def padded(block_of):
        rows, columns = block_of.shape
        return jnp.pad(block_of, ((0, 16 - rows), (0, 4 * cells - columns)))

    def plain(rows, columns, shift):
        return (jnp.arange(columns) == jnp.arange(rows)[:, None] + shift).astype(f32)

    ends = cells + 2
    stator = (table[cells - 1 : 2 * cells + 1, 0 : 4 * cells], table[0 : 3 * cells, cells : 3 * cells].T)
    rotor_side = (table[:, 2 * cells - 1 : 3 * cells + 1].T, table[cells : 3 * cells, cells : 4 * cells])
    sides = []
    for at_interface, inside, pair, shifts in (
        (block == middle, block > 0, stator, (2 * cells - 1, 0)),
        (block == middle - 1, block < n_block - 1, rotor_side, (cells - 1, cells)),
    ):
        forth = jnp.where(at_interface, pair[0], plain(ends, 4 * cells, shifts[0])) * inside
        back = jnp.where(at_interface, pair[1], plain(2 * cells, 3 * cells, shifts[1]))
        sides.append(
            jnp.concatenate(
                [padded(forth), padded(back), padded(forth[1 : cells + 1, cells : 3 * cells])[:cells]], axis=0
            )
        )
    return jnp.stack(sides)


def shards(
    flow_state, cotangent, mix_theta, mix_axial, mix_radial, intersection_slot, intersection_code
):
    fields, columns, layers, radii = flow_state.shape
    sector, block = lax.axis_index("azim"), lax.axis_index("block")
    n_sector, n_block = lax.axis_size("azim"), lax.axis_size("block")
    middle = n_block // 2

    at = lambda s, b: s * n_block + b
    sectors, blocks = range(n_sector), range(n_block)
    pairs_a = [(i, i ^ 1) for i in sectors]
    pairs_b = [(i, (i + 1 if i % 2 else i - 1) % n_sector) for i in sectors]
    pairs_wrap = [(i, j) for i, j in pairs_b if abs(i - j) > 1]
    pairs_near = [(i, j) for i, j in pairs_b if abs(i - j) == 1]
    pairs_x = [(b, b - 2) for b in range(2, n_block, 2)] + [(b, b + 2) for b in range(1, n_block - 2, 2)]
    pairs_long = [(b, b ^ 1) for b in blocks]
    pairs_pass = [(at(i, b), at(j, b ^ 1)) for i, j in pairs_wrap for b in blocks]
    pairs_far, pairs_far_wrap = [], []
    for s in sectors:
        for b, shift, relay in ((middle - 1, 2, middle + 1), (middle, -2, middle - 2)):
            if 0 <= s + shift < n_sector:
                pairs_far.append((at(s, b), at(s + shift, relay)))
            else:
                pairs_far_wrap.append((at(s, b), at((s + shift) % n_sector, n_block - 1 - b)))

    place = jnp.stack(
        [
            block % 2,
            1 - sector % 2,
            block != middle,
            (block == middle + 1) | (block == middle - 2),
            block == middle + 1,
            sector,
        ]
    ).astype(jnp.int32)
    mixers = (mix_theta, mix_axial, mix_radial)

    shape = lambda *dims: jax.ShapeDtypeStruct(dims, f32)
    whole = shape(*flow_state.shape)
    inner = shape(fields, columns - 2, layers, radii)
    wide = shape(fields, columns + 2, layers, radii)
    half_out = shape(fields, columns - 4, layers - 16, radii)
    outer_out = shape(fields, 4, layers - 16, radii)
    face = shape(2, 2, fields, columns, radii)
    side = shape(2, fields, 2 * layers + columns, radii)
    sent = shape(8 * fields + (4 * fields + 7) // 8, columns, radii)
    far_face = shape(2, fields, columns, radii)
    work = 4 * 5 * 5 * 3 * columns * layers * radii

    (xsend,) = call(pack_axial_kernel, (place, flow_state, cotangent), [face], name="pack_axial")
    arrived = lax.ppermute(xsend, "block", pairs_x)
    own, send_wrap, farsend = call(
        pack_own_kernel, (place, flow_state, cotangent), [face, side, far_face], name="pack_own"
    )
    far = lax.ppermute(farsend, ("azim", "block"), pairs_far)
    got_wrap = lax.ppermute(send_wrap, "azim", pairs_wrap)
    (payload,) = call(
        payload_kernel,
        (place, intersection_slot.T, intersection_code.T, arrived, own, far),
        [sent],
        name="payload",
    )
    faces = lax.ppermute(payload, "block", pairs_long)

    place_later, payload = lax.optimization_barrier((place, payload))
    section, adjoint, reverse_ends, advanced_inner, sensitivity_inner, send_a, send_b = call(
        inner_kernel,
        (place_later, *mixers, flow_state, cotangent),
        [inner, inner, shape(2, fields, columns, radii), half_out, half_out, side, side],
        scratch=[inner.shape],
        flops=20 * work,
        name="inner",
    )
    send_a, payload, slots, codes = lax.optimization_barrier(
        (send_a, payload, intersection_slot, intersection_code)
    )
    pass_wrap = lax.ppermute(payload, ("azim", "block"), pairs_pass)
    weights = interface_weights(slots, codes, columns, sector, block, n_block)
    got_a = lax.ppermute(send_a, "azim", pairs_a)
    got_b = lax.ppermute(send_b, "azim", pairs_near)
    faces, section, weights, pass_wrap, farsend = lax.optimization_barrier(
        (faces, section, weights, pass_wrap, farsend)
    )
    pass_a = lax.ppermute(faces, "azim", pairs_a)
    pass_b = lax.ppermute(faces, "azim", pairs_near)
    far_wrap = lax.ppermute(farsend, ("azim", "block"), pairs_far_wrap)
    section, adjoint, ends, advanced_outer, sensitivity_outer = call(
        outer_kernel,
        (place, *mixers, flow_state, cotangent, got_a, got_b, got_wrap, section, adjoint, reverse_ends),
        [wide, wide, shape(2, 3, fields, 16, radii), outer_out, outer_out],
        scratch=[(2, fields, 4, layers, radii), (2, fields, 4, layers, radii), (2, fields, 2, layers, radii)],
        flops=0,
        name="outer",
    )
    span = 2 * fields * radii
    return tuple(
        call(
            last_kernel,
            (place, *mixers, flow_state, cotangent, section, adjoint, ends, faces, pass_a, pass_b, pass_wrap, far_wrap)
            + (got_a, got_b, got_wrap, weights)
            + (advanced_inner, sensitivity_inner, advanced_outer, sensitivity_outer),
            [whole, whole],
            scratch=[
                (2, 4 * columns, span),
                (2, 2 * columns, span),
                (2, 3 * columns, span),
                (2, 16, span),
                (2, 2 * columns, span),
                (2, columns, span),
                (2, 2, fields, columns + 2, 8, radii),
                (2, fields, 16, radii),
            ],
            flops=0,
            name="last",
        )
    )


def solution(mesh):
    placed = (
        P(None, "azim", "block", None),
        P(None, "azim", "block", None),
        P(),
        P(),
        P(),
        P(),
        P(),
    )
    return jax.shard_map(
        shards,
        mesh=mesh,
        in_specs=placed,
        out_specs=(P(None, "azim", "block", None), P(None, "azim", "block", None)),
        check_vma=False,
    )
```
